32 devices in a mesh: dp: 8 (over z, x), tensor: 4 (over y, core).
Axes of the slice: x: 2, y: 2, z: 4, core: 2. Of those that a mesh axis runs over, the one named last changes fastest.
Arguments:
- hidden_in: bfloat16 [8192, 2048], P(('dp', 'tensor')), may hold values from -6 to 6
- cotangent: bfloat16 [8192, 2048], P(('dp', 'tensor')), may hold values from -6 to 6
- seq_lengths: int32 [8], P('dp'), may hold values from 769 to 1024, as said below
- expert_ids: int32 [8192, 8], P(('dp', 'tensor')), may hold values from 0 to 63, all different within a row; in each aligned block of 256 rows (0 to 255, 256 to 511, ...) at most 32 rows name the same one
- attn_gain: bfloat16 [2048], replicated, may hold values from 0.099609375 to 1.8984375
- w_query: bfloat16 [2048, 2048], P(None, 'tensor'), may hold values from -0.125 to 0.125
- w_key: bfloat16 [2048, 2048], P(None, 'tensor'), may hold values from -0.125 to 0.125
- w_value: bfloat16 [2048, 2048], P(None, 'tensor'), may hold values from -0.125 to 0.125
- query_gain: bfloat16 [2048], P('tensor'), may hold values from 0.099609375 to 1.8984375
- key_gain: bfloat16 [2048], P('tensor'), may hold values from 0.099609375 to 1.8984375
- w_out: bfloat16 [2048, 2048], P('tensor'), may hold values from -1 to 1
- ffn_gain: bfloat16 [2048], replicated, may hold values from 0.099609375 to 1.8984375
- w_router: bfloat16 [2048, 64], replicated, may hold values from -0.0625 to 0.0625
- w_gate: bfloat16 [64, 2048, 1024], P('dp', None, 'tensor'), may hold values from -0.125 to 0.125
- w_up: bfloat16 [64, 2048, 1024], P('dp', None, 'tensor'), may hold values from -0.125 to 0.125
- w_down: bfloat16 [64, 1024, 2048], P('dp', 'tensor'), may hold values from -4 to 4
Outputs:
- output: bfloat16 [8192, 2048], P(('dp', 'tensor'))
- grad_input: bfloat16 [8192, 2048], P(('dp', 'tensor'))
- grad_w_query: float32 [2048, 2048], P(None, 'tensor')
- grad_w_key: float32 [2048, 2048], P(None, 'tensor')
- grad_w_value: float32 [2048, 2048], P(None, 'tensor')
- grad_query_gain: float32 [2048], P('tensor')
- grad_key_gain: float32 [2048], P('tensor')
- grad_w_out: float32 [2048, 2048], P('tensor')
- grad_attn_gain: float32 [2048], replicated
- grad_ffn_gain: float32 [2048], replicated
- grad_w_router: float32 [2048, 64], replicated
- grad_w_gate: float32 [64, 2048, 1024], P('dp', None, 'tensor')
- grad_w_up: float32 [64, 2048, 1024], P('dp', None, 'tensor')
- grad_w_down: float32 [64, 1024, 2048], P('dp', 'tensor')
The draws below stay inside these ranges and needn't reach their ends.
Inputs may be any that keep to these rules, and one draw needn't show every extreme that they name: `expert_ids`: among the 256 rows of one device (aligned blocks), every expert is named by exactly 32 rows; a row names 8 different experts. Sequence g is live at positions below seq_lengths[g]; some sequence is live in full.
All inputs are finite; a program needn't handle non-finite values.
Results may differ from the reference program's by a relative error of at most 0.023.
Values may be sent and summed in bfloat16 or wider, within the bound.
No kernel may reach another device: no remote copies, remote signals or barrier semaphores. Data moves between devices by JAX's collectives and lax.ppermute only.
A program may use at most 640 MiB of HBM per device.

```python
import math
import jax
import jax.numpy as jnp
import numpy as np
from jax import lax

D = 2048
HEADS = 16
HDIM = 128
FF = 1024
EXPERTS = 64
TOPK = 8
TOK_DEV = 256
SEQ = 1024
GROUPS = 8
TOKENS = 8192
CAP = 32
N_TENSOR = 4


def draw_seq_lengths(key, part):
    key = jax.random.fold_in(key, 7)
    first_key, second_key = jax.random.split(key)
    shortest = SEQ - SEQ // 4 + 1
    lengths = jax.random.randint(first_key, (GROUPS,), shortest, SEQ + 1)
    chosen = jax.random.randint(second_key, (), 0, GROUPS)
    return jnp.where(jnp.arange(GROUPS) == chosen, SEQ, lengths).astype(jnp.int32)


def steps_of(key, shape, pieces, low, top_value):
    loudness, own = 1.0, jax.random.fold_in(key, 6)
    for axis_at, shards_of in pieces:
        steps = jnp.exp(jax.random.uniform(jax.random.fold_in(own, axis_at), (shards_of,), jnp.float32, low / len(pieces), top_value / len(pieces)))
        loudness = loudness * jnp.repeat(steps, shape[axis_at] // shards_of).reshape([-1 if axis == axis_at else 1 for axis in range(len(shape))])
    return loudness


def deal_out(rng, own, number, rows, amount, top, limit, slope):
    ranking = jax.random.permutation(rng, amount)
    crowded, common = load_shares(amount, rows * top, limit, slope, True), load_shares(amount, rows * top, limit, slope, False)
    places = jnp.arange(amount)

    def named(sizes, rotation):
        used = int((sizes > 0).sum())
        fixed = max(1, used // 4)
        shifted = fixed + (places - fixed + rotation * (used - fixed)) % max(1, amount - fixed)
        return jnp.zeros((amount,), jnp.int32).at[ranking[jnp.where(places < fixed, places, shifted)]].set(jnp.asarray(sizes, jnp.int32))

    sizes = jnp.where(number % 4 == 0, named(crowded, number // 4), named(common, number - number // 4 - 1))
    mixed = jax.random.permutation(jax.random.fold_in(own, 3), amount)
    donor, sink = mixed[0:amount // 2 * 2:2], mixed[1:amount // 2 * 2:2]
    room = jnp.minimum(sizes[donor] - 1, limit - sizes[sink]) // 2
    room = jnp.where((donor == ranking[0]) | (sink == ranking[0]) | (sizes[sink] == 0), 0, jnp.maximum(room, 0))
    shifted = jax.random.randint(jax.random.fold_in(own, 4), (amount // 2,), 0, 1 << 20) % (room + 1)
    sizes = sizes.at[donor].add(-shifted).at[sink].add(shifted)
    labels = jnp.searchsorted(jnp.cumsum(sizes), jnp.arange(rows * top), side="right").astype(jnp.int32)
    listing = labels.reshape(top, rows).T
    listing = listing[jax.random.permutation(jax.random.fold_in(own, 1), rows)]
    rotation = jax.random.randint(jax.random.fold_in(own, 2), (rows, 1), 0, top)
    return jnp.take_along_axis(listing, (jnp.arange(top)[None, :] + rotation) % top, axis=1)


def load_shares(count, total, bound, lean, full):
    loads = [(1 << 20) // math.isqrt(rank ** lean) + 1 for rank in range(1, count + 1)]
    largest = bound if full else min(bound, max(-(-total // count), total * loads[0] // sum(loads)))
    least = 1 if total - largest >= count - 1 else 0
    counts, spare = [largest] + [least] * (count - 1), total - largest - least * (count - 1)
    while spare > 0:
        candidates = [i for i in range(1, count) if counts[i] < largest] or [i for i in range(1, count) if counts[i] < bound]
        mass, remaining = sum([loads[i] for i in candidates]), spare
        for i in candidates:
            more = min(bound - counts[i], max(1, remaining * loads[i] // mass), spare)
            counts[i] = counts[i] + more
            spare = spare - more
    return np.array(counts)


def centred(own_key, extent, width, limit, shards=(), held_as=jnp.bfloat16):
    drawn = jax.random.normal(own_key, extent, jnp.float32) * width
    if len(shards) > 0:
        drawn = steps_of(own_key, extent, shards, -0.22, 0.18) * drawn
    return jnp.clip(drawn, min=-limit, max=limit).astype(held_as)


def setup_inputs(seed: int = 0) -> dict:
    streams_of = jax.random.split(jax.random.key(seed), 17)
    hidden_in = centred(streams_of[0], (TOKENS, D), 1.0, 6.0, ((0, 32),))
    cotangent = centred(streams_of[1], (TOKENS, D), 1.0, 6.0, ((0, 32),))
    seq_lengths = draw_seq_lengths(jax.random.fold_in(streams_of[16], 71), 0)
    expert_ids_keys = jax.random.split(jax.random.fold_in(streams_of[3], 1), TOKENS // TOK_DEV)
    expert_ids_turns = jax.random.permutation(jax.random.fold_in(streams_of[3], 3), TOKENS // TOK_DEV)
    expert_ids = jax.vmap(lambda own, number: deal_out(jax.random.fold_in(streams_of[3], 2), own, number, TOK_DEV, EXPERTS, TOPK, CAP, 1))(expert_ids_keys, expert_ids_turns).reshape((TOKENS, TOPK))
    attn_gain = jnp.clip(1.0 + 0.18 * jax.random.normal(streams_of[4], (D,), jnp.float32), 0.099609375, 1.8984375).astype(jnp.bfloat16)
    w_query = centred(streams_of[5], (D, D), D ** -0.5, 0.125, ((1, 4),))
    w_key = centred(streams_of[6], (D, D), D ** -0.5, 0.125, ((1, 4),))
    w_value = centred(streams_of[7], (D, D), D ** -0.5, 0.125, ((1, 4),))
    query_gain = jnp.clip(1.0 + 0.18 * jax.random.normal(streams_of[8], (D,), jnp.float32), 0.099609375, 1.8984375).astype(jnp.bfloat16)
    key_gain = jnp.clip(1.0 + 0.18 * jax.random.normal(streams_of[9], (D,), jnp.float32), 0.099609375, 1.8984375).astype(jnp.bfloat16)
    w_out = centred(streams_of[10], (D, D), (D * 16 // SEQ) ** -0.5, 1.0, ((0, 4),))
    ffn_gain = jnp.clip(1.0 + 0.18 * jax.random.normal(streams_of[11], (D,), jnp.float32), 0.099609375, 1.8984375).astype(jnp.bfloat16)
    w_router = centred(streams_of[12], (D, EXPERTS), (4 * D) ** -0.5, 0.0625)
    w_gate = centred(streams_of[13], (EXPERTS, D, FF), D ** -0.5, 0.125, ((0, 8), (2, 4)))
    w_up = centred(streams_of[14], (EXPERTS, D, FF), D ** -0.5, 0.125, ((0, 8), (2, 4)))
    w_down = centred(streams_of[15], (EXPERTS, FF, D), (24.0 / FF ** 0.5), 4.0, ((0, 8), (1, 4)))
    return dict(hidden_in=hidden_in, cotangent=cotangent, seq_lengths=seq_lengths, expert_ids=expert_ids, attn_gain=attn_gain, w_query=w_query, w_key=w_key, w_value=w_value, query_gain=query_gain, key_gain=key_gain, w_out=w_out, ffn_gain=ffn_gain, w_router=w_router, w_gate=w_gate, w_up=w_up, w_down=w_down)


EPS = 1e-05
ROPE_BASE = 10000.0
HIGH = lax.Precision.HIGHEST

@jax.custom_vjp
def low(v):
    return lax.optimization_barrier(v.astype(jnp.bfloat16)).astype(jnp.float32)

@jax.custom_vjp
def low_back(v):
    return v

def low_keep(v):
    return (low(v), None)

def low_pass(kept, grad):
    return (grad,)

def back_keep(v):
    return (v, None)

def back_low(kept, grad):
    return (low(grad),)
low.defvjp(low_keep, low_pass)
low_back.defvjp(back_keep, back_low)

def rms_scale(values):
    return lax.rsqrt(lax.optimization_barrier(jnp.mean(values * values, axis=-1, keepdims=True)) + EPS)

def rope_tables(count):
    half_width = HDIM // 2
    frequency = jnp.exp(-(jnp.arange(half_width, dtype=jnp.float32) * 2.0 / HDIM) * math.log(ROPE_BASE))
    angles = jnp.arange(count, dtype=jnp.float32)[:, None] * frequency[None, :]
    return (jnp.cos(angles)[:, None, :], jnp.sin(angles)[:, None, :])

def rotate(values_in, cosine, sine_table):
    half_width = values_in.shape[-1] // 2
    front_half = values_in[..., :half_width]
    back_half = values_in[..., half_width:]
    return jnp.concatenate([front_half * cosine - back_half * sine_table, back_half * cosine + front_half * sine_table], axis=-1)

def one_group(weights, resid, group_ids, length):
    w_query, w_key, w_value, query_gain, key_gain, w_out, attn_gain, ffn_gain, w_router, w_gate, w_up, w_down = weights
    seq_len = resid.shape[0]
    attn_in = low(resid * rms_scale(resid) * attn_gain)
    query_proj = low_back(jnp.dot(attn_in, w_query, precision=HIGH))
    key_proj = low_back(jnp.dot(attn_in, w_key, precision=HIGH))
    value_proj = low_back(jnp.dot(attn_in, w_value, precision=HIGH))
    cosine, sine_table = rope_tables(seq_len)
    query = low(rotate((query_proj * rms_scale(query_proj) * query_gain).reshape(seq_len, HEADS, HDIM), cosine, sine_table))
    keys = low(rotate((key_proj * rms_scale(key_proj) * key_gain).reshape(seq_len, HEADS, HDIM), cosine, sine_table))
    values_low = low(value_proj.reshape(seq_len, HEADS, HDIM))
    scores = low_back(jnp.einsum('qhd,khd->hqk', query, keys, precision=HIGH) * HDIM ** (-0.5))
    positions = jnp.arange(seq_len)
    allowed = (positions[None, :] <= positions[:, None]) & (positions[None, :] < length)
    scores = jnp.where(allowed[None], scores, -1e+30)
    soft = low(jax.nn.softmax(scores, axis=-1))
    attended = jnp.einsum('hqk,khd->qhd', soft, values_low, precision=HIGH).reshape(seq_len, D)
    attended = low(low_back(attended))
    attn_rows = low_back(jnp.dot(attended, w_out, precision=HIGH))
    mixed = resid + attn_rows
    ffn_in = low(mixed * rms_scale(mixed) * ffn_gain)
    logits = low_back(jnp.dot(ffn_in, w_router, precision=HIGH))
    router_probs = jax.nn.softmax(logits, axis=-1)
    gate_values = jnp.take_along_axis(router_probs, group_ids, axis=1)
    flat_ids = group_ids.reshape(-1)
    sort_order = jnp.argsort(flat_ids, stable=True)
    inverse = jnp.argsort(sort_order)
    expert_rows = ffn_in[sort_order // TOPK].reshape(EXPERTS, -1, D)
    range_width = FF // N_TENSOR
    expert_out = jnp.zeros(expert_rows.shape, jnp.float32)
    for quarter in range(N_TENSOR):
        rows_here = low_back(expert_rows)
        lower = quarter * range_width
        upper = lower + range_width
        gate_pre = low_back(jnp.einsum('erd,edf->erf', rows_here, w_gate[:, :, lower:upper], precision=HIGH))
        up_pre = low_back(jnp.einsum('erd,edf->erf', rows_here, w_up[:, :, lower:upper], precision=HIGH))
        acts = low(jax.nn.silu(gate_pre) * up_pre)
        expert_out = expert_out + low(jnp.einsum('erf,efd->erd', acts, w_down[:, lower:upper, :], precision=HIGH))
    expert_out = low_back(expert_out)
    per_choice = expert_out.reshape(-1, D)[inverse].reshape(seq_len, TOPK, D)
    return mixed + jnp.einsum('sk,skd->sd', gate_values, per_choice, precision=HIGH)

def forward(weights, resid_all, expert_ids, seq_lengths):
    grouped = resid_all.reshape(GROUPS, SEQ, D)
    group_ids = expert_ids.reshape(GROUPS, SEQ, TOPK)
    step_fn = jax.checkpoint(one_group)

    def scan_body(carry, inputs):
        return (carry, step_fn(weights, inputs[0], inputs[1], inputs[2]))
    _, outputs = lax.scan(scan_body, None, (grouped, group_ids, seq_lengths))
    return outputs.reshape(TOKENS, D)

def reference(hidden_in, cotangent, seq_lengths, expert_ids, attn_gain, w_query, w_key, w_value, query_gain, key_gain, w_out, ffn_gain, w_router, w_gate, w_up, w_down):
    weights = (w_query.astype(jnp.float32), w_key.astype(jnp.float32), w_value.astype(jnp.float32), query_gain.astype(jnp.float32), key_gain.astype(jnp.float32), w_out.astype(jnp.float32), attn_gain.astype(jnp.float32), ffn_gain.astype(jnp.float32), w_router.astype(jnp.float32), w_gate.astype(jnp.float32), w_up.astype(jnp.float32), w_down.astype(jnp.float32))
    resid = hidden_in.astype(jnp.float32)
    result, pull = jax.vjp(lambda inputs, params: forward(params, inputs, expert_ids, seq_lengths), resid, weights)
    grad_resid, grads = pull(cotangent.astype(jnp.float32))
    return (result.astype(jnp.bfloat16), grad_resid.astype(jnp.bfloat16), grads[0], grads[1], grads[2], grads[3], grads[4], grads[5], grads[6], grads[7], grads[8], grads[9], grads[10], grads[11])
```

```python
import functools
import math

import jax
import jax.numpy as jnp
from jax import lax
from jax.experimental import pallas as pl
from jax.experimental.pallas import tpu as pltpu
from jax.sharding import PartitionSpec as P

HDIM = 128
EPS = 1e-05
ROPE_BASE = 10000.0
BOTH = ("dp", "tensor")
F32 = jnp.float32
BF16 = jnp.bfloat16
fence = lax.optimization_barrier


def rms_scale(values):
    return lax.rsqrt(jnp.mean(values * values, axis=-1, keepdims=True) + EPS)


def rope_tables(count, head_width):
    half_width = head_width // 2
    frequency = jnp.exp(
        -(jnp.arange(half_width, dtype=F32) * 2.0 / head_width) * math.log(ROPE_BASE)
    )
    angles = jnp.arange(count, dtype=F32)[:, None] * frequency[None, :]
    return (jnp.cos(angles), jnp.sin(angles))


def rotate(values_in, cosine, sine_table):
    half_width = values_in.shape[-1] // 2
    front_half = values_in[..., :half_width]
    back_half = values_in[..., half_width:]
    return jnp.concatenate(
        [
            front_half * cosine - back_half * sine_table,
            back_half * cosine + front_half * sine_table,
        ],
        axis=-1,
    )


def unrotate(grads_in, cosine, sine_table):
    return rotate(grads_in, cosine, -sine_table)


def contract_rows(left, right):
    return lax.dot_general(left, right, (((0,), (0,)), ((), ())), preferred_element_type=F32)


def times_transpose(left, right):
    return lax.dot_general(left, right, (((1,), (1,)), ((), ())), preferred_element_type=F32)


def add_low(*terms):
    total = terms[0].astype(F32)
    for term in terms[1:]:
        total = total + term.astype(F32)
    return total.astype(BF16)


def add_wide(*terms):
    total = terms[0].astype(F32)
    for term in terms[1:]:
        total = total + term.astype(F32)
    return total


def swap_tensor(value, bit):
    count = lax.axis_size("tensor")
    return lax.ppermute(value, "tensor", [(s, s ^ bit) for s in range(count)])


def tensor_gather(block):
    across = swap_tensor(block, 2)
    mate = swap_tensor(block, 1)
    return [block, mate, across, swap_tensor(across, 1)]


def tensor_scatter(blocks):
    across = add_low(blocks[2], swap_tensor(blocks[3], 1))
    here = add_wide(blocks[0], swap_tensor(blocks[1], 1))
    return here + swap_tensor(across, 2).astype(F32)


CHUNKS = (
    ((0, 0, 0, 0), (1, 0, 0, 0), (0, 1, 0, 0), (0, 0, 1, 0), (0, 0, 0, 1), (0, 1, 0, 1), (0, 0, 1, 1), (2, 0, 0, 0)),
    ((1, 1, 0, 0), (1, 0, 1, 0), (1, 0, 0, 1), (1, 1, 0, 1), (1, 0, 1, 1), (3, 0, 0, 0), (2, 1, 0, 0), (2, 0, 1, 0)),
    ((2, 0, 0, 1), (2, 1, 0, 1), (2, 0, 1, 1), (3, 1, 0, 0), (3, 0, 1, 0), (3, 0, 0, 1), (3, 1, 0, 1), (3, 0, 1, 1)),
    ((0, 1, 1, 0), (2, 1, 1, 0), (0, 1, 1, 1), (2, 1, 1, 1), (1, 1, 1, 0), (3, 1, 1, 0), (1, 1, 1, 1), (3, 1, 1, 1)),
)
PLACES = tuple(place for chunk in CHUNKS for place in chunk)
RING = 4


def device_pairs(move):
    pairs = []
    for z in range(RING):
        for x in range(2):
            for y in range(2):
                for c in range(2):
                    tz, tx, ty, tc = move(z, x, y, c)
                    pairs.append(((z * 2 + x) * 4 + y * 2 + c, (tz * 2 + tx) * 4 + ty * 2 + tc))
    return pairs


def send_x(value):
    return lax.ppermute(value, BOTH, device_pairs(lambda z, x, y, c: (z, x ^ 1, y, c)))


def send_y(value):
    return lax.ppermute(value, BOTH, device_pairs(lambda z, x, y, c: (z, x, y ^ 1, c)))


def send_c(value):
    return lax.ppermute(value, BOTH, device_pairs(lambda z, x, y, c: (z, x, y, c ^ 1)))


def send_z(value):
    return lax.ppermute(value, BOTH, device_pairs(lambda z, x, y, c: ((z - 1) % RING, x, y, c)))


def gather_everywhere(block):
    out = {(0, 0, 0, 0): block}

    def cross(*places):
        for k, dx, dy in places:
            out[k, dx, dy, 1] = send_c(out[k, dx, dy, 0])

    col_1, x_0, y_0 = fence((send_z(block), send_x(block), send_y(block)))
    out[1, 0, 0, 0], out[0, 1, 0, 0], out[0, 0, 1, 0] = col_1, x_0, y_0
    cross((0, 0, 0), (0, 1, 0), (0, 0, 1))
    col_2, x_1, y_1 = fence((send_z(col_1), send_x(col_1), send_y(col_1)))
    out[2, 0, 0, 0], out[1, 1, 0, 0], out[1, 0, 1, 0] = col_2, x_1, y_1
    cross((1, 0, 0), (1, 1, 0), (1, 0, 1))
    col_3, x_2, y_2 = fence((send_z(col_2), send_x(col_2), send_y(col_2)))
    out[3, 0, 0, 0], out[2, 1, 0, 0], out[2, 0, 1, 0] = col_3, x_2, y_2
    cross((2, 0, 0), (2, 1, 0), (2, 0, 1))
    x_3, y_3, x_0, y_2 = fence((send_x(col_3), send_y(col_3), x_0, y_2))
    out[3, 1, 0, 0], out[3, 0, 1, 0] = x_3, y_3
    cross((3, 0, 0), (3, 1, 0), (3, 0, 1))
    d_0, d_2, x_1, y_3 = fence((send_y(x_0), send_x(y_2), x_1, y_3))
    out[0, 1, 1, 0], out[2, 1, 1, 0] = d_0, d_2
    cross((0, 1, 1), (2, 1, 1))
    out[1, 1, 1, 0], out[3, 1, 1, 0] = send_y(x_1), send_x(y_3)
    cross((1, 1, 1), (3, 1, 1))
    return out


def scatter_everywhere(parts):
    held = {}
    for dx, dy in ((1, 1), (0, 1), (1, 0), (0, 0)):
        for k in (1, 2, 3, 0):
            held[k, dx, dy] = add_low(parts[k, dx, dy, 0], send_c(parts[k, dx, dy, 1]))
    by_x, by_y = fence((send_x(held[1, 1, 1]), send_y(held[2, 1, 1])))
    held[1, 0, 1] = add_low(held[1, 0, 1], by_x)
    held[2, 1, 0] = add_low(held[2, 1, 0], by_y)
    third, zeroth, _ = fence((held[3, 1, 1], held[0, 1, 1], by_x))
    by_x, by_y = fence((send_x(third), send_y(zeroth)))
    held[3, 0, 1] = add_low(held[3, 0, 1], by_x)
    held[0, 1, 0] = add_low(held[0, 1, 0], by_y)
    last, total = by_x, None
    for k in (1, 2, 3, 0):
        for_x, for_y, _ = fence((held[k, 1, 0], held[k, 0, 1], last))
        if total is None:
            by_x, by_y = fence((send_x(for_x), send_y(for_y)))
            total = add_low(held[k, 0, 0], by_x, by_y)
        else:
            by_x, by_y, by_z = fence((send_x(for_x), send_y(for_y), send_z(total)))
            total = (add_low if k else add_wide)(held[k, 0, 0], by_x, by_y, by_z)
        last = by_x
    return total


def place_indices():
    group, member = lax.axis_index("dp"), lax.axis_index("tensor")
    z, x, y, c = group // 2, group % 2, member // 2, member % 2
    absolute = jnp.stack(
        [(((z + k) % RING) * 2 + (x ^ dx)) * 4 + (y ^ dy) * 2 + (c ^ dc) for k, dx, dy, dc in PLACES]
    )
    table = [0] * len(PLACES)
    for position, (k, dx, dy, dc) in enumerate(PLACES):
        table[((k * 2 + dx) * 2 + dy) * 2 + dc] = position
    numbers = jnp.arange(len(PLACES))
    other_z, other_x = numbers // 8, (numbers // 4) % 2
    other_y, other_c = (numbers // 2) % 2, numbers % 2
    offset = ((((other_z - z) % RING) * 2 + (other_x ^ x)) * 2 + (other_y ^ y)) * 2 + (other_c ^ c)
    return absolute, jnp.asarray(table, jnp.int32)[offset]


def nn(left, right):
    return lax.dot_general(left, right, (((1,), (0,)), ((), ())), preferred_element_type=F32)


def nt(left, right):
    return lax.dot_general(left, right, (((1,), (1,)), ((), ())), preferred_element_type=F32)


def pick_rows(picks_ref, blocks, rows_ref, slot_count, width):
    experts = rows_ref.shape[0]
    for b, block in enumerate(blocks):
        for low in range(0, block.shape[1], width):
            columns = pl.ds(low, width)
            picked = nn(picks_ref[b], block[:, columns]).astype(BF16)
            for e in range(experts):
                rows_ref[e, pl.ds(b * slot_count, slot_count), columns] = picked[
                    e * slot_count : (e + 1) * slot_count
                ]


def give_rows(gives_ref, rows_ref, blocks, slot_count, width):
    experts = rows_ref.shape[0]
    for b, block in enumerate(blocks):
        for low in range(0, block.shape[1], width):
            columns = pl.ds(low, width)
            slots = jnp.concatenate(
                [rows_ref[e, pl.ds(b * slot_count, slot_count), columns] for e in range(experts)], axis=0
            )
            block[:, columns] = nn(gives_ref[b], slots).astype(BF16)


def cot_kernel(count, slot_count, picks_ref, down_ref, *refs):
    blocks, (rows_out, acts_out, rows_ref) = refs[:count], refs[count:]
    e = pl.program_id(0)

    @pl.when(e == 0)
    def _():
        pick_rows(picks_ref, blocks, rows_ref, slot_count, 512)

    rows = rows_ref[e]
    rows_out[0] = rows
    acts_out[0] = nt(rows, down_ref[0])


def main_kernel(count, slot_count, picks_ref, gives_ref, acts_ref, gates_ref, gate_ref, up_ref, *refs):
    blocks = refs[:count]
    rows_out, scaled_out, d_gate_out, d_up_out, inner_out = refs[count : count + 5]
    results = refs[count + 5 : 2 * count + 5]
    rows_ref = refs[2 * count + 5]
    e = pl.program_id(0)

    @pl.when(e == 0)
    def _():
        pick_rows(picks_ref, blocks, rows_ref, slot_count, 512)

    rows = rows_ref[e]
    rows_out[0] = rows
    pre, up = nn(rows, gate_ref[0]), nn(rows, up_ref[0])
    cot_acts = acts_ref[0]
    gate = jnp.concatenate([gates_ref[0]] * (pre.shape[1] // gates_ref.shape[2]), axis=1)
    sig = jax.nn.sigmoid(pre)
    silu = pre * sig
    acts = silu * up
    scaled_out[0] = (gate * acts).astype(BF16)
    inner = acts.astype(BF16).astype(F32) * cot_acts
    half = inner.shape[1] // 2
    inner_out[0] = inner[:, :half] + inner[:, half:]
    d_acts = gate * cot_acts
    d_pre = (d_acts * up * sig * (1.0 + pre * (1.0 - sig))).astype(BF16)
    d_up = (d_acts * silu).astype(BF16)
    d_gate_out[0] = d_pre
    d_up_out[0] = d_up
    rows_ref[e] = (nt(d_pre, gate_ref[0]) + nt(d_up, up_ref[0])).astype(BF16)

    @pl.when(e == pl.num_programs(0) - 1)
    def _():
        give_rows(gives_ref, rows_ref, results, slot_count, 512)


def out_kernel(count, slot_count, gives_ref, scaled_ref, down_ref, *refs):
    results, rows_ref = refs[:count], refs[count]
    e = pl.program_id(0)
    rows_ref[e] = nn(scaled_ref[0], down_ref[0]).astype(BF16)

    @pl.when(e == pl.num_programs(0) - 1)
    def _():
        give_rows(gives_ref, rows_ref, results, slot_count, 512)


def per_expert(*shape):
    return pl.BlockSpec((1,) + shape, lambda e: (e,) + (0,) * len(shape))


def resident(*shape):
    return pl.BlockSpec(shape, lambda e: (0,) * len(shape), pipeline_mode=pl.Buffered(1))


def cot_chunk(picks, w_down, blocks, slot_count):
    experts, hidden, width = w_down.shape
    count, tokens = len(blocks), blocks[0].shape[0]
    rows = count * slot_count
    return pl.pallas_call(
        functools.partial(cot_kernel, count, slot_count),
        grid=(experts,),
        in_specs=[resident(*picks.shape), per_expert(hidden, width)] + [resident(tokens, width)] * count,
        out_specs=[per_expert(rows, width), per_expert(rows, hidden)],
        out_shape=[
            jax.ShapeDtypeStruct((experts, rows, width), BF16),
            jax.ShapeDtypeStruct((experts, rows, hidden), F32),
        ],
        scratch_shapes=[pltpu.VMEM((experts, rows, width), BF16)],
        compiler_params=pltpu.CompilerParams(vmem_limit_bytes=40 << 20),
        cost_estimate=pl.CostEstimate(
            flops=2 * experts * rows * width * (hidden + tokens),
            bytes_accessed=2 * (count * tokens * width + experts * (rows + hidden) * width),
            transcendentals=0,
        ),
    )(picks, w_down, *blocks)


def main_chunk(picks, gives, cot_acts, gates, w_gate, w_up, blocks, slot_count):
    experts, width, hidden = w_gate.shape
    count, tokens = len(blocks), blocks[0].shape[0]
    rows = count * slot_count
    lanes = gates.shape[-1]
    outs = pl.pallas_call(
        functools.partial(main_kernel, count, slot_count),
        grid=(experts,),
        in_specs=[
            resident(*picks.shape),
            resident(*gives.shape),
            per_expert(rows, hidden),
            per_expert(rows, lanes),
            per_expert(width, hidden),
            per_expert(width, hidden),
        ]
        + [resident(tokens, width)] * count,
        out_specs=[
            per_expert(rows, width),
            per_expert(rows, hidden),
            per_expert(rows, hidden),
            per_expert(rows, hidden),
            per_expert(rows, hidden // 2),
        ]
        + [resident(tokens, width)] * count,
        out_shape=[
            jax.ShapeDtypeStruct((experts, rows, width), BF16),
            jax.ShapeDtypeStruct((experts, rows, hidden), BF16),
            jax.ShapeDtypeStruct((experts, rows, hidden), BF16),
            jax.ShapeDtypeStruct((experts, rows, hidden), BF16),
            jax.ShapeDtypeStruct((experts, rows, hidden // 2), F32),
        ]
        + [jax.ShapeDtypeStruct((tokens, width), BF16)] * count,
        scratch_shapes=[pltpu.VMEM((experts, rows, width), BF16)],
        compiler_params=pltpu.CompilerParams(vmem_limit_bytes=50 << 20),
        cost_estimate=pl.CostEstimate(
            flops=2 * experts * rows * width * (4 * hidden + 2 * tokens),
            bytes_accessed=2 * (2 * count * tokens * width + experts * (rows + 2 * hidden) * width),
            transcendentals=experts * rows * hidden,
        ),
    )(picks, gives, cot_acts, gates, w_gate, w_up, *blocks)
    return outs[:5], outs[5:]


def out_chunk(gives, scaled, w_down, slot_count):
    experts, hidden, width = w_down.shape
    count, tokens = gives.shape[:2]
    rows = count * slot_count
    return pl.pallas_call(
        functools.partial(out_kernel, count, slot_count),
        grid=(experts,),
        in_specs=[resident(*gives.shape), per_expert(rows, hidden), per_expert(hidden, width)],
        out_specs=[resident(tokens, width)] * count,
        out_shape=[jax.ShapeDtypeStruct((tokens, width), BF16)] * count,
        scratch_shapes=[pltpu.VMEM((experts, rows, width), BF16)],
        compiler_params=pltpu.CompilerParams(vmem_limit_bytes=40 << 20),
        cost_estimate=pl.CostEstimate(
            flops=2 * experts * rows * width * (hidden + tokens),
            bytes_accessed=2 * (count * tokens * width + experts * (rows + hidden) * width),
            transcendentals=0,
        ),
    )(gives, scaled, w_down)


def grad_kernel(count, *refs):
    rows, cots, scaled, d_gate, d_up = (refs[i * count : (i + 1) * count] for i in range(5))
    gate_out, up_out, down_out = refs[5 * count :]

    def total(lefts, rights):
        value = None
        for left, right in zip(lefts, rights):
            term = contract_rows(left[0], right[0])
            value = term if value is None else value + term
        return value

    gate_out[0] = total(rows, d_gate)
    up_out[0] = total(rows, d_up)
    down_out[0] = total(scaled, cots)


def expert_grads(rows, cots, scaled, d_gate, d_up):
    count = len(rows)
    experts, slots, width = rows[0].shape
    hidden = scaled[0].shape[2]
    tile = 512

    def wide(e, n):
        return (e, 0, n)

    def narrow(e, n):
        return (e, 0, 0)

    wide_spec = pl.BlockSpec((1, slots, tile), wide)
    narrow_spec = pl.BlockSpec((1, slots, hidden), narrow)
    return pl.pallas_call(
        functools.partial(grad_kernel, count),
        grid=(experts, width // tile),
        in_specs=[wide_spec] * (2 * count) + [narrow_spec] * (3 * count),
        out_specs=[
            pl.BlockSpec((1, tile, hidden), lambda e, n: (e, n, 0)),
            pl.BlockSpec((1, tile, hidden), lambda e, n: (e, n, 0)),
            pl.BlockSpec((1, hidden, tile), lambda e, n: (e, 0, n)),
        ],
        out_shape=[
            jax.ShapeDtypeStruct((experts, width, hidden), F32),
            jax.ShapeDtypeStruct((experts, width, hidden), F32),
            jax.ShapeDtypeStruct((experts, hidden, width), F32),
        ],
        compiler_params=pltpu.CompilerParams(vmem_limit_bytes=40 << 20),
        cost_estimate=pl.CostEstimate(
            flops=6 * experts * count * slots * width * hidden,
            bytes_accessed=4 * experts * count * slots * width + 12 * experts * width * hidden,
            transcendentals=0,
        ),
    )(*rows, *cots, *scaled, *d_gate, *d_up)


class GatheredExperts:
    def __init__(self, expert_ids, cotangent, w_gate, w_up, w_down, expert_total):
        tok_rows, self.topk = expert_ids.shape
        self.tok_rows = tok_rows
        self.w_gate, self.w_up, self.w_down = w_gate, w_up, w_down
        self.experts = w_gate.shape[0]
        self.slot_count = tok_rows * self.topk // expert_total
        self.absolute, self.position = place_indices()
        devices = len(PLACES)
        ids = lax.all_gather(expert_ids.T, BOTH, axis=0, tiled=False)[self.absolute]
        first = lax.axis_index("dp") * self.experts
        wanted = first + jnp.arange(self.experts)
        self.match = ids[:, None, :, :] == wanted[None, :, None, None]
        hot = jnp.any(self.match, axis=2)
        earlier = jnp.triu(jnp.ones((tok_rows, tok_rows), F32), 1).astype(BF16)
        rank = jnp.einsum("pet,tu->peu", hot.astype(BF16), earlier, preferred_element_type=F32)
        slot_of = jnp.where(hot, rank, -1.0)
        slots = jnp.arange(self.slot_count, dtype=F32)
        picks = (slot_of[:, :, None, :] == slots[None, None, :, None]).astype(BF16)
        self.picks = picks.reshape(devices, self.experts * self.slot_count, tok_rows)
        slot_turned = slot_of.transpose(0, 2, 1)
        gives = (slot_turned[:, :, :, None] == slots[None, None, None, :]).astype(BF16)
        self.gives = gives.reshape(devices, tok_rows, self.experts * self.slot_count)
        cot_blocks = gather_everywhere(cotangent)
        self.cots = [
            cot_chunk(self.part(self.picks, i), w_down, [cot_blocks[p] for p in chunk], self.slot_count)
            for i, chunk in enumerate(CHUNKS)
        ]

    def part(self, array, i):
        size = len(CHUNKS[i])
        return array[i * size : (i + 1) * size]

    def run(self, ffn_in, gate_values):
        devices, slots = len(PLACES), self.slot_count
        gates = lax.all_gather(gate_values.T, BOTH, axis=0, tiled=False)[self.absolute]
        token_gates = jnp.sum(jnp.where(self.match, gates[:, None, :, :], 0.0), axis=2)
        picks = self.picks.reshape(devices, self.experts, slots, self.tok_rows)
        slot_gates = jnp.sum(picks.astype(F32) * token_gates[:, :, None, :], axis=3)
        slot_gates = slot_gates.transpose(1, 0, 2).reshape(self.experts, devices * slots, 1)
        slot_gates = jnp.broadcast_to(slot_gates, (self.experts, devices * slots, 128))
        blocks = gather_everywhere(ffn_in)
        kept, d_parts = [], {}
        for i, chunk in enumerate(CHUNKS):
            size = len(chunk) * slots
            saved, results = main_chunk(
                self.part(self.picks, i),
                self.part(self.gives, i),
                self.cots[i][1],
                slot_gates[:, i * size : (i + 1) * size],
                self.w_gate,
                self.w_up,
                [blocks[p] for p in chunk],
                slots,
            )
            kept.append(saved)
            d_parts.update(zip(chunk, results))
        d_ffn = scatter_everywhere(d_parts)
        inner = jnp.concatenate([jnp.sum(saved[4], axis=-1) for saved in kept], axis=1)
        inner = inner.reshape(self.experts, devices, slots).transpose(1, 0, 2)
        d_probs = jnp.sum(picks.astype(F32) * inner[:, :, :, None], axis=2)
        d_probs = d_probs[self.position]
        arrived = lax.all_to_all(d_probs, BOTH, split_axis=0, concat_axis=0, tiled=True)
        tensor_count = lax.axis_size("tensor")
        d_probs = jnp.sum(
            arrived.reshape(-1, tensor_count, self.experts, self.tok_rows), axis=1
        ).reshape(-1, self.tok_rows).T
        self.kept = kept
        return d_ffn, d_probs

    def output(self, after):
        parts = {}
        for i, chunk in enumerate(CHUNKS):
            results = out_chunk(self.part(self.gives, i), self.kept[i][1], self.w_down, self.slot_count)
            parts.update(zip(chunk, results))
        held, _ = fence((parts, after))
        return scatter_everywhere(held)

    def grads(self):
        rows, scaled, d_gate, d_up, _ = zip(*self.kept)
        return expert_grads(rows, [cot[0] for cot in self.cots], scaled, d_gate, d_up)


class SentExperts:
    def __init__(self, expert_ids, cotangent, w_gate, w_up, w_down, expert_total):
        self.ids, self.cotangent = expert_ids, cotangent
        self.w_gate, self.w_up, self.w_down = w_gate, w_up, w_down
        self.expert_total = expert_total
        self.groups, self.members = lax.axis_size("dp"), lax.axis_size("tensor")
        self.experts = w_gate.shape[0]
        self.slot_count = expert_ids.size // expert_total

    def send_out(self, rows):
        width = rows.shape[1]
        per_group = self.experts * self.slot_count
        copies = jnp.broadcast_to(
            rows.reshape(self.groups, 1, per_group, width), (self.groups, self.members, per_group, width)
        ).reshape(-1, per_group, width)
        arrived = lax.all_to_all(copies, BOTH, split_axis=0, concat_axis=0, tiled=True)
        return arrived.reshape(-1, self.experts, self.slot_count, width)

    def send_back(self, parts):
        width = parts.shape[-1]
        per_group = self.experts * self.slot_count
        returned = lax.all_to_all(
            parts.reshape(-1, per_group, width), BOTH, split_axis=0, concat_axis=0, tiled=True
        )
        returned = returned.reshape(self.groups, self.members, per_group, width)
        return jnp.sum(returned.astype(F32), axis=1).reshape(-1, width)

    def run(self, ffn_in, gate_values):
        tok_rows, topk = self.ids.shape
        width = ffn_in.shape[1]
        order = jnp.argsort(self.ids.reshape(-1), stable=True)
        inverse = jnp.argsort(order)
        wide = dict(preferred_element_type=F32)
        rows = self.send_out(ffn_in[order // topk])
        pre = jnp.einsum("secd,edf->secf", rows, self.w_gate, **wide)
        up = jnp.einsum("secd,edf->secf", rows, self.w_up, **wide)
        sig = jax.nn.sigmoid(pre)
        silu = pre * sig
        acts = (silu * up).astype(BF16)
        part = jnp.einsum("secf,efd->secd", acts, self.w_down, **wide).astype(BF16)
        choice_out = self.send_back(part)[inverse].reshape(tok_rows, topk, width)
        self.mix = jnp.sum(gate_values[:, :, None] * choice_out, axis=1)
        d_result = self.cotangent.astype(F32)
        d_gates = jnp.sum(choice_out * d_result[:, None, :], axis=2)
        d_out = (gate_values[:, :, None] * d_result[:, None, :]).astype(BF16)
        d_out = self.send_out(d_out.reshape(-1, width)[order])
        d_acts = jnp.einsum("secd,efd->secf", d_out, self.w_down, **wide)
        d_pre = (d_acts * up * sig * (1.0 + pre * (1.0 - sig))).astype(BF16)
        d_up = (d_acts * silu).astype(BF16)
        self.weight_grads = (
            jnp.einsum("secd,secf->edf", rows, d_pre, **wide),
            jnp.einsum("secd,secf->edf", rows, d_up, **wide),
            jnp.einsum("secf,secd->efd", acts, d_out, **wide),
        )
        d_rows = jnp.einsum("secf,edf->secd", d_pre, self.w_gate, **wide) + jnp.einsum(
            "secf,edf->secd", d_up, self.w_up, **wide
        )
        d_sorted = self.send_back(d_rows.astype(BF16))
        d_ffn = jnp.sum(d_sorted[inverse].reshape(tok_rows, topk, width), axis=1)
        hot = self.ids[:, :, None] == jnp.arange(self.expert_total)[None, None, :]
        d_probs = jnp.sum(jnp.where(hot, d_gates[:, :, None], 0.0), axis=1)
        return d_ffn, d_probs

    def output(self, after):
        return self.mix

    def grads(self):
        return self.weight_grads


def local(
    hidden_in,
    cotangent,
    seq_lengths,
    expert_ids,
    attn_gain,
    w_query,
    w_key,
    w_value,
    query_gain,
    key_gain,
    w_out,
    ffn_gain,
    w_router,
    w_gate,
    w_up,
    w_down,
):
    tensor_count = lax.axis_size("tensor")
    group_count = lax.axis_size("dp")
    tok_rows, model_width = hidden_in.shape
    expert_total = w_router.shape[1]
    seq_len = tok_rows * tensor_count
    local_width = w_query.shape[1]
    head_width = HDIM
    local_heads = local_width // head_width
    block_rows = min(512, seq_len)
    block_count = seq_len // block_rows
    score_scale = head_width ** (-0.5)
    live_length = seq_lengths[0]
    gathered_plan = (group_count, tensor_count) == (2 * RING, 4)
    experts_kind = GatheredExperts if gathered_plan else SentExperts

    member = lax.axis_index("tensor")
    blocks_at = member ^ jnp.arange(tensor_count)
    cosine, sine_table = rope_tables(seq_len, head_width)
    half_width = head_width // 2
    cosine = cosine.reshape(tensor_count, tok_rows, half_width)[blocks_at].reshape(seq_len, 1, half_width)
    sine_table = sine_table.reshape(tensor_count, tok_rows, half_width)[blocks_at].reshape(
        seq_len, 1, half_width
    )
    positions = (blocks_at[:, None] * tok_rows + jnp.arange(tok_rows)[None, :]).reshape(-1)
    key_live = positions < live_length

    resid = hidden_in.astype(F32)
    scale_one = rms_scale(resid)
    normed = resid * scale_one
    attn_in = (normed * attn_gain.astype(F32)).astype(BF16)
    gathered = jnp.concatenate(tensor_gather(attn_in), axis=0)
    q_raw = jnp.dot(gathered, w_query, preferred_element_type=F32)
    k_raw = jnp.dot(gathered, w_key, preferred_element_type=F32)
    v_raw = jnp.dot(gathered, w_value, preferred_element_type=F32)
    experts = experts_kind(expert_ids, cotangent, w_gate, w_up, w_down, expert_total)

    def token_sums(*values):
        stacked = jnp.stack([jnp.sum(value, axis=1).reshape(tensor_count, tok_rows) for value in values])
        summed = lax.psum(stacked[:, blocks_at], "tensor")
        return summed[:, blocks_at].reshape(len(values), seq_len)

    q_square, k_square = token_sums(q_raw * q_raw, k_raw * k_raw)
    q_rscale = lax.rsqrt(q_square / model_width + EPS)[:, None]
    k_rscale = lax.rsqrt(k_square / model_width + EPS)[:, None]
    query_hat = q_raw * q_rscale
    key_hat = k_raw * k_rscale
    q_gain = query_gain.astype(F32)
    k_gain = key_gain.astype(F32)
    q_rot = rotate(
        (query_hat * q_gain).reshape(seq_len, local_heads, head_width), cosine, sine_table
    ).astype(BF16)
    k_rot = rotate(
        (key_hat * k_gain).reshape(seq_len, local_heads, head_width), cosine, sine_table
    ).astype(BF16)
    v_low = v_raw.astype(BF16).reshape(seq_len, local_heads, head_width)
    q_blocks = q_rot.reshape(block_count, block_rows, local_heads, head_width)
    q_positions = positions.reshape(block_count, block_rows)

    def allowed_mask(q_pos):
        return ((positions[None, :] <= q_pos[:, None]) & key_live[None, :])[None]

    def attend(inputs):
        q_block, q_pos = inputs
        scores = jnp.einsum("qhd,khd->hqk", q_block, k_rot, preferred_element_type=F32) * score_scale
        scores = jnp.where(allowed_mask(q_pos), scores, -1e30)
        row_max = jnp.max(scores, axis=-1, keepdims=True)
        exp_scores = jnp.exp(scores - row_max)
        row_total = jnp.sum(exp_scores, axis=-1, keepdims=True)
        soft_low = (exp_scores / row_total).astype(BF16)
        attended = jnp.einsum("hqk,khd->qhd", soft_low, v_low, preferred_element_type=F32)
        return (attended, (row_max + jnp.log(row_total))[..., 0])

    o_blocks, lse_blocks = lax.map(attend, (q_blocks, q_positions))
    o_low = o_blocks.reshape(seq_len, local_width).astype(BF16)
    projected = jnp.dot(o_low, w_out, preferred_element_type=F32).astype(BF16)
    attn_rows = tensor_scatter(jnp.split(projected, tensor_count, axis=0))
    mixed = resid + attn_rows
    scale_two = rms_scale(mixed)
    mixed_norm = mixed * scale_two
    ffn_in = (mixed_norm * ffn_gain.astype(F32)).astype(BF16)
    logits = jnp.dot(ffn_in, w_router, preferred_element_type=F32)
    router_probs = jax.nn.softmax(logits, axis=-1)
    gate_values = jnp.take_along_axis(router_probs, expert_ids, axis=1)
    d_ffn, d_probs = experts.run(ffn_in, gate_values)
    d_result = cotangent.astype(F32)
    d_logits = (
        router_probs * (d_probs - jnp.sum(router_probs * d_probs, axis=-1, keepdims=True))
    ).astype(BF16)
    router_part = contract_rows(ffn_in, d_logits)
    d_ffn = d_ffn + times_transpose(d_logits, w_router)
    ffn_gain_part = jnp.sum(d_ffn * mixed_norm, axis=0)
    d_norm_two = d_ffn * ffn_gain.astype(F32)
    d_mixed = d_result + scale_two * (
        d_norm_two - mixed_norm * jnp.mean(d_norm_two * mixed_norm, axis=-1, keepdims=True)
    )
    d_attn = d_mixed.astype(BF16)
    d_attn_all = jnp.concatenate(tensor_gather(d_attn), axis=0)
    result = mixed + experts.output(d_attn_all)
    grad_w_out = contract_rows(o_low, d_attn_all)
    d_attended = (
        times_transpose(d_attn_all, w_out)
        .astype(BF16)
        .reshape(block_count, block_rows, local_heads, head_width)
    )

    def attend_back(carry, inputs):
        dk_total, dv_total = carry
        q_block, do_block, lse_block, q_pos = inputs
        scores = jnp.einsum("qhd,khd->hqk", q_block, k_rot, preferred_element_type=F32) * score_scale
        allowed = allowed_mask(q_pos)
        scores = jnp.where(allowed, scores, -1e30)
        soft = jnp.where(allowed, jnp.exp(scores - lse_block[..., None]), 0.0)
        d_weights = jnp.einsum("qhd,khd->hqk", do_block, v_low, preferred_element_type=F32)
        d_scores = (soft * (d_weights - jnp.sum(soft * d_weights, axis=-1, keepdims=True))).astype(BF16)
        dq_block = jnp.einsum("hqk,khd->qhd", d_scores, k_rot, preferred_element_type=F32) * score_scale
        dk_total = (
            dk_total
            + jnp.einsum("hqk,qhd->khd", d_scores, q_block, preferred_element_type=F32) * score_scale
        )
        dv_total = dv_total + jnp.einsum(
            "hqk,qhd->khd", soft.astype(BF16), do_block, preferred_element_type=F32
        )
        return ((dk_total, dv_total), dq_block)

    zero_field = jnp.zeros((seq_len, local_heads, head_width), F32)
    (dk_rot, dv_full), dq_blocks = lax.scan(
        attend_back, (zero_field, zero_field), (q_blocks, d_attended, lse_blocks, q_positions)
    )
    dq_gain = unrotate(
        dq_blocks.reshape(seq_len, local_heads, head_width), cosine, sine_table
    ).reshape(seq_len, local_width)
    dk_gain = unrotate(dk_rot, cosine, sine_table).reshape(seq_len, local_width)
    query_gain_part = jnp.sum(dq_gain * query_hat, axis=0)
    key_gain_part = jnp.sum(dk_gain * key_hat, axis=0)
    dq_hat = dq_gain * q_gain
    dk_hat = dk_gain * k_gain
    q_inner, k_inner = token_sums(dq_hat * query_hat, dk_hat * key_hat)
    dq_raw = (q_rscale * (dq_hat - query_hat * (q_inner / model_width)[:, None])).astype(BF16)
    dk_raw = (k_rscale * (dk_hat - key_hat * (k_inner / model_width)[:, None])).astype(BF16)
    dv_raw = dv_full.reshape(seq_len, local_width).astype(BF16)
    grad_query = contract_rows(gathered, dq_raw)
    grad_key = contract_rows(gathered, dk_raw)
    grad_value = contract_rows(gathered, dv_raw)
    total_term = times_transpose(dq_raw, w_query)
    total_term = total_term + times_transpose(dk_raw, w_key)
    total_term = (total_term + times_transpose(dv_raw, w_value)).astype(BF16)
    d_attn_in = tensor_scatter(jnp.split(total_term, tensor_count, axis=0))
    attn_gain_part = jnp.sum(d_attn_in * normed, axis=0)
    d_norm_one = d_attn_in * attn_gain.astype(F32)
    d_input = d_mixed + scale_one * (
        d_norm_one - normed * jnp.mean(d_norm_one * normed, axis=-1, keepdims=True)
    )
    grad_w_gate, grad_w_up, grad_w_down = experts.grads()

    def dp_sum(value):
        return lax.psum(value.astype(BF16), "dp").astype(F32)

    return (
        result.astype(BF16),
        d_input.astype(BF16),
        dp_sum(grad_query),
        dp_sum(grad_key),
        dp_sum(grad_value),
        dp_sum(query_gain_part),
        dp_sum(key_gain_part),
        dp_sum(grad_w_out),
        lax.psum(attn_gain_part, BOTH),
        lax.psum(ffn_gain_part, BOTH),
        lax.psum(router_part, BOTH),
        grad_w_gate,
        grad_w_up,
        grad_w_down,
    )


def solution(mesh):
    rows, columns = P(BOTH, None), P(None, "tensor")
    return jax.shard_map(
        local,
        mesh=mesh,
        in_specs=(
            rows,
            rows,
            P("dp"),
            rows,
            P(),
            columns,
            columns,
            columns,
            P("tensor"),
            P("tensor"),
            P("tensor", None),
            P(),
            P(),
            P("dp", None, "tensor"),
            P("dp", None, "tensor"),
            P("dp", "tensor", None),
        ),
        out_specs=(
            rows,
            rows,
            columns,
            columns,
            columns,
            P("tensor"),
            P("tensor"),
            P("tensor", None),
            P(),
            P(),
            P(),
            P("dp", None, "tensor"),
            P("dp", None, "tensor"),
            P("dp", "tensor", None),
        ),
        check_vma=False,
    )
```

```python
import functools
import math

import jax
import jax.numpy as jnp
from jax import lax
from jax.experimental import pallas as pl
from jax.experimental.pallas import tpu as pltpu
from jax.sharding import PartitionSpec as P

HDIM = 128
EPS = 1e-05
ROPE_BASE = 10000.0
BOTH = ("dp", "tensor")
F32 = jnp.float32
BF16 = jnp.bfloat16
VMEM_GRANT = 60 << 20
fence = lax.optimization_barrier


def rms_scale(values):
    return lax.rsqrt(jnp.mean(values * values, axis=-1, keepdims=True) + EPS)


def rope_tables(count, head_width):
    half_width = head_width // 2
    frequency = jnp.exp(
        -(jnp.arange(half_width, dtype=F32) * 2.0 / head_width) * math.log(ROPE_BASE)
    )
    angles = jnp.arange(count, dtype=F32)[:, None] * frequency[None, :]
    return (jnp.cos(angles), jnp.sin(angles))


def rotate(values_in, cosine, sine_table):
    half_width = values_in.shape[-1] // 2
    front_half = values_in[..., :half_width]
    back_half = values_in[..., half_width:]
    return jnp.concatenate(
        [
            front_half * cosine - back_half * sine_table,
            back_half * cosine + front_half * sine_table,
        ],
        axis=-1,
    )


def unrotate(grads_in, cosine, sine_table):
    return rotate(grads_in, cosine, -sine_table)


def contract_rows(left, right):
    return lax.dot_general(left, right, (((0,), (0,)), ((), ())), preferred_element_type=F32)


def times_transpose(left, right):
    return lax.dot_general(left, right, (((1,), (1,)), ((), ())), preferred_element_type=F32)


def add_low(*terms):
    total = terms[0].astype(F32)
    for term in terms[1:]:
        total = total + term.astype(F32)
    return total.astype(BF16)


def add_wide(*terms):
    total = terms[0].astype(F32)
    for term in terms[1:]:
        total = total + term.astype(F32)
    return total


RING = 4
COLUMNS = (
    ((0, 0, 0), (1, 0, 0), (0, 1, 0), (0, 0, 1)),
    ((2, 0, 0), (1, 1, 0), (1, 0, 1), (2, 1, 0)),
    ((3, 0, 0), (3, 1, 0), (2, 0, 1), (3, 0, 1)),
    ((1, 1, 1), (2, 1, 1)),
    ((0, 1, 1), (3, 1, 1)),
)
CHUNKS = tuple(tuple(chip + (dc,) for dc in (0, 1) for chip in chips) for chips in COLUMNS)
STARTS = tuple(sum(len(chunk) for chunk in CHUNKS[:i]) for i in range(len(CHUNKS)))
PLACES = tuple(place for chunk in CHUNKS for place in chunk)
MOVES = {
    "x": lambda z, x, y, c: (z, x ^ 1, y, c),
    "y": lambda z, x, y, c: (z, x, y ^ 1, c),
    "c": lambda z, x, y, c: (z, x, y, c ^ 1),
    "z": lambda z, x, y, c: ((z - 1) % RING, x, y, c),
    "u1": lambda z, x, y, c: ((z + 1) % RING, x, y, c),
    "u2": lambda z, x, y, c: ((z + 2) % RING, x, y, c),
    "u3": lambda z, x, y, c: ((z + 3) % RING, x, y, c),
    "z1": lambda z, x, y, c: (z ^ 1, x, y, c),
    "z2": lambda z, x, y, c: (z ^ 2, x, y, c),
}


def device_pairs(move):
    pairs = []
    for z in range(RING):
        for x in range(2):
            for y in range(2):
                for c in range(2):
                    tz, tx, ty, tc = move(z, x, y, c)
                    pairs.append(((z * 2 + x) * 4 + y * 2 + c, (tz * 2 + tx) * 4 + ty * 2 + tc))
    return pairs


def send(value, axis):
    return lax.ppermute(value, BOTH, device_pairs(MOVES[axis]))


def small_sum(value, axes):
    for axis in axes:
        value = value + send(value, axis)
    return value


def hop(axis, k, dx, dy):
    return {"z": ((k + 1) % RING, dx, dy), "x": (k, dx ^ 1, dy), "y": (k, dx, dy ^ 1)}[axis]


class Stages:
    def __init__(self, token):
        self.token = token

    def run(self, sends, works=()):
        values, args, _ = fence(([s[0] for s in sends], [w[1] for w in works], self.token))
        got, crossed = [], []
        for value, (_, axis) in zip(values, sends):
            if axis == "c" and len(crossed) >= 2:
                value, _ = fence((value, crossed[-2]))
            got.append(send(value, axis))
            if axis == "c":
                crossed.append(got[-1])
        made = [work(*arg) for (work, _), arg in zip(works, args)]
        got, made = fence((got, made))
        self.token = jax.tree.leaves((got, made))[0]
        return got, made


class Gather:
    def __init__(self, block):
        self.held = {(0, 0, 0, 0): block}

    def sends(self, hops):
        return [(self.held[chip + (0,)], axis) for axis, chip in hops]

    def take(self, hops, got):
        for (axis, chip), value in zip(hops, got):
            self.held[chip + (1,) if axis == "c" else hop(axis, *chip) + (0,)] = value

    def chunk(self, i):
        chunk = CHUNKS[i]
        late = [place for place in chunk if place not in self.held]
        values = [self.held[place] for place in chunk if place in self.held]
        return values, [self.held[place[:3] + (0,)] for place in late], late

    @staticmethod
    def complete(i, values, crossing, late):
        blocks = dict(zip([place for place in CHUNKS[i] if place not in late], values))
        done = []
        for place, value in zip(late, crossing):
            if len(done) >= 2:
                value, _ = fence((value, done[-2]))
            done.append(send(value, "c"))
            blocks[place] = done[-1]
        return [blocks[place] for place in CHUNKS[i]]


class Scatter:
    def __init__(self):
        self.held = {}

    def put(self, i, sums):
        for chip, value in zip(COLUMNS[i], sums):
            self.held.setdefault(chip, []).append(value)

    def sends(self, hops):
        return [(add_low(*self.held[chip]), axis) for axis, chip in hops]

    def take(self, hops, got):
        for (axis, chip), value in zip(hops, got):
            self.held.setdefault(hop(axis, *chip), []).append(value)

    def total(self):
        return add_wide(*self.held[0, 0, 0])


class DpSum:
    def __init__(self, value):
        group = lax.axis_index("dp")
        self.z, self.x = group // 2, group % 2
        self.value = value
        self.half, self.piece = value.shape[0] // 2, value.shape[0] // (2 * RING)

    def split_x(self):
        return [(lax.dynamic_slice_in_dim(self.value, (1 - self.x) * self.half, self.half), "x")]

    def add_x(self, got):
        self.sum = add_low(lax.dynamic_slice_in_dim(self.value, self.x * self.half, self.half), got[0])

    def split_z(self):
        return [
            (lax.dynamic_slice_in_dim(self.sum, ((self.z + d) % RING) * self.piece, self.piece), f"u{d}")
            for d in (1, 2, 3)
        ]

    def add_z(self, got):
        self.part = add_low(lax.dynamic_slice_in_dim(self.sum, self.z * self.piece, self.piece), *got)

    def join_z(self):
        return [(self.part, f"u{d}") for d in (1, 2, 3)]

    def took_z(self, got):
        stack = jnp.stack([self.part] + list(got))
        order = (self.z - jnp.arange(RING)) % RING
        self.whole_half = stack[order].reshape(self.half, -1)

    def join_x(self):
        return [(self.whole_half, "x")]

    def took_x(self, got):
        mine, other = self.whole_half, got[0]
        first = jnp.where(self.x == 0, mine, other)
        second = jnp.where(self.x == 0, other, mine)
        self.result = jnp.concatenate([first, second], axis=0).astype(F32)


def core_sum(near, far):
    return pair_sum(near, send(far, "c"))


def place_indices():
    group, member = lax.axis_index("dp"), lax.axis_index("tensor")
    z, x, y, c = group // 2, group % 2, member // 2, member % 2
    absolute = jnp.stack(
        [(((z + k) % RING) * 2 + (x ^ dx)) * 4 + (y ^ dy) * 2 + (c ^ dc) for k, dx, dy, dc in PLACES]
    )
    table = [0] * len(PLACES)
    for position, (k, dx, dy, dc) in enumerate(PLACES):
        table[((k * 2 + dx) * 2 + dy) * 2 + dc] = position
    numbers = jnp.arange(len(PLACES))
    other_z, other_x = numbers // 8, (numbers // 4) % 2
    other_y, other_c = (numbers // 2) % 2, numbers % 2
    offset = ((((other_z - z) % RING) * 2 + (other_x ^ x)) * 2 + (other_y ^ y)) * 2 + (other_c ^ c)
    return absolute, jnp.asarray(table, jnp.int32)[offset]


def nn(left, right):
    return lax.dot_general(left, right, (((1,), (0,)), ((), ())), preferred_element_type=F32)


def nt(left, right):
    return lax.dot_general(left, right, (((1,), (1,)), ((), ())), preferred_element_type=F32)


def pick_rows(picks_ref, blocks, rows_ref, slot_count, width):
    experts = rows_ref.shape[0]
    for b, block in enumerate(blocks):
        for low in range(0, block.shape[1], width):
            columns = pl.ds(low, width)
            picked = nn(picks_ref[b], block[:, columns]).astype(BF16)
            for e in range(experts):
                rows_ref[e, pl.ds(b * slot_count, slot_count), columns] = picked[
                    e * slot_count : (e + 1) * slot_count
                ]


def give_rows(picks_ref, rows_ref, blocks, slot_count, width):
    experts = rows_ref.shape[0]
    for b, block in enumerate(blocks):
        for low in range(0, block.shape[1], width):
            columns = pl.ds(low, width)
            slots = jnp.concatenate(
                [rows_ref[e, pl.ds(b * slot_count, slot_count), columns] for e in range(experts)], axis=0
            )
            block[:, columns] = contract_rows(picks_ref[b], slots).astype(BF16)


def cot_kernel(count, slot_count, picks_ref, down_ref, *refs):
    blocks, (rows_out, acts_out, rows_ref) = refs[:count], refs[count:]
    e = pl.program_id(0)

    @pl.when(e == 0)
    def _():
        pick_rows(picks_ref, blocks, rows_ref, slot_count, 512)

    rows = rows_ref[e]
    rows_out[0] = rows
    acts_out[0] = nt(rows, down_ref[0])


def main_kernel(count, slot_count, picks_ref, gates_ref, acts_ref, gate_ref, up_ref, *refs):
    blocks = refs[:count]
    rows_out, scaled_out, d_gate_out, d_up_out, d_probs_out = refs[count : count + 5]
    near_out, far_out, rows_ref = refs[count + 5 :]
    results = [out.at[b] for out in (near_out, far_out) for b in range(count // 2)]
    e = pl.program_id(0)

    @pl.when(e == 0)
    def _():
        pick_rows(picks_ref, blocks, rows_ref, slot_count, 512)

    rows = rows_ref[e]
    rows_out[0] = rows
    pre, up = nn(rows, gate_ref[0]), nn(rows, up_ref[0])
    cot_acts = acts_ref[0]
    own_slots = pl.ds(pl.multiple_of(e * slot_count, slot_count), slot_count)
    own_picks = [picks_ref[b, own_slots, :].astype(F32) for b in range(count)]
    gate = jnp.concatenate(
        [
            jnp.sum(pick * gates_ref[b, pl.ds(e, 1), :], axis=1, keepdims=True)
            for b, pick in enumerate(own_picks)
        ],
        axis=0,
    )
    sig = jax.nn.sigmoid(pre)
    silu = pre * sig
    acts = silu * up
    scaled_out[0] = (gate * acts).astype(BF16)
    inner = jnp.sum(acts.astype(BF16).astype(F32) * cot_acts, axis=1, keepdims=True)
    for b, pick in enumerate(own_picks):
        here = inner[b * slot_count : (b + 1) * slot_count]
        d_probs_out[b, pl.ds(e, 1), :] = jnp.sum(pick * here, axis=0, keepdims=True)
    d_acts = gate * cot_acts
    d_pre = (d_acts * up * sig * (1.0 + pre * (1.0 - sig))).astype(BF16)
    d_up = (d_acts * silu).astype(BF16)
    d_gate_out[0] = d_pre
    d_up_out[0] = d_up
    rows_ref[e] = (nt(d_pre, gate_ref[0]) + nt(d_up, up_ref[0])).astype(BF16)

    @pl.when(e == pl.num_programs(0) - 1)
    def _():
        give_rows(picks_ref, rows_ref, results, slot_count, 512)


def out_kernel(count, slot_count, picks_ref, scaled_ref, down_ref, *refs):
    near_out, far_out, rows_ref = refs
    results = [out.at[b] for out in (near_out, far_out) for b in range(count // 2)]
    e = pl.program_id(0)
    rows_ref[e] = nn(scaled_ref[0], down_ref[0]).astype(BF16)

    @pl.when(e == pl.num_programs(0) - 1)
    def _():
        give_rows(picks_ref, rows_ref, results, slot_count, 512)


def per_expert(*shape):
    return pl.BlockSpec((1,) + shape, lambda e: (e,) + (0,) * len(shape))


def resident(*shape):
    return pl.BlockSpec(shape, lambda e: (0,) * len(shape), pipeline_mode=pl.Buffered(1))


def cot_chunk(picks, w_down, blocks, slot_count):
    experts, hidden, width = w_down.shape
    count, tokens = len(blocks), blocks[0].shape[0]
    rows = count * slot_count
    return pl.pallas_call(
        functools.partial(cot_kernel, count, slot_count),
        grid=(experts,),
        in_specs=[resident(*picks.shape), per_expert(hidden, width)] + [resident(tokens, width)] * count,
        out_specs=[per_expert(rows, width), per_expert(rows, hidden)],
        out_shape=[
            jax.ShapeDtypeStruct((experts, rows, width), BF16),
            jax.ShapeDtypeStruct((experts, rows, hidden), F32),
        ],
        scratch_shapes=[pltpu.VMEM((experts, rows, width), BF16)],
        compiler_params=pltpu.CompilerParams(vmem_limit_bytes=VMEM_GRANT),
        cost_estimate=pl.CostEstimate(
            flops=2 * experts * rows * width * (hidden + tokens),
            bytes_accessed=2 * (count * tokens * width + experts * (rows + hidden) * width),
            transcendentals=0,
        ),
    )(picks, w_down, *blocks)


def main_chunk(picks, gates, cot_acts, w_gate, w_up, blocks, slot_count):
    experts, width, hidden = w_gate.shape
    count, tokens = len(blocks), blocks[0].shape[0]
    rows = count * slot_count
    outs = pl.pallas_call(
        functools.partial(main_kernel, count, slot_count),
        grid=(experts,),
        in_specs=[
            resident(*picks.shape),
            resident(*gates.shape),
            per_expert(rows, hidden),
            per_expert(width, hidden),
            per_expert(width, hidden),
        ]
        + [resident(tokens, width)] * count,
        out_specs=[
            per_expert(rows, width),
            per_expert(rows, hidden),
            per_expert(rows, hidden),
            per_expert(rows, hidden),
            resident(*gates.shape),
        ]
        + [resident(count // 2, tokens, width)] * 2,
        out_shape=[
            jax.ShapeDtypeStruct((experts, rows, width), BF16),
            jax.ShapeDtypeStruct((experts, rows, hidden), BF16),
            jax.ShapeDtypeStruct((experts, rows, hidden), BF16),
            jax.ShapeDtypeStruct((experts, rows, hidden), BF16),
            jax.ShapeDtypeStruct(gates.shape, F32),
        ]
        + [jax.ShapeDtypeStruct((count // 2, tokens, width), BF16)] * 2,
        scratch_shapes=[pltpu.VMEM((experts, rows, width), BF16)],
        compiler_params=pltpu.CompilerParams(vmem_limit_bytes=VMEM_GRANT),
        cost_estimate=pl.CostEstimate(
            flops=2 * experts * rows * width * (4 * hidden + 2 * tokens),
            bytes_accessed=2 * (2 * count * tokens * width + experts * (rows + 2 * hidden) * width),
            transcendentals=experts * rows * hidden,
        ),
    )(picks, gates, cot_acts, w_gate, w_up, *blocks)
    return outs[:5], outs[5:]


def out_chunk(picks, scaled, w_down, slot_count):
    experts, hidden, width = w_down.shape
    count, _, tokens = picks.shape
    rows = count * slot_count
    return pl.pallas_call(
        functools.partial(out_kernel, count, slot_count),
        grid=(experts,),
        in_specs=[resident(*picks.shape), per_expert(rows, hidden), per_expert(hidden, width)],
        out_specs=[resident(count // 2, tokens, width)] * 2,
        out_shape=[jax.ShapeDtypeStruct((count // 2, tokens, width), BF16)] * 2,
        scratch_shapes=[pltpu.VMEM((experts, rows, width), BF16)],
        compiler_params=pltpu.CompilerParams(vmem_limit_bytes=VMEM_GRANT),
        cost_estimate=pl.CostEstimate(
            flops=2 * experts * rows * width * (hidden + tokens),
            bytes_accessed=2 * (count * tokens * width + experts * (rows + hidden) * width),
            transcendentals=0,
        ),
    )(picks, scaled, w_down)


def grad_kernel(count, *refs):
    rows, cots, scaled, d_gate, d_up = (refs[i * count : (i + 1) * count] for i in range(5))
    gate_out, up_out, down_out = refs[-3:]

    def total(lefts, rights):
        value = None
        for left, right in zip(lefts, rights):
            term = contract_rows(left[0], right[0])
            value = term if value is None else value + term
        return value

    gate_out[0] = total(rows, d_gate)
    up_out[0] = total(rows, d_up)
    down_out[0] = total(scaled, cots)


def expert_grads(rows, cots, scaled, d_gate, d_up, first, last, earlier=None, tile=512):
    count, experts, width = len(rows), rows[0].shape[0], rows[0].shape[2]
    hidden = scaled[0].shape[2]
    slots = sum(part.shape[1] for part in rows)
    wide = [pl.BlockSpec((1, part.shape[1], tile), lambda e, n: (first + e, 0, n)) for part in rows]
    narrow = [pl.BlockSpec((1, part.shape[1], hidden), lambda e, n: (first + e, 0, 0)) for part in rows]
    tall = pl.BlockSpec((1, tile, hidden), lambda e, n: (first + e, n, 0))
    given = [] if earlier is None else list(earlier)
    return pl.pallas_call(
        functools.partial(grad_kernel, count),
        grid=(last - first, width // tile),
        in_specs=wide * 2 + narrow * 3 + [pl.BlockSpec(memory_space=pl.ANY)] * len(given),
        out_specs=[tall, tall, pl.BlockSpec((1, hidden, tile), lambda e, n: (first + e, 0, n))],
        out_shape=[
            jax.ShapeDtypeStruct((experts, width, hidden), F32),
            jax.ShapeDtypeStruct((experts, width, hidden), F32),
            jax.ShapeDtypeStruct((experts, hidden, width), F32),
        ],
        input_output_aliases={5 * count + i: i for i in range(len(given))},
        compiler_params=pltpu.CompilerParams(vmem_limit_bytes=VMEM_GRANT),
        cost_estimate=pl.CostEstimate(
            flops=6 * (last - first) * slots * width * hidden,
            bytes_accessed=(last - first) * (4 * slots * width + 12 * width * hidden),
            transcendentals=0,
        ),
    )(*rows, *cots, *scaled, *d_gate, *d_up, *given)


def qkv_kernel(*refs):
    blocks, (q_w, k_w, v_w, q_out, k_out, v_out, q_sq, k_sq) = refs[:-8], refs[-8:]
    lanes = q_sq.shape[1]
    rows = blocks[0].shape[0]
    for b, block in enumerate(blocks):
        here = pl.ds(b * rows, rows)
        for weight, out, squares in ((q_w, q_out, q_sq), (k_w, k_out, k_sq)):
            value = nn(block[...], weight[...])
            out[here, :] = value
            value = value * value
            total = value[:, :lanes]
            for low in range(lanes, value.shape[1], lanes):
                total = total + value[:, low : low + lanes]

            @pl.when(pl.program_id(0) == 0)
            def _(squares=squares, total=total):
                squares[here, :] = total

            @pl.when(pl.program_id(0) > 0)
            def _(squares=squares, total=total):
                squares[here, :] += total

        v_out[here, :] = nn(block[...], v_w[...]).astype(BF16)


def qkv(blocks, w_query, w_key, w_value, tile=256):
    rows, depth = blocks[0].shape
    width = w_query.shape[1]
    count = len(blocks) * rows
    weight = pl.BlockSpec((depth, tile), lambda n: (0, n))
    out = pl.BlockSpec((count, tile), lambda n: (0, n))
    return pl.pallas_call(
        qkv_kernel,
        grid=(width // tile,),
        in_specs=[resident(rows, depth)] * len(blocks) + [weight] * 3,
        out_specs=[out] * 3 + [resident(count, HDIM)] * 2,
        out_shape=[
            jax.ShapeDtypeStruct((count, width), F32),
            jax.ShapeDtypeStruct((count, width), F32),
            jax.ShapeDtypeStruct((count, width), BF16),
            jax.ShapeDtypeStruct((count, HDIM), F32),
            jax.ShapeDtypeStruct((count, HDIM), F32),
        ],
        compiler_params=pltpu.CompilerParams(vmem_limit_bytes=VMEM_GRANT),
        cost_estimate=pl.CostEstimate(
            flops=6 * count * depth * width,
            bytes_accessed=2 * count * depth + 6 * depth * width + 10 * count * width,
            transcendentals=0,
        ),
    )(*blocks, w_query, w_key, w_value)


def pair_kernel(near_ref, far_ref, *outs):
    for b, out in enumerate(outs):
        out[...] = (near_ref[b].astype(F32) + far_ref[b].astype(F32)).astype(BF16)


def pair_sum(near, far, tile=64):
    count, rows, width = near.shape
    stack = pl.BlockSpec((count, tile, width), lambda i: (0, i, 0))
    return pl.pallas_call(
        pair_kernel,
        grid=(rows // tile,),
        in_specs=[stack, stack],
        out_specs=[pl.BlockSpec((tile, width), lambda i: (i, 0))] * count,
        out_shape=[jax.ShapeDtypeStruct((rows, width), BF16)] * count,
        compiler_params=pltpu.CompilerParams(vmem_limit_bytes=VMEM_GRANT),
        cost_estimate=pl.CostEstimate(
            flops=count * rows * width, bytes_accessed=6 * count * rows * width, transcendentals=0
        ),
    )(near, far)


def turn(values, cosine, sine):
    return values * cosine + pltpu.roll(values, values.shape[1] // 2, 1) * sine


def attend_kernel(
    row_block, scale, q_ref, k_ref, v_ref, cols_ref, qg_ref, kg_ref, cos_ref, sin_ref, kpos_ref,
    out_ref, lse_ref, qrot_ref, krot_ref,
):
    cosine, sine = cos_ref[...], sin_ref[...]
    qrot_ref[...] = turn(q_ref[...] * cols_ref[:, 0:1] * qg_ref[...], cosine, sine).astype(BF16)
    krot_ref[...] = turn(k_ref[...] * cols_ref[:, 1:2] * kg_ref[...], cosine, sine).astype(BF16)
    for low in range(0, q_ref.shape[0], row_block):
        rows = pl.ds(low, row_block)
        scores = nt(qrot_ref[rows, :], krot_ref[...]) * scale
        scores = jnp.where(kpos_ref[...] <= cols_ref[rows, 2:3], scores, -1e30)
        top = jnp.max(scores, axis=1, keepdims=True)
        powers = jnp.exp(scores - top)
        total = jnp.sum(powers, axis=1, keepdims=True)
        soft = (powers * (1.0 / total)).astype(BF16)
        out_ref[rows, :] = nn(soft, v_ref[...]).astype(BF16)
        lse_ref[rows, :] = jnp.broadcast_to(top + jnp.log(total), (row_block, HDIM))


def attend_back_kernel(
    row_block, scale, q_ref, k_ref, v_ref, qrot_ref, krot_ref, do_ref, lse_ref, cols_ref, qg_ref, kg_ref,
    cos_ref, sin_ref, kpos_ref,
    dq_ref, dk_ref, dv_ref, qgain_ref, kgain_ref, qin_ref, kin_ref, dq_acc, dk_acc, dv_acc,
):
    for low in range(0, q_ref.shape[0], row_block):
        rows = pl.ds(low, row_block)
        query, d_out = qrot_ref[rows, :], do_ref[rows, :]
        scores = nt(query, krot_ref[...]) * scale
        soft = jnp.where(kpos_ref[...] <= cols_ref[rows, 2:3], jnp.exp(scores - lse_ref[rows, 0:1]), 0.0)
        d_weights = nt(d_out, v_ref[...])
        spread = soft * d_weights
        mean = jnp.sum(spread, axis=1, keepdims=True)
        d_scores = (spread - soft * mean).astype(BF16)
        dq_acc[rows, :] = nn(d_scores, krot_ref[...]) * scale
        d_keys = contract_rows(d_scores, query)
        d_values = contract_rows(soft.astype(BF16), d_out)
        if low:
            dk_acc[...] += d_keys
            dv_acc[...] += d_values
        else:
            dk_acc[...] = d_keys
            dv_acc[...] = d_values
    dv_ref[...] = dv_acc[...].astype(BF16)
    cosine, sine = cos_ref[...], -sin_ref[...]
    for lane, raw_ref, gain_ref, grad, hat_ref, gain_out, inner_out in (
        (0, q_ref, qg_ref, dq_acc[...], dq_ref, qgain_ref, qin_ref),
        (1, k_ref, kg_ref, dk_acc[...] * scale, dk_ref, kgain_ref, kin_ref),
    ):
        hat = raw_ref[...] * cols_ref[:, lane : lane + 1]
        turned = turn(grad, cosine, sine)
        gain_out[...] = jnp.sum(turned * hat, axis=0, keepdims=True)
        d_hat = turned * gain_ref[...]
        hat_ref[...] = d_hat
        inner = d_hat * hat

        @pl.when(pl.program_id(0) == 0)
        def _(inner=inner, inner_out=inner_out):
            inner_out[...] = inner

        @pl.when(pl.program_id(0) > 0)
        def _(inner=inner, inner_out=inner_out):
            inner_out[...] += inner


def head_columns(rows):
    return pl.BlockSpec((rows, HDIM), lambda h: (0, h))


def whole(*shape):
    return pl.BlockSpec(shape, lambda h: (0,) * len(shape))


def attend_forward(q_raw, k_raw, v_low, cols, q_gain, k_gain, cosine, sine, kpos):
    seq_len, width = q_raw.shape
    heads = width // HDIM
    part, one = head_columns(seq_len), head_columns(1)
    return pl.pallas_call(
        functools.partial(attend_kernel, min(256, seq_len), HDIM ** (-0.5)),
        grid=(heads,),
        in_specs=[part, part, part, whole(seq_len, HDIM), one, one]
        + [whole(seq_len, HDIM), whole(seq_len, HDIM), whole(1, seq_len)],
        out_specs=[part, part, part, part],
        out_shape=[
            jax.ShapeDtypeStruct((seq_len, width), BF16),
            jax.ShapeDtypeStruct((seq_len, width), F32),
            jax.ShapeDtypeStruct((seq_len, width), BF16),
            jax.ShapeDtypeStruct((seq_len, width), BF16),
        ],
        compiler_params=pltpu.CompilerParams(vmem_limit_bytes=VMEM_GRANT),
        cost_estimate=pl.CostEstimate(
            flops=4 * seq_len * seq_len * width,
            bytes_accessed=20 * seq_len * width,
            transcendentals=heads * seq_len * seq_len,
        ),
    )(q_raw, k_raw, v_low, cols, q_gain, k_gain, cosine, sine, kpos)


def attend_backward(
    q_raw, k_raw, v_low, q_rot, k_rot, d_out, lse, cols, q_gain, k_gain, cosine, sine, kpos
):
    seq_len, width = q_raw.shape
    heads = width // HDIM
    part, one = head_columns(seq_len), head_columns(1)
    return pl.pallas_call(
        functools.partial(attend_back_kernel, min(256, seq_len), HDIM ** (-0.5)),
        grid=(heads,),
        in_specs=[part, part, part, part, part, part, part, whole(seq_len, HDIM), one, one]
        + [whole(seq_len, HDIM), whole(seq_len, HDIM), whole(1, seq_len)],
        out_specs=[part, part, part, one, one, whole(seq_len, HDIM), whole(seq_len, HDIM)],
        out_shape=[
            jax.ShapeDtypeStruct((seq_len, width), F32),
            jax.ShapeDtypeStruct((seq_len, width), F32),
            jax.ShapeDtypeStruct((seq_len, width), BF16),
            jax.ShapeDtypeStruct((1, width), F32),
            jax.ShapeDtypeStruct((1, width), F32),
            jax.ShapeDtypeStruct((seq_len, HDIM), F32),
            jax.ShapeDtypeStruct((seq_len, HDIM), F32),
        ],
        scratch_shapes=[pltpu.VMEM((seq_len, HDIM), F32)] * 3,
        compiler_params=pltpu.CompilerParams(vmem_limit_bytes=VMEM_GRANT),
        cost_estimate=pl.CostEstimate(
            flops=10 * seq_len * seq_len * width,
            bytes_accessed=32 * seq_len * width,
            transcendentals=heads * seq_len * seq_len,
        ),
    )(q_raw, k_raw, v_low, q_rot, k_rot, d_out, lse, cols, q_gain, k_gain, cosine, sine, kpos)


def local_gathered(
    hidden_in,
    cotangent,
    seq_lengths,
    expert_ids,
    attn_gain,
    w_query,
    w_key,
    w_value,
    query_gain,
    key_gain,
    w_out,
    ffn_gain,
    w_router,
    w_gate,
    w_up,
    w_down,
):
    tensor_count = lax.axis_size("tensor")
    group_count = lax.axis_size("dp")
    tok_rows, model_width = hidden_in.shape
    topk = expert_ids.shape[1]
    expert_total = w_router.shape[1]
    experts = w_gate.shape[0]
    slot_count = tok_rows * topk // expert_total
    devices = len(PLACES)
    seq_len = tok_rows * tensor_count
    local_width = w_query.shape[1]
    half_width = HDIM // 2
    live_length = seq_lengths[0]
    absolute, position = place_indices()

    member = lax.axis_index("tensor")
    blocks_at = member ^ jnp.arange(tensor_count)
    cosine, sine = (
        table.reshape(tensor_count, tok_rows, half_width)[blocks_at].reshape(seq_len, half_width)
        for table in rope_tables(seq_len, HDIM)
    )
    cosine = jnp.concatenate([cosine, cosine], axis=1)
    sine = jnp.concatenate([-sine, sine], axis=1)
    positions = (blocks_at[:, None] * tok_rows + jnp.arange(tok_rows)[None, :]).reshape(-1)
    never = 2 * seq_len
    key_pos = jnp.where(positions < live_length, positions, never).astype(F32)[None, :]

    def token_sums(*values):
        stacked = jnp.stack([value.reshape(tensor_count, tok_rows) for value in values])
        summed = lax.psum(stacked[:, blocks_at], "tensor")
        return summed[:, blocks_at].reshape(len(values), seq_len)

    def to_groups(by_expert):
        copies = jnp.broadcast_to(
            by_expert.reshape(group_count, 1, experts, tok_rows),
            (group_count, tensor_count, experts, tok_rows),
        ).reshape(devices, experts, tok_rows)
        return lax.all_to_all(copies, BOTH, split_axis=0, concat_axis=0, tiled=True)[absolute]

    resid = hidden_in.astype(F32)
    scale_one = rms_scale(resid)
    normed = resid * scale_one
    attn_in = (normed * attn_gain.astype(F32)).astype(BF16)
    q_gain = query_gain.astype(F32)[None, :]
    k_gain = key_gain.astype(F32)[None, :]

    hot = jnp.any(expert_ids.T[None, :, :] == jnp.arange(expert_total)[:, None, None], axis=1)
    earlier = jnp.triu(jnp.ones((tok_rows, tok_rows), F32), 1).astype(BF16)
    rank = jnp.dot(hot.astype(BF16), earlier, preferred_element_type=F32)
    slot_of = to_groups(jnp.where(hot, rank, -1.0))
    slots = jnp.arange(slot_count, dtype=F32)
    picks_wide = (slot_of[:, :, None, :] == slots[None, None, :, None]).astype(BF16)
    picks = [
        picks_wide[low : low + len(chunk)].reshape(len(chunk), experts * slot_count, tok_rows)
        for chunk, low in zip(CHUNKS, STARTS)
    ]

    stages = Stages(attn_in)
    cot, ffn = Gather(cotangent), Gather(None)
    d_sum, out_sum = Scatter(), Scatter()
    order = range(len(CHUNKS))
    cot_rows, cot_acts, kept = {}, {}, {}

    def advance(works=(), extra=(), **hops):
        tables = {"cot": cot, "ffn": ffn, "d": d_sum, "out": out_sum}
        sends = list(extra)
        spans = []
        for name, moves in hops.items():
            spans.append((tables[name], moves, len(sends)))
            sends += tables[name].sends(moves)
        got, made = stages.run(sends, works)
        for table, moves, low in spans:
            table.take(moves, got[low : low + len(moves)])
        return got[: len(extra)], made

    def cot_work(i):
        values, crossing, late = cot.chunk(i)

        def work(picks_i, w_down_i, values, crossing):
            return cot_chunk(picks_i, w_down_i, Gather.complete(i, values, crossing, late), slot_count)

        return work, (picks[i], w_down, values, crossing)

    def cot_done(i, made):
        cot_rows[i], cot_acts[i] = made

    def main_work(i):
        values, crossing, late = ffn.chunk(i)

        def work(picks_i, gates_i, acts_i, gate_w, up_w, values, crossing):
            blocks = Gather.complete(i, values, crossing, late)
            return main_chunk(picks_i, gates_i, acts_i, gate_w, up_w, blocks, slot_count)

        gates_i = token_gates[STARTS[i] : STARTS[i] + len(CHUNKS[i])]
        return work, (picks[i], gates_i, cot_acts[i], w_gate, w_up, values, crossing)

    def out_work(i):
        def work(picks_i, scaled_i, w_down_i):
            return out_chunk(picks_i, scaled_i, w_down_i, slot_count)

        return work, (picks[i], kept[i][1], w_down)

    (across, mate), _ = advance(
        extra=[(attn_in, "y"), (attn_in, "c")], cot=[("z", (0, 0, 0)), ("x", (0, 0, 0))]
    )

    def project(block, mate, across, w_query, w_key, w_value):
        blocks = [block, mate, across, send(across, "c")]
        q_raw, k_raw, v_low, q_square, k_square = qkv(blocks, w_query, w_key, w_value)
        squares = token_sums(jnp.sum(q_square, axis=1), jnp.sum(k_square, axis=1))
        return jnp.concatenate(blocks, axis=0), q_raw, k_raw, v_low, squares

    _, (made,) = advance(
        [(project, (attn_in, mate, across, w_query, w_key, w_value))],
        cot=[("z", (1, 0, 0)), ("x", (1, 0, 0)), ("y", (0, 0, 0)), ("c", (0, 0, 0)), ("c", (1, 0, 0))],
    )
    gathered, q_raw, k_raw, v_low, squares = made

    def columns_of(squares):
        scales = lax.rsqrt(squares / model_width + EPS)
        columns = jnp.stack([scales[0], scales[1], positions.astype(F32)], axis=1)
        return jnp.pad(columns, ((0, 0), (0, HDIM - columns.shape[1])))

    cols = columns_of(squares)
    _, (made,) = advance(
        [(attend_forward, (q_raw, k_raw, v_low, cols, q_gain, k_gain, cosine, sine, key_pos))],
        cot=[("z", (2, 0, 0)), ("x", (2, 0, 0)), ("y", (1, 0, 0)), ("c", (0, 1, 0)), ("c", (0, 0, 1))],
    )
    o_low, lse, q_rot, k_rot = made

    def project_back(o_low, w_out):
        parts = [
            jnp.dot(o_low[r * tok_rows : (r + 1) * tok_rows], w_out, preferred_element_type=F32).astype(BF16)
            for r in range(tensor_count)
        ]
        across = add_low(parts[2], send(parts[3], "c"))
        return add_wide(parts[0], send(parts[1], "c")) + send(across, "y").astype(F32)

    _, (attn_rows, made) = advance(
        [(project_back, (o_low, w_out)), cot_work(0)],
        cot=[("x", (3, 0, 0)), ("c", (2, 0, 0)), ("c", (1, 1, 0))],
    )
    cot_done(0, made)
    mixed = resid + attn_rows
    scale_two = rms_scale(mixed)
    mixed_norm = mixed * scale_two
    ffn_in = (mixed_norm * ffn_gain.astype(F32)).astype(BF16)
    ffn.held[0, 0, 0, 0] = ffn_in

    def route(ffn_in, w_router):
        logits = jnp.dot(ffn_in, w_router, preferred_element_type=F32)
        router_probs = jax.nn.softmax(logits, axis=-1)
        return router_probs, to_groups(router_probs.T)

    _, ((router_probs, token_gates),) = advance(
        [(route, (ffn_in, w_router))],
        ffn=[("z", (0, 0, 0)), ("x", (0, 0, 0)), ("y", (0, 0, 0))],
        cot=[("c", (1, 0, 1)), ("c", (2, 1, 0))],
    )
    _, (made,) = advance(
        [cot_work(1)],
        ffn=[("z", (1, 0, 0)), ("x", (1, 0, 0)), ("y", (1, 0, 0))]
        + [("c", (0, 0, 0)), ("c", (0, 1, 0)), ("c", (1, 0, 0)), ("c", (0, 0, 1))],
    )
    cot_done(1, made)
    _, (made,) = advance(
        [main_work(0)],
        ffn=[("z", (2, 0, 0)), ("x", (2, 0, 0)), ("c", (2, 0, 0))],
        cot=[("y", (2, 0, 0)), ("c", (3, 0, 0))],
    )
    kept[0], near, far = made[0], *made[1]
    _, (made,) = advance(
        [(core_sum, (near, far))],
        ffn=[("x", (3, 0, 0)), ("c", (1, 1, 0)), ("c", (1, 0, 1)), ("c", (2, 1, 0))],
        cot=[("y", (3, 0, 0))],
    )
    d_sum.put(0, made)
    _, (made,) = advance(
        [main_work(1)],
        ffn=[("y", (2, 0, 0))],
        cot=[("x", (0, 0, 1)), ("c", (3, 1, 0)), ("c", (2, 0, 1))],
    )
    kept[1], near, far = made[0], *made[1]
    _, (made, other) = advance(
        [(core_sum, (near, far)), cot_work(2)],
        ffn=[("y", (3, 0, 0)), ("c", (3, 0, 0)), ("c", (3, 1, 0))],
        cot=[("x", (1, 0, 1))],
    )
    d_sum.put(1, made)
    cot_done(2, other)
    _, (made,) = advance(
        [main_work(2)],
        cot=[("x", (2, 0, 1)), ("y", (3, 1, 0)), ("c", (0, 1, 1))],
    )
    kept[2], near, far = made[0], *made[1]
    _, (made, other, third) = advance(
        [(core_sum, (near, far)), cot_work(3), cot_work(4)],
        ffn=[("x", (2, 0, 1)), ("y", (1, 1, 0))],
    )
    d_sum.put(2, made)
    cot_done(3, other)
    cot_done(4, third)
    _, (made,) = advance([main_work(3)], ffn=[("x", (3, 0, 1)), ("y", (0, 1, 0))])
    kept[3], near, far = made[0], *made[1]
    _, (made,) = advance([(core_sum, (near, far))], ffn=[("c", (0, 1, 1)), ("c", (3, 1, 1))])
    d_sum.put(3, made)

    def last_main(*args):
        saved, (near, far) = main_work_four[0](*args)
        return saved, core_sum(near, far)

    main_work_four = main_work(4)
    _, (made,) = advance([(last_main, main_work_four[1])], d=[("x", (1, 1, 1)), ("y", (2, 1, 1))])
    kept[4] = made[0]
    d_sum.put(4, made[1])

    def return_probs(*d_probs):
        d_probs = jnp.concatenate(d_probs, axis=0)[position]
        arrived = lax.all_to_all(d_probs, BOTH, split_axis=0, concat_axis=0, tiled=True)
        arrived = arrived.reshape(group_count, tensor_count, experts, tok_rows)
        return jnp.sum(arrived, axis=1).reshape(expert_total, tok_rows).T

    outs = {}
    _, (outs[0], d_probs) = advance(
        [out_work(0), (return_probs, tuple(kept[i][4] for i in order))],
        d=[("x", (3, 1, 1)), ("y", (0, 1, 1))],
    )
    _, (outs[1], made) = advance(
        [out_work(1), (core_sum, tuple(outs[0]))], d=[("x", (1, 1, 0)), ("y", (1, 0, 1))]
    )
    out_sum.put(0, made)
    _, (outs[2], made) = advance(
        [out_work(2), (core_sum, tuple(outs[1]))],
        d=[("x", (2, 1, 0)), ("y", (2, 0, 1)), ("z", (1, 0, 0))],
    )
    out_sum.put(1, made)
    _, (outs[3], outs[4], made) = advance(
        [out_work(3), out_work(4), (core_sum, tuple(outs[2]))],
        d=[("x", (3, 1, 0)), ("y", (3, 0, 1)), ("z", (2, 0, 0))],
    )
    out_sum.put(2, made)
    _, (made, other) = advance(
        [(core_sum, tuple(outs[3])), (core_sum, tuple(outs[4]))],
        d=[("x", (0, 1, 0)), ("y", (0, 0, 1)), ("z", (3, 0, 0))],
    )
    out_sum.put(3, made)
    out_sum.put(4, other)
    d_ffn = d_sum.total()

    d_result = cotangent.astype(F32)
    d_logits = (
        router_probs * (d_probs - jnp.sum(router_probs * d_probs, axis=-1, keepdims=True))
    ).astype(BF16)
    router_part = contract_rows(d_logits, ffn_in)
    d_ffn = d_ffn + times_transpose(d_logits, w_router)
    ffn_gain_part = jnp.sum(d_ffn * mixed_norm, axis=0)
    d_norm_two = d_ffn * ffn_gain.astype(F32)
    d_mixed = d_result + scale_two * (
        d_norm_two - mixed_norm * jnp.mean(d_norm_two * mixed_norm, axis=-1, keepdims=True)
    )
    d_attn = d_mixed.astype(BF16)
    router_sums = jnp.concatenate(
        [router_part, jnp.broadcast_to(ffn_gain_part[None, :], (8, model_width))], axis=0
    )

    (across, mate, other), _ = advance(
        extra=[(d_attn, "y"), (d_attn, "c"), (router_sums, "z1")], out=[("x", (1, 1, 1))]
    )
    router_sums = router_sums + other

    def attend_back(d_attn, mate, across, o_low, w_out, gathered, *rest):
        d_attn_all = jnp.concatenate([d_attn, mate, across, send(across, "c")], axis=0)
        d_attended = times_transpose(d_attn_all, w_out).astype(BF16)
        q_raw, k_raw, v_low, q_rot, k_rot, lse, cols = rest
        made = attend_backward(
            q_raw, k_raw, v_low, q_rot, k_rot, d_attended, lse, cols, q_gain, k_gain, cosine, sine, key_pos
        )
        return made, contract_rows(o_low, d_attn_all).astype(BF16), contract_rows(gathered, made[2]).astype(BF16)

    _, (made,) = advance(
        [
            (
                attend_back,
                (d_attn, mate, across, o_low, w_out, gathered, q_raw, k_raw, v_low, q_rot, k_rot, lse, cols),
            )
        ],
        out=[("x", (3, 1, 1)), ("x", (1, 1, 0)), ("y", (2, 1, 1)), ("y", (0, 1, 1))],
    )
    (dq_hat, dk_hat, dv_raw, query_gain_part, key_gain_part, q_inner, k_inner), grad_w_out, grad_value = made
    grad_w_out, grad_value = lax.psum((grad_w_out, grad_value), "dp")

    def norm_back(q_raw, k_raw, cols, dq_hat, dk_hat, q_inner, k_inner):
        inner = token_sums(jnp.sum(q_inner, axis=1), jnp.sum(k_inner, axis=1)) / model_width
        raws = []
        for n, (raw, d_hat) in enumerate(((q_raw, dq_hat), (k_raw, dk_hat))):
            scale = cols[:, n : n + 1]
            raws.append((scale * (d_hat - raw * scale * inner[n][:, None])).astype(BF16))
        return raws

    (other,), ((dq_raw, dk_raw),) = advance(
        [(norm_back, (q_raw, k_raw, cols, dq_hat, dk_hat, q_inner, k_inner))],
        extra=[(router_sums, "z2")],
        out=[("x", (3, 1, 0)), ("y", (1, 0, 1))],
    )
    router_sums = router_sums + other

    def projections_back(gathered, dq_raw, dk_raw, dv_raw, w_query, w_key, w_value):
        grads = [contract_rows(gathered, part).astype(BF16) for part in (dk_raw, dq_raw)]
        total_term = times_transpose(dq_raw, w_query)
        total_term = total_term + times_transpose(dk_raw, w_key)
        total_term = (total_term + times_transpose(dv_raw, w_value)).astype(BF16)
        return grads, total_term

    (other,), (((grad_key, grad_query), total_term),) = advance(
        [(projections_back, (gathered, dq_raw, dk_raw, dv_raw, w_query, w_key, w_value))],
        extra=[(router_sums, "c")],
        out=[("x", (2, 1, 0)), ("y", (2, 0, 1)), ("z", (1, 0, 0))],
    )
    router_sums = router_sums + other

    key_sum, query_sum = DpSum(grad_key), DpSum(grad_query)

    def saved(n):
        return [kept[i][n] for i in order]

    def grads_of(first, last, earlier=None):
        all_cots = [cot_rows[i] for i in order]

        def work(*args):
            return expert_grads(*args[:5], first, last, args[5] if len(args) > 5 else None)

        args = (saved(0), all_cots, saved(1), saved(2), saved(3))
        return work, args if earlier is None else args + (earlier,)

    thirds = [experts * n // 3 for n in range(4)]
    parts = jnp.split(total_term, tensor_count, axis=0)
    (d_far, d_near, *got), _ = advance(
        extra=[(parts[3], "c"), (parts[1], "c")] + key_sum.split_x(), out=[("y", (3, 0, 1))]
    )
    key_sum.add_x(got)
    (d_across, *got), (made,) = advance(
        [grads_of(thirds[0], thirds[1])],
        extra=[(add_low(parts[2], d_far), "y")] + query_sum.split_x() + key_sum.split_z(),
    )
    query_sum.add_x(got[:1])
    key_sum.add_z(got[1:])
    d_attn_in = add_wide(parts[0], d_near, d_across)
    attn_gain_part = jnp.sum(d_attn_in * normed, axis=0)
    d_norm_one = d_attn_in * attn_gain.astype(F32)
    d_input = d_mixed + scale_one * (
        d_norm_one - normed * jnp.mean(d_norm_one * normed, axis=-1, keepdims=True)
    )
    got, (made,) = advance(
        [grads_of(thirds[1], thirds[2], made)], extra=key_sum.join_z(), out=[("x", (0, 1, 0)), ("y", (0, 0, 1))]
    )
    key_sum.took_z(got)
    (other, *got), ((grad_w_gate, grad_w_up, grad_w_down),) = advance(
        [grads_of(thirds[2], thirds[3], made)],
        extra=[(router_sums, "y")] + key_sum.join_x() + query_sum.split_z(),
    )
    router_sums = router_sums + other
    key_sum.took_x(got[:1])
    query_sum.add_z(got[1:])
    (other, *got), _ = advance(
        extra=[(attn_gain_part, "c")] + query_sum.join_z(), out=[("z", (2, 0, 0))]
    )
    attn_gain_part = attn_gain_part + other
    query_sum.took_z(got)
    (other, third, *got), _ = advance(
        extra=[(attn_gain_part, "y"), (router_sums, "x")] + query_sum.join_x(), out=[("z", (3, 0, 0))]
    )
    query_sum.took_x(got)
    router_sums = router_sums + third
    gain_sums = small_sum(
        jnp.concatenate([attn_gain_part + other, query_gain_part[0], key_gain_part[0]]), ("x", "z1", "z2")
    )
    result = mixed + out_sum.total()
    return (
        result.astype(BF16),
        d_input.astype(BF16),
        query_sum.result,
        key_sum.result,
        grad_value.astype(F32),
        gain_sums[model_width : model_width + local_width],
        gain_sums[model_width + local_width :],
        grad_w_out.astype(F32),
        gain_sums[:model_width],
        router_sums[expert_total],
        router_sums[:expert_total].T,
        grad_w_gate,
        grad_w_up,
        grad_w_down,
    )


def local_sent(
    hidden_in,
    cotangent,
    seq_lengths,
    expert_ids,
    attn_gain,
    w_query,
    w_key,
    w_value,
    query_gain,
    key_gain,
    w_out,
    ffn_gain,
    w_router,
    w_gate,
    w_up,
    w_down,
):
    tensor_count = lax.axis_size("tensor")
    group_count = lax.axis_size("dp")
    device_total = tensor_count * group_count
    tok_rows, model_width = hidden_in.shape
    topk_count = expert_ids.shape[1]
    local_experts = w_gate.shape[0]
    expert_total = w_router.shape[1]
    slot_count = tok_rows * topk_count // expert_total
    per_group = local_experts * slot_count
    seq_len = tok_rows * tensor_count
    local_width = w_query.shape[1]
    head_width = HDIM
    local_heads = local_width // head_width
    block_rows = min(512, seq_len)
    block_count = seq_len // block_rows
    score_scale = head_width ** (-0.5)
    live_length = seq_lengths[0]
    cosine, sine_table = (table[:, None, :] for table in rope_tables(seq_len, head_width))
    key_pos = jnp.arange(seq_len)
    key_live = key_pos < live_length

    def send_out(rows_low):
        grouped_rows = rows_low.reshape(group_count, 1, per_group, model_width)
        copies = jnp.broadcast_to(
            grouped_rows, (group_count, tensor_count, per_group, model_width)
        ).reshape(device_total, per_group, model_width)
        arrived = lax.all_to_all(copies, ("dp", "tensor"), split_axis=0, concat_axis=0, tiled=True)
        return arrived.reshape(device_total, local_experts, slot_count, model_width)

    def send_back(parts_low):
        returned = lax.all_to_all(
            parts_low.reshape(device_total, per_group, model_width),
            ("dp", "tensor"),
            split_axis=0,
            concat_axis=0,
            tiled=True,
        )
        return jnp.sum(
            returned.reshape(group_count, tensor_count, per_group, model_width).astype(F32),
            axis=1,
        ).reshape(-1, model_width)

    resid = hidden_in.astype(F32)
    scale_one = rms_scale(resid)
    normed = resid * scale_one
    attn_in = (normed * attn_gain.astype(F32)).astype(BF16)
    gathered = lax.all_gather(attn_in, "tensor", axis=0, tiled=True)
    q_raw = jnp.dot(gathered, w_query, preferred_element_type=F32)
    k_raw = jnp.dot(gathered, w_key, preferred_element_type=F32)
    v_raw = jnp.dot(gathered, w_value, preferred_element_type=F32)
    q_square, k_square = lax.psum(
        (jnp.sum(q_raw * q_raw, axis=1), jnp.sum(k_raw * k_raw, axis=1)), "tensor"
    )
    q_rscale = lax.rsqrt(q_square / model_width + EPS)[:, None]
    k_rscale = lax.rsqrt(k_square / model_width + EPS)[:, None]
    query_hat = q_raw * q_rscale
    key_hat = k_raw * k_rscale
    q_gain = query_gain.astype(F32)
    k_gain = key_gain.astype(F32)
    q_rot = rotate(
        (query_hat * q_gain).reshape(seq_len, local_heads, head_width), cosine, sine_table
    ).astype(BF16)
    k_rot = rotate(
        (key_hat * k_gain).reshape(seq_len, local_heads, head_width), cosine, sine_table
    ).astype(BF16)
    v_low = v_raw.astype(BF16).reshape(seq_len, local_heads, head_width)
    starts = jnp.arange(block_count) * block_rows
    q_blocks = q_rot.reshape(block_count, block_rows, local_heads, head_width)

    def allowed_mask(row_start):
        q_pos = row_start + jnp.arange(block_rows)
        return ((key_pos[None, :] <= q_pos[:, None]) & key_live[None, :])[None]

    def attend(inputs):
        q_block, row_start = inputs
        scores = (
            jnp.einsum("qhd,khd->hqk", q_block, k_rot, preferred_element_type=F32)
            * score_scale
        )
        scores = jnp.where(allowed_mask(row_start), scores, -1e30)
        row_max = jnp.max(scores, axis=-1, keepdims=True)
        exp_scores = jnp.exp(scores - row_max)
        row_total = jnp.sum(exp_scores, axis=-1, keepdims=True)
        soft_low = (exp_scores / row_total).astype(BF16)
        attended = jnp.einsum("hqk,khd->qhd", soft_low, v_low, preferred_element_type=F32)
        return (attended, (row_max + jnp.log(row_total))[..., 0])

    o_blocks, lse_blocks = lax.map(attend, (q_blocks, starts))
    o_low = o_blocks.reshape(seq_len, local_width).astype(BF16)
    attn_rows = lax.psum_scatter(
        jnp.dot(o_low, w_out, preferred_element_type=F32),
        "tensor",
        scatter_dimension=0,
        tiled=True,
    )
    mixed = resid + attn_rows
    scale_two = rms_scale(mixed)
    mixed_norm = mixed * scale_two
    ffn_in = (mixed_norm * ffn_gain.astype(F32)).astype(BF16)
    logits = jnp.dot(ffn_in, w_router, preferred_element_type=F32)
    router_probs = jax.nn.softmax(logits, axis=-1)
    expert_hot = (expert_ids[:, :, None] == jnp.arange(expert_total)[None, None, :]).astype(
        F32
    )
    gate_values = jnp.einsum("tke,te->tk", expert_hot, router_probs)
    flat_ids = expert_ids.reshape(-1)
    sort_order = jnp.argsort(flat_ids, stable=True)
    inverse = jnp.argsort(sort_order)
    expert_in = send_out(ffn_in[sort_order // topk_count])
    gate_pre = jnp.einsum("secd,edf->secf", expert_in, w_gate, preferred_element_type=F32)
    up_pre = jnp.einsum("secd,edf->secf", expert_in, w_up, preferred_element_type=F32)
    silu_gate = jax.nn.silu(gate_pre)
    acts = (silu_gate * up_pre).astype(BF16)
    partial_value = jnp.einsum(
        "secf,efd->secd", acts, w_down, preferred_element_type=F32
    ).astype(BF16)
    out_sorted = send_back(partial_value)
    out_assign = out_sorted[inverse].reshape(tok_rows, topk_count, model_width)
    expert_mix = jnp.einsum("tk,tkd->td", gate_values, out_assign)
    result = mixed + expert_mix
    d_result = cotangent.astype(F32)
    d_gates = jnp.einsum("tkd,td->tk", out_assign, d_result)
    d_out = (
        (gate_values[:, :, None] * d_result[:, None, :])
        .astype(BF16)
        .reshape(-1, model_width)[sort_order]
    )
    d_arrived = send_out(d_out)
    d_acts = jnp.einsum("secd,efd->secf", d_arrived, w_down, preferred_element_type=F32)
    sigmoid_gate = jax.nn.sigmoid(gate_pre)
    d_gate_pre = (d_acts * up_pre * sigmoid_gate * (1.0 + gate_pre * (1.0 - sigmoid_gate))).astype(
        BF16
    )
    d_up_pre = (d_acts * silu_gate).astype(BF16)
    grad_w_down = jnp.einsum("secf,secd->efd", acts, d_arrived, preferred_element_type=F32)
    grad_w_gate = jnp.einsum(
        "secd,secf->edf", expert_in, d_gate_pre, preferred_element_type=F32
    )
    grad_w_up = jnp.einsum(
        "secd,secf->edf", expert_in, d_up_pre, preferred_element_type=F32
    )
    d_rows = (
        jnp.einsum("secf,edf->secd", d_gate_pre, w_gate, preferred_element_type=F32)
        + jnp.einsum("secf,edf->secd", d_up_pre, w_up, preferred_element_type=F32)
    ).astype(BF16)
    d_sorted = send_back(d_rows)
    d_ffn = jnp.sum(d_sorted[inverse].reshape(tok_rows, topk_count, model_width), axis=1)
    d_probs = jnp.einsum("tk,tke->te", d_gates, expert_hot)
    d_logits = (
        router_probs * (d_probs - jnp.sum(router_probs * d_probs, axis=-1, keepdims=True))
    ).astype(BF16)
    router_part = contract_rows(ffn_in, d_logits)
    d_ffn = d_ffn + times_transpose(d_logits, w_router)
    ffn_gain_part = jnp.sum(d_ffn * mixed_norm, axis=0)
    d_norm_two = d_ffn * ffn_gain.astype(F32)
    d_mixed = d_result + scale_two * (
        d_norm_two - mixed_norm * jnp.mean(d_norm_two * mixed_norm, axis=-1, keepdims=True)
    )
    d_attn = d_mixed.astype(BF16)
    d_attn_all = lax.all_gather(d_attn, "tensor", axis=0, tiled=True)
    grad_w_out = contract_rows(o_low, d_attn_all)
    d_attended = (
        times_transpose(d_attn_all, w_out)
        .astype(BF16)
        .reshape(block_count, block_rows, local_heads, head_width)
    )

    def attend_back(carry, inputs):
        dk_total, dv_total = carry
        q_block, do_block, lse_block, row_start = inputs
        scores = (
            jnp.einsum("qhd,khd->hqk", q_block, k_rot, preferred_element_type=F32)
            * score_scale
        )
        allowed = allowed_mask(row_start)
        scores = jnp.where(allowed, scores, -1e30)
        soft = jnp.where(allowed, jnp.exp(scores - lse_block[..., None]), 0.0)
        d_weights = jnp.einsum("qhd,khd->hqk", do_block, v_low, preferred_element_type=F32)
        d_scores = (soft * (d_weights - jnp.sum(soft * d_weights, axis=-1, keepdims=True))).astype(
            BF16
        )
        dq_block = (
            jnp.einsum("hqk,khd->qhd", d_scores, k_rot, preferred_element_type=F32)
            * score_scale
        )
        dk_total = (
            dk_total
            + jnp.einsum("hqk,qhd->khd", d_scores, q_block, preferred_element_type=F32)
            * score_scale
        )
        dv_total = dv_total + jnp.einsum(
            "hqk,qhd->khd", soft.astype(BF16), do_block, preferred_element_type=F32
        )
        return ((dk_total, dv_total), dq_block)

    zero_field = jnp.zeros((seq_len, local_heads, head_width), F32)
    (dk_rot, dv_full), dq_blocks = lax.scan(
        attend_back, (zero_field, zero_field), (q_blocks, d_attended, lse_blocks, starts)
    )
    dq_gain = unrotate(
        dq_blocks.reshape(seq_len, local_heads, head_width), cosine, sine_table
    ).reshape(seq_len, local_width)
    dk_gain = unrotate(dk_rot, cosine, sine_table).reshape(seq_len, local_width)
    query_gain_part = jnp.sum(dq_gain * query_hat, axis=0)
    key_gain_part = jnp.sum(dk_gain * key_hat, axis=0)
    dq_hat = dq_gain * q_gain
    dk_hat = dk_gain * k_gain
    q_inner, k_inner = lax.psum(
        (jnp.sum(dq_hat * query_hat, axis=1), jnp.sum(dk_hat * key_hat, axis=1)), "tensor"
    )
    dq_raw = (q_rscale * (dq_hat - query_hat * (q_inner / model_width)[:, None])).astype(
        BF16
    )
    dk_raw = (k_rscale * (dk_hat - key_hat * (k_inner / model_width)[:, None])).astype(BF16)
    dv_raw = dv_full.reshape(seq_len, local_width).astype(BF16)
    grad_query = contract_rows(gathered, dq_raw)
    grad_key = contract_rows(gathered, dk_raw)
    grad_value = contract_rows(gathered, dv_raw)
    total_term = times_transpose(dq_raw, w_query)
    total_term = total_term + times_transpose(dk_raw, w_key)
    d_attn_in = lax.psum_scatter(
        (total_term + times_transpose(dv_raw, w_value)).astype(BF16),
        "tensor",
        scatter_dimension=0,
        tiled=True,
    ).astype(F32)
    attn_gain_part = jnp.sum(d_attn_in * normed, axis=0)
    d_norm_one = d_attn_in * attn_gain.astype(F32)
    d_input = d_mixed + scale_one * (
        d_norm_one - normed * jnp.mean(d_norm_one * normed, axis=-1, keepdims=True)
    )
    dp_sums = (
        lax.psum(grad_query.astype(BF16), "dp").astype(F32),
        lax.psum(grad_key.astype(BF16), "dp").astype(F32),
        lax.psum(grad_value.astype(BF16), "dp").astype(F32),
        lax.psum(query_gain_part.astype(BF16), "dp").astype(F32),
        lax.psum(key_gain_part.astype(BF16), "dp").astype(F32),
        lax.psum(grad_w_out.astype(BF16), "dp").astype(F32),
    )
    shared = lax.psum((attn_gain_part, ffn_gain_part, router_part), ("dp", "tensor"))
    return (
        result.astype(BF16),
        d_input.astype(BF16),
        dp_sums[0],
        dp_sums[1],
        dp_sums[2],
        dp_sums[3],
        dp_sums[4],
        dp_sums[5],
        shared[0],
        shared[1],
        shared[2],
        grad_w_gate,
        grad_w_up,
        grad_w_down,
    )


def solution(mesh):
    rows, columns = P(BOTH, None), P(None, "tensor")
    gathered_plan = (mesh.shape["dp"], mesh.shape["tensor"]) == (2 * RING, 4)
    return jax.shard_map(
        local_gathered if gathered_plan else local_sent,
        mesh=mesh,
        in_specs=(
            rows,
            rows,
            P("dp"),
            rows,
            P(),
            columns,
            columns,
            columns,
            P("tensor"),
            P("tensor"),
            P("tensor", None),
            P(),
            P(),
            P("dp", None, "tensor"),
            P("dp", None, "tensor"),
            P("dp", "tensor", None),
        ),
        out_specs=(
            rows,
            rows,
            columns,
            columns,
            columns,
            P("tensor"),
            P("tensor"),
            P("tensor", None),
            P(),
            P(),
            P(),
            P("dp", None, "tensor"),
            P("dp", None, "tensor"),
            P("dp", "tensor", None),
        ),
        check_vma=False,
    )
```

```python
import functools
import math

import jax
import jax.numpy as jnp
from jax import lax
from jax.experimental import pallas as pl
from jax.experimental.pallas import tpu as pltpu
from jax.sharding import PartitionSpec as P

HDIM = 128
EPS = 1e-05
ROPE_BASE = 10000.0
BOTH = ("dp", "tensor")
F32 = jnp.float32
BF16 = jnp.bfloat16
VMEM_GRANT = 60 << 20
fence = lax.optimization_barrier


def rms_scale(values):
    return lax.rsqrt(jnp.mean(values * values, axis=-1, keepdims=True) + EPS)


def rope_tables(count, head_width):
    half_width = head_width // 2
    frequency = jnp.exp(
        -(jnp.arange(half_width, dtype=F32) * 2.0 / head_width) * math.log(ROPE_BASE)
    )
    angles = jnp.arange(count, dtype=F32)[:, None] * frequency[None, :]
    return (jnp.cos(angles), jnp.sin(angles))


def rotate(values_in, cosine, sine_table):
    half_width = values_in.shape[-1] // 2
    front_half = values_in[..., :half_width]
    back_half = values_in[..., half_width:]
    return jnp.concatenate(
        [
            front_half * cosine - back_half * sine_table,
            back_half * cosine + front_half * sine_table,
        ],
        axis=-1,
    )


def unrotate(grads_in, cosine, sine_table):
    return rotate(grads_in, cosine, -sine_table)


def contract_rows(left, right):
    return lax.dot_general(left, right, (((0,), (0,)), ((), ())), preferred_element_type=F32)


def times_transpose(left, right):
    return lax.dot_general(left, right, (((1,), (1,)), ((), ())), preferred_element_type=F32)


def add_low(*terms):
    total = terms[0].astype(F32)
    for term in terms[1:]:
        total = total + term.astype(F32)
    return total.astype(BF16)


def add_wide(*terms):
    total = terms[0].astype(F32)
    for term in terms[1:]:
        total = total + term.astype(F32)
    return total


RING = 4
COLUMNS = (
    ((0, 0, 0), (1, 0, 0), (0, 1, 0), (0, 0, 1)),
    ((2, 0, 0), (1, 1, 0), (1, 0, 1), (2, 1, 0)),
    ((3, 0, 0), (3, 1, 0), (2, 0, 1), (3, 0, 1)),
    ((1, 1, 1), (2, 1, 1)),
    ((0, 1, 1), (3, 1, 1)),
)
CHUNKS = tuple(tuple(chip + (dc,) for dc in (0, 1) for chip in chips) for chips in COLUMNS)
STARTS = tuple(sum(len(chunk) for chunk in CHUNKS[:i]) for i in range(len(CHUNKS)))
PLACES = tuple(place for chunk in CHUNKS for place in chunk)
MOVES = {
    "x": lambda z, x, y, c: (z, x ^ 1, y, c),
    "y": lambda z, x, y, c: (z, x, y ^ 1, c),
    "c": lambda z, x, y, c: (z, x, y, c ^ 1),
    "z": lambda z, x, y, c: ((z - 1) % RING, x, y, c),
    "u1": lambda z, x, y, c: ((z + 1) % RING, x, y, c),
    "u2": lambda z, x, y, c: ((z + 2) % RING, x, y, c),
    "u3": lambda z, x, y, c: ((z + 3) % RING, x, y, c),
    "z1": lambda z, x, y, c: (z ^ 1, x, y, c),
    "z2": lambda z, x, y, c: (z ^ 2, x, y, c),
}


def device_pairs(move):
    pairs = []
    for z in range(RING):
        for x in range(2):
            for y in range(2):
                for c in range(2):
                    tz, tx, ty, tc = move(z, x, y, c)
                    pairs.append(((z * 2 + x) * 4 + y * 2 + c, (tz * 2 + tx) * 4 + ty * 2 + tc))
    return pairs


def send(value, axis):
    return lax.ppermute(value, BOTH, device_pairs(MOVES[axis]))


def small_sum(value, axes):
    for axis in axes:
        value = value + send(value, axis)
    return value


def hop(axis, k, dx, dy):
    return {"z": ((k + 1) % RING, dx, dy), "x": (k, dx ^ 1, dy), "y": (k, dx, dy ^ 1)}[axis]


class Stages:
    def __init__(self, token):
        self.token = token

    def run(self, sends, works=()):
        values, args, _ = fence(([s[0] for s in sends], [w[1] for w in works], self.token))
        got, crossed = [], []
        for value, (_, axis) in zip(values, sends):
            if axis == "c" and len(crossed) >= 2:
                value, _ = fence((value, crossed[-2]))
            got.append(send(value, axis))
            if axis == "c":
                crossed.append(got[-1])
        made = [work(*arg) for (work, _), arg in zip(works, args)]
        got, made = fence((got, made))
        self.token = jax.tree.leaves((got, made))[0]
        return got, made


class Gather:
    def __init__(self, block):
        self.held = {(0, 0, 0, 0): block}

    def sends(self, hops):
        return [(self.held[chip + (0,)], axis) for axis, chip in hops]

    def take(self, hops, got):
        for (axis, chip), value in zip(hops, got):
            self.held[chip + (1,) if axis == "c" else hop(axis, *chip) + (0,)] = value

    def chunk(self, i):
        chunk = CHUNKS[i]
        late = [place for place in chunk if place not in self.held]
        values = [self.held[place] for place in chunk if place in self.held]
        return values, [self.held[place[:3] + (0,)] for place in late], late

    @staticmethod
    def complete(i, values, crossing, late):
        blocks = dict(zip([place for place in CHUNKS[i] if place not in late], values))
        done = []
        for place, value in zip(late, crossing):
            if len(done) >= 2:
                value, _ = fence((value, done[-2]))
            done.append(send(value, "c"))
            blocks[place] = done[-1]
        return [blocks[place] for place in CHUNKS[i]]


class Scatter:
    def __init__(self):
        self.held = {}

    def put(self, i, sums):
        for chip, value in zip(COLUMNS[i], sums):
            self.held.setdefault(chip, []).append(value)

    def sends(self, hops):
        groups = [self.held[chip] for _, chip in hops]
        added = [group for group in groups if len(group) > 1]
        sums = iter(block_sums(added) if added else ())
        return [(next(sums) if len(group) > 1 else group[0], axis) for group, (axis, _) in zip(groups, hops)]

    def take(self, hops, got):
        for (axis, chip), value in zip(hops, got):
            self.held.setdefault(hop(axis, *chip), []).append(value)

    def total(self):
        return add_wide(*self.held[0, 0, 0])


class DpSum:
    def __init__(self, value):
        group = lax.axis_index("dp")
        self.z, self.x = group // 2, group % 2
        self.value = value
        self.half, self.piece = value.shape[0] // 2, value.shape[0] // (2 * RING)

    def split_x(self):
        return [(lax.dynamic_slice_in_dim(self.value, (1 - self.x) * self.half, self.half), "x")]

    def add_x(self, got):
        self.sum = add_low(lax.dynamic_slice_in_dim(self.value, self.x * self.half, self.half), got[0])

    def split_z(self):
        return [
            (lax.dynamic_slice_in_dim(self.sum, ((self.z + d) % RING) * self.piece, self.piece), f"u{d}")
            for d in (1, 2, 3)
        ]

    def add_z(self, got):
        self.part = add_low(lax.dynamic_slice_in_dim(self.sum, self.z * self.piece, self.piece), *got)

    def join_z(self):
        return [(self.part, f"u{d}") for d in (1, 2, 3)]

    def took_z(self, got):
        stack = jnp.stack([self.part] + list(got))
        order = (self.z - jnp.arange(RING)) % RING
        self.whole_half = stack[order].reshape(self.half, -1)

    def join_x(self):
        return [(self.whole_half, "x")]

    def took_x(self, got):
        mine, other = self.whole_half, got[0]
        first = jnp.where(self.x == 0, mine, other)
        second = jnp.where(self.x == 0, other, mine)
        self.result = jnp.concatenate([first, second], axis=0).astype(F32)


def core_sum(near, far):
    return pair_sum(near, send(far, "c"))


def place_indices():
    group, member = lax.axis_index("dp"), lax.axis_index("tensor")
    z, x, y, c = group // 2, group % 2, member // 2, member % 2
    absolute = jnp.stack(
        [(((z + k) % RING) * 2 + (x ^ dx)) * 4 + (y ^ dy) * 2 + (c ^ dc) for k, dx, dy, dc in PLACES]
    )
    table = [0] * len(PLACES)
    for position, (k, dx, dy, dc) in enumerate(PLACES):
        table[((k * 2 + dx) * 2 + dy) * 2 + dc] = position
    numbers = jnp.arange(len(PLACES))
    other_z, other_x = numbers // 8, (numbers // 4) % 2
    other_y, other_c = (numbers // 2) % 2, numbers % 2
    offset = ((((other_z - z) % RING) * 2 + (other_x ^ x)) * 2 + (other_y ^ y)) * 2 + (other_c ^ c)
    return absolute, jnp.asarray(table, jnp.int32)[offset]


def nn(left, right):
    return lax.dot_general(left, right, (((1,), (0,)), ((), ())), preferred_element_type=F32)


def nt(left, right):
    return lax.dot_general(left, right, (((1,), (1,)), ((), ())), preferred_element_type=F32)


def pick_rows(picks_ref, blocks, rows_ref, slot_count, width):
    experts = rows_ref.shape[0]
    for b, block in enumerate(blocks):
        for low in range(0, block.shape[1], width):
            columns = pl.ds(low, width)
            picked = nn(picks_ref[b], block[:, columns]).astype(BF16)
            for e in range(experts):
                rows_ref[e, pl.ds(b * slot_count, slot_count), columns] = picked[
                    e * slot_count : (e + 1) * slot_count
                ]


def give_rows(picks_ref, rows_ref, blocks, slot_count, width, first=0):
    experts = rows_ref.shape[0]
    for b, block in enumerate(blocks):
        for low in range(0, block.shape[1], width):
            columns = pl.ds(low, width)
            slots = jnp.concatenate(
                [rows_ref[e, pl.ds(first + b * slot_count, slot_count), columns] for e in range(experts)],
                axis=0,
            )
            block[:, columns] = contract_rows(picks_ref[b], slots).astype(BF16)


def cot_kernel(count, slot_count, picks_ref, down_ref, *refs):
    blocks, (rows_out, acts_out, rows_ref) = refs[:count], refs[count:]
    e = pl.program_id(0)

    @pl.when(e == 0)
    def _():
        pick_rows(picks_ref, blocks, rows_ref, slot_count, 512)

    rows = rows_ref[e]
    rows_out[0] = rows
    acts_out[0] = nt(rows, down_ref[0])


def main_kernel(count, slot_count, picks_ref, gates_ref, acts_ref, gate_ref, up_ref, *refs):
    blocks = refs[:count]
    rows_out, scaled_out, d_gate_out, d_up_out, d_probs_out = refs[count : count + 5]
    near_out, far_out, rows_ref = refs[count + 5 :]
    results = [out.at[b] for out in (near_out, far_out) for b in range(count // 2)]
    e = pl.program_id(0)

    @pl.when(e == 0)
    def _():
        pick_rows(picks_ref, blocks, rows_ref, slot_count, 512)

    rows = rows_ref[e]
    rows_out[0] = rows
    pre, up = nn(rows, gate_ref[0]), nn(rows, up_ref[0])
    cot_acts = acts_ref[0]
    own_slots = pl.ds(pl.multiple_of(e * slot_count, slot_count), slot_count)
    own_picks = [picks_ref[b, own_slots, :].astype(F32) for b in range(count)]
    gate = jnp.concatenate(
        [
            jnp.sum(pick * gates_ref[b, pl.ds(e, 1), :], axis=1, keepdims=True)
            for b, pick in enumerate(own_picks)
        ],
        axis=0,
    )
    sig = jax.nn.sigmoid(pre)
    silu = pre * sig
    acts = silu * up
    scaled_out[0] = (gate * acts).astype(BF16)
    inner = jnp.sum(acts.astype(BF16).astype(F32) * cot_acts, axis=1, keepdims=True)
    for b, pick in enumerate(own_picks):
        here = inner[b * slot_count : (b + 1) * slot_count]
        d_probs_out[b, pl.ds(e, 1), :] = jnp.sum(pick * here, axis=0, keepdims=True)
    d_acts = gate * cot_acts
    d_pre = (d_acts * up * sig * (1.0 + pre * (1.0 - sig))).astype(BF16)
    d_up = (d_acts * silu).astype(BF16)
    d_gate_out[0] = d_pre
    d_up_out[0] = d_up
    rows_ref[e] = (nt(d_pre, gate_ref[0]) + nt(d_up, up_ref[0])).astype(BF16)

    @pl.when(e == pl.num_programs(0) - 1)
    def _():
        give_rows(picks_ref, rows_ref, results, slot_count, 512)


def out_kernel(parts, slot_count, *refs):
    picks, scaled, down_ref = refs[:parts], refs[parts : 2 * parts], refs[2 * parts]
    near_out, far_out, rows_ref = refs[2 * parts + 1 :]
    e = pl.program_id(0)
    rows = scaled[0][0] if parts == 1 else jnp.concatenate([part[0] for part in scaled], axis=0)
    rows_ref[e] = nn(rows, down_ref[0]).astype(BF16)

    @pl.when(e == pl.num_programs(0) - 1)
    def _():
        low, done = 0, 0
        for part in picks:
            count = part.shape[0]
            half = count // 2
            results = [out.at[done + b] for out in (near_out, far_out) for b in range(half)]
            give_rows(part, rows_ref, results, slot_count, 512, low)
            low, done = low + count * slot_count, done + half


def per_expert(*shape):
    return pl.BlockSpec((1,) + shape, lambda e: (e,) + (0,) * len(shape))


def resident(*shape):
    return pl.BlockSpec(shape, lambda e: (0,) * len(shape), pipeline_mode=pl.Buffered(1))


def cot_chunk(picks, w_down, blocks, slot_count):
    experts, hidden, width = w_down.shape
    count, tokens = len(blocks), blocks[0].shape[0]
    rows = count * slot_count
    return pl.pallas_call(
        functools.partial(cot_kernel, count, slot_count),
        grid=(experts,),
        in_specs=[resident(*picks.shape), per_expert(hidden, width)] + [resident(tokens, width)] * count,
        out_specs=[per_expert(rows, width), per_expert(rows, hidden)],
        out_shape=[
            jax.ShapeDtypeStruct((experts, rows, width), BF16),
            jax.ShapeDtypeStruct((experts, rows, hidden), F32),
        ],
        scratch_shapes=[pltpu.VMEM((experts, rows, width), BF16)],
        compiler_params=pltpu.CompilerParams(vmem_limit_bytes=VMEM_GRANT),
        cost_estimate=pl.CostEstimate(
            flops=2 * experts * rows * width * (hidden + tokens),
            bytes_accessed=2 * (count * tokens * width + experts * (rows + hidden) * width),
            transcendentals=0,
        ),
    )(picks, w_down, *blocks)


def main_chunk(picks, gates, cot_acts, acts_at, w_gate, w_up, blocks, slot_count):
    experts, width, hidden = w_gate.shape
    count, tokens = len(blocks), blocks[0].shape[0]
    rows = count * slot_count
    outs = pl.pallas_call(
        functools.partial(main_kernel, count, slot_count),
        grid=(experts,),
        in_specs=[
            resident(*picks.shape),
            resident(*gates.shape),
            pl.BlockSpec((1, rows, hidden), lambda e: (e, acts_at, 0)),
            per_expert(width, hidden),
            per_expert(width, hidden),
        ]
        + [resident(tokens, width)] * count,
        out_specs=[
            per_expert(rows, width),
            per_expert(rows, hidden),
            per_expert(rows, hidden),
            per_expert(rows, hidden),
            resident(*gates.shape),
        ]
        + [resident(count // 2, tokens, width)] * 2,
        out_shape=[
            jax.ShapeDtypeStruct((experts, rows, width), BF16),
            jax.ShapeDtypeStruct((experts, rows, hidden), BF16),
            jax.ShapeDtypeStruct((experts, rows, hidden), BF16),
            jax.ShapeDtypeStruct((experts, rows, hidden), BF16),
            jax.ShapeDtypeStruct(gates.shape, F32),
        ]
        + [jax.ShapeDtypeStruct((count // 2, tokens, width), BF16)] * 2,
        scratch_shapes=[pltpu.VMEM((experts, rows, width), BF16)],
        compiler_params=pltpu.CompilerParams(vmem_limit_bytes=VMEM_GRANT),
        cost_estimate=pl.CostEstimate(
            flops=2 * experts * rows * width * (4 * hidden + 2 * tokens),
            bytes_accessed=2 * (2 * count * tokens * width + experts * (rows + 2 * hidden) * width),
            transcendentals=experts * rows * hidden,
        ),
    )(picks, gates, cot_acts, w_gate, w_up, *blocks)
    return outs[:5], outs[5:]


def out_chunk(picks, scaled, w_down, slot_count):
    experts, hidden, width = w_down.shape
    tokens = picks[0].shape[2]
    count = sum(part.shape[0] for part in picks)
    rows = count * slot_count
    return pl.pallas_call(
        functools.partial(out_kernel, len(picks), slot_count),
        grid=(experts,),
        in_specs=[resident(*part.shape) for part in picks]
        + [per_expert(*part.shape[1:]) for part in scaled]
        + [per_expert(hidden, width)],
        out_specs=[resident(count // 2, tokens, width)] * 2,
        out_shape=[jax.ShapeDtypeStruct((count // 2, tokens, width), BF16)] * 2,
        scratch_shapes=[pltpu.VMEM((experts, rows, width), BF16)],
        compiler_params=pltpu.CompilerParams(vmem_limit_bytes=VMEM_GRANT),
        cost_estimate=pl.CostEstimate(
            flops=2 * experts * rows * width * (hidden + tokens),
            bytes_accessed=2 * (count * tokens * width + experts * (rows + hidden) * width),
            transcendentals=0,
        ),
    )(*picks, *scaled, w_down)


def grad_kernel(count, *refs):
    rows, cots, scaled, d_gate, d_up = (refs[i * count : (i + 1) * count] for i in range(5))
    gate_out, up_out, down_out = refs[-3:]

    def total(lefts, rights):
        value = None
        for left, right in zip(lefts, rights):
            term = contract_rows(left[0], right[0])
            value = term if value is None else value + term
        return value

    gate_out[0] = total(rows, d_gate)
    up_out[0] = total(rows, d_up)
    down_out[0] = total(scaled, cots)


def expert_grads(rows, cots, scaled, d_gate, d_up, cots_at, first, last, earlier=None, tile=512):
    count, experts, width = len(rows), rows[0].shape[0], rows[0].shape[2]
    hidden = scaled[0].shape[2]
    slots = sum(part.shape[1] for part in rows)
    wide = [pl.BlockSpec((1, part.shape[1], tile), lambda e, n: (first + e, 0, n)) for part in rows]
    wide_cots = [
        pl.BlockSpec((1, part.shape[1], tile), lambda e, n, at=at: (first + e, at, n))
        for part, at in zip(rows, cots_at)
    ]
    narrow = [pl.BlockSpec((1, part.shape[1], hidden), lambda e, n: (first + e, 0, 0)) for part in rows]
    tall = pl.BlockSpec((1, tile, hidden), lambda e, n: (first + e, n, 0))
    given = [] if earlier is None else list(earlier)
    return pl.pallas_call(
        functools.partial(grad_kernel, count),
        grid=(last - first, width // tile),
        in_specs=wide + wide_cots + narrow * 3 + [pl.BlockSpec(memory_space=pl.ANY)] * len(given),
        out_specs=[tall, tall, pl.BlockSpec((1, hidden, tile), lambda e, n: (first + e, 0, n))],
        out_shape=[
            jax.ShapeDtypeStruct((experts, width, hidden), F32),
            jax.ShapeDtypeStruct((experts, width, hidden), F32),
            jax.ShapeDtypeStruct((experts, hidden, width), F32),
        ],
        input_output_aliases={5 * count + i: i for i in range(len(given))},
        compiler_params=pltpu.CompilerParams(vmem_limit_bytes=VMEM_GRANT),
        cost_estimate=pl.CostEstimate(
            flops=6 * (last - first) * slots * width * hidden,
            bytes_accessed=(last - first) * (4 * slots * width + 12 * width * hidden),
            transcendentals=0,
        ),
    )(*rows, *cots, *scaled, *d_gate, *d_up, *given)


def sums_kernel(counts, *refs):
    terms, outs = refs[: sum(counts)], refs[sum(counts) :]
    for count, out in zip(counts, outs):
        value = terms[0][...].astype(F32)
        for term in terms[1:count]:
            value = value + term[...].astype(F32)
        out[...] = value.astype(BF16)
        terms = terms[count:]


def block_sums(groups, tile=64):
    rows, width = groups[0][0].shape
    counts = [len(group) for group in groups]
    block = pl.BlockSpec((tile, width), lambda i: (i, 0))
    return pl.pallas_call(
        functools.partial(sums_kernel, counts),
        grid=(rows // tile,),
        in_specs=[block] * sum(counts),
        out_specs=[block] * len(groups),
        out_shape=[jax.ShapeDtypeStruct((rows, width), BF16)] * len(groups),
        compiler_params=pltpu.CompilerParams(vmem_limit_bytes=VMEM_GRANT),
        cost_estimate=pl.CostEstimate(
            flops=sum(counts) * rows * width,
            bytes_accessed=2 * (sum(counts) + len(groups)) * rows * width,
            transcendentals=0,
        ),
    )(*[term for group in groups for term in group])


def qkv_kernel(*refs):
    blocks, (q_w, k_w, v_w, q_out, k_out, v_out, q_sq, k_sq) = refs[:-8], refs[-8:]
    lanes = q_sq.shape[1]
    rows = blocks[0].shape[0]
    for b, block in enumerate(blocks):
        here = pl.ds(b * rows, rows)
        for weight, out, squares in ((q_w, q_out, q_sq), (k_w, k_out, k_sq)):
            value = nn(block[...], weight[...])
            out[here, :] = value
            value = value * value
            total = value[:, :lanes]
            for low in range(lanes, value.shape[1], lanes):
                total = total + value[:, low : low + lanes]

            @pl.when(pl.program_id(0) == 0)
            def _(squares=squares, total=total):
                squares[here, :] = total

            @pl.when(pl.program_id(0) > 0)
            def _(squares=squares, total=total):
                squares[here, :] += total

        v_out[here, :] = nn(block[...], v_w[...]).astype(BF16)


def qkv(blocks, w_query, w_key, w_value, tile=256):
    rows, depth = blocks[0].shape
    width = w_query.shape[1]
    count = len(blocks) * rows
    weight = pl.BlockSpec((depth, tile), lambda n: (0, n))
    out = pl.BlockSpec((count, tile), lambda n: (0, n))
    return pl.pallas_call(
        qkv_kernel,
        grid=(width // tile,),
        in_specs=[resident(rows, depth)] * len(blocks) + [weight] * 3,
        out_specs=[out] * 3 + [resident(count, HDIM)] * 2,
        out_shape=[
            jax.ShapeDtypeStruct((count, width), F32),
            jax.ShapeDtypeStruct((count, width), F32),
            jax.ShapeDtypeStruct((count, width), BF16),
            jax.ShapeDtypeStruct((count, HDIM), F32),
            jax.ShapeDtypeStruct((count, HDIM), F32),
        ],
        compiler_params=pltpu.CompilerParams(vmem_limit_bytes=VMEM_GRANT),
        cost_estimate=pl.CostEstimate(
            flops=6 * count * depth * width,
            bytes_accessed=2 * count * depth + 6 * depth * width + 10 * count * width,
            transcendentals=0,
        ),
    )(*blocks, w_query, w_key, w_value)


def pair_kernel(near_ref, far_ref, *outs):
    for b, out in enumerate(outs):
        out[...] = (near_ref[b].astype(F32) + far_ref[b].astype(F32)).astype(BF16)


def pair_sum(near, far, tile=64):
    count, rows, width = near.shape
    stack = pl.BlockSpec((count, tile, width), lambda i: (0, i, 0))
    return pl.pallas_call(
        pair_kernel,
        grid=(rows // tile,),
        in_specs=[stack, stack],
        out_specs=[pl.BlockSpec((tile, width), lambda i: (i, 0))] * count,
        out_shape=[jax.ShapeDtypeStruct((rows, width), BF16)] * count,
        compiler_params=pltpu.CompilerParams(vmem_limit_bytes=VMEM_GRANT),
        cost_estimate=pl.CostEstimate(
            flops=count * rows * width, bytes_accessed=6 * count * rows * width, transcendentals=0
        ),
    )(near, far)


def turn(values, cosine, sine):
    return values * cosine + pltpu.roll(values, values.shape[1] // 2, 1) * sine


def attend_kernel(
    row_block, scale, q_ref, k_ref, v_ref, cols_ref, qg_ref, kg_ref, cos_ref, sin_ref, kpos_ref,
    out_ref, lse_ref, qrot_ref, krot_ref,
):
    cosine, sine = cos_ref[...], sin_ref[...]
    qrot_ref[...] = turn(q_ref[...] * cols_ref[:, 0:1] * qg_ref[...], cosine, sine).astype(BF16)
    krot_ref[...] = turn(k_ref[...] * cols_ref[:, 1:2] * kg_ref[...], cosine, sine).astype(BF16)
    for low in range(0, q_ref.shape[0], row_block):
        rows = pl.ds(low, row_block)
        scores = nt(qrot_ref[rows, :], krot_ref[...]) * scale
        scores = jnp.where(kpos_ref[...] <= cols_ref[rows, 2:3], scores, -1e30)
        top = jnp.max(scores, axis=1, keepdims=True)
        powers = jnp.exp(scores - top)
        total = jnp.sum(powers, axis=1, keepdims=True)
        soft = (powers * (1.0 / total)).astype(BF16)
        out_ref[rows, :] = nn(soft, v_ref[...]).astype(BF16)
        lse_ref[rows, :] = jnp.broadcast_to(top + jnp.log(total), (row_block, HDIM))


def attend_back_kernel(
    row_block, scale, q_ref, k_ref, v_ref, qrot_ref, krot_ref, do_ref, lse_ref, cols_ref, qg_ref, kg_ref,
    cos_ref, sin_ref, kpos_ref,
    dq_ref, dk_ref, dv_ref, qgain_ref, kgain_ref, qin_ref, kin_ref, dq_acc, dk_acc, dv_acc,
):
    for low in range(0, q_ref.shape[0], row_block):
        rows = pl.ds(low, row_block)
        query, d_out = qrot_ref[rows, :], do_ref[rows, :]
        scores = nt(query, krot_ref[...]) * scale
        soft = jnp.where(kpos_ref[...] <= cols_ref[rows, 2:3], jnp.exp(scores - lse_ref[rows, 0:1]), 0.0)
        d_weights = nt(d_out, v_ref[...])
        spread = soft * d_weights
        mean = jnp.sum(spread, axis=1, keepdims=True)
        d_scores = (spread - soft * mean).astype(BF16)
        dq_acc[rows, :] = nn(d_scores, krot_ref[...]) * scale
        d_keys = contract_rows(d_scores, query)
        d_values = contract_rows(soft.astype(BF16), d_out)
        if low:
            dk_acc[...] += d_keys
            dv_acc[...] += d_values
        else:
            dk_acc[...] = d_keys
            dv_acc[...] = d_values
    dv_ref[...] = dv_acc[...].astype(BF16)
    cosine, sine = cos_ref[...], -sin_ref[...]
    for lane, raw_ref, gain_ref, grad, hat_ref, gain_out, inner_out in (
        (0, q_ref, qg_ref, dq_acc[...], dq_ref, qgain_ref, qin_ref),
        (1, k_ref, kg_ref, dk_acc[...] * scale, dk_ref, kgain_ref, kin_ref),
    ):
        hat = raw_ref[...] * cols_ref[:, lane : lane + 1]
        turned = turn(grad, cosine, sine)
        gain_out[...] = jnp.sum(turned * hat, axis=0, keepdims=True)
        d_hat = turned * gain_ref[...]
        hat_ref[...] = d_hat
        inner = d_hat * hat

        @pl.when(pl.program_id(0) == 0)
        def _(inner=inner, inner_out=inner_out):
            inner_out[...] = inner

        @pl.when(pl.program_id(0) > 0)
        def _(inner=inner, inner_out=inner_out):
            inner_out[...] += inner


def head_columns(rows):
    return pl.BlockSpec((rows, HDIM), lambda h: (0, h))


def whole(*shape):
    return pl.BlockSpec(shape, lambda h: (0,) * len(shape))


def attend_forward(q_raw, k_raw, v_low, cols, q_gain, k_gain, cosine, sine, kpos):
    seq_len, width = q_raw.shape
    heads = width // HDIM
    part, one = head_columns(seq_len), head_columns(1)
    return pl.pallas_call(
        functools.partial(attend_kernel, min(256, seq_len), HDIM ** (-0.5)),
        grid=(heads,),
        in_specs=[part, part, part, whole(seq_len, HDIM), one, one]
        + [whole(seq_len, HDIM), whole(seq_len, HDIM), whole(1, seq_len)],
        out_specs=[part, part, part, part],
        out_shape=[
            jax.ShapeDtypeStruct((seq_len, width), BF16),
            jax.ShapeDtypeStruct((seq_len, width), F32),
            jax.ShapeDtypeStruct((seq_len, width), BF16),
            jax.ShapeDtypeStruct((seq_len, width), BF16),
        ],
        compiler_params=pltpu.CompilerParams(vmem_limit_bytes=VMEM_GRANT),
        cost_estimate=pl.CostEstimate(
            flops=4 * seq_len * seq_len * width,
            bytes_accessed=20 * seq_len * width,
            transcendentals=heads * seq_len * seq_len,
        ),
    )(q_raw, k_raw, v_low, cols, q_gain, k_gain, cosine, sine, kpos)


def attend_backward(
    q_raw, k_raw, v_low, q_rot, k_rot, d_out, lse, cols, q_gain, k_gain, cosine, sine, kpos
):
    seq_len, width = q_raw.shape
    heads = width // HDIM
    part, one = head_columns(seq_len), head_columns(1)
    return pl.pallas_call(
        functools.partial(attend_back_kernel, min(256, seq_len), HDIM ** (-0.5)),
        grid=(heads,),
        in_specs=[part, part, part, part, part, part, part, whole(seq_len, HDIM), one, one]
        + [whole(seq_len, HDIM), whole(seq_len, HDIM), whole(1, seq_len)],
        out_specs=[part, part, part, one, one, whole(seq_len, HDIM), whole(seq_len, HDIM)],
        out_shape=[
            jax.ShapeDtypeStruct((seq_len, width), F32),
            jax.ShapeDtypeStruct((seq_len, width), F32),
            jax.ShapeDtypeStruct((seq_len, width), BF16),
            jax.ShapeDtypeStruct((1, width), F32),
            jax.ShapeDtypeStruct((1, width), F32),
            jax.ShapeDtypeStruct((seq_len, HDIM), F32),
            jax.ShapeDtypeStruct((seq_len, HDIM), F32),
        ],
        scratch_shapes=[pltpu.VMEM((seq_len, HDIM), F32)] * 3,
        compiler_params=pltpu.CompilerParams(vmem_limit_bytes=VMEM_GRANT),
        cost_estimate=pl.CostEstimate(
            flops=10 * seq_len * seq_len * width,
            bytes_accessed=32 * seq_len * width,
            transcendentals=heads * seq_len * seq_len,
        ),
    )(q_raw, k_raw, v_low, q_rot, k_rot, d_out, lse, cols, q_gain, k_gain, cosine, sine, kpos)


def local_gathered(
    hidden_in,
    cotangent,
    seq_lengths,
    expert_ids,
    attn_gain,
    w_query,
    w_key,
    w_value,
    query_gain,
    key_gain,
    w_out,
    ffn_gain,
    w_router,
    w_gate,
    w_up,
    w_down,
):
    tensor_count = lax.axis_size("tensor")
    group_count = lax.axis_size("dp")
    tok_rows, model_width = hidden_in.shape
    topk = expert_ids.shape[1]
    expert_total = w_router.shape[1]
    experts = w_gate.shape[0]
    slot_count = tok_rows * topk // expert_total
    devices = len(PLACES)
    seq_len = tok_rows * tensor_count
    local_width = w_query.shape[1]
    half_width = HDIM // 2
    live_length = seq_lengths[0]
    absolute, position = place_indices()

    member = lax.axis_index("tensor")
    blocks_at = member ^ jnp.arange(tensor_count)

    def turn_tables(blocks_at):
        cosine, sine = (
            table.reshape(tensor_count, tok_rows, half_width)[blocks_at].reshape(seq_len, half_width)
            for table in rope_tables(seq_len, HDIM)
        )
        return jnp.concatenate([cosine, cosine], axis=1), jnp.concatenate([-sine, sine], axis=1)

    positions = (blocks_at[:, None] * tok_rows + jnp.arange(tok_rows)[None, :]).reshape(-1)
    never = 2 * seq_len
    key_pos = jnp.where(positions < live_length, positions, never).astype(F32)[None, :]

    def token_sums(*values):
        stacked = jnp.stack([value.reshape(tensor_count, tok_rows) for value in values])
        summed = lax.psum(stacked[:, blocks_at], "tensor")
        return summed[:, blocks_at].reshape(len(values), seq_len)

    def to_groups(by_expert):
        copies = jnp.broadcast_to(
            by_expert.reshape(group_count, 1, experts, tok_rows),
            (group_count, tensor_count, experts, tok_rows),
        ).reshape(devices, experts, tok_rows)
        return lax.all_to_all(copies, BOTH, split_axis=0, concat_axis=0, tiled=True)[absolute]

    resid = hidden_in.astype(F32)
    scale_one = rms_scale(resid)
    normed = resid * scale_one
    attn_in = (normed * attn_gain.astype(F32)).astype(BF16)
    q_gain = query_gain.astype(F32)[None, :]
    k_gain = key_gain.astype(F32)[None, :]

    hot = jnp.any(expert_ids.T[None, :, :] == jnp.arange(expert_total)[:, None, None], axis=1)
    earlier = jnp.triu(jnp.ones((tok_rows, tok_rows), F32), 1).astype(BF16)
    rank = jnp.dot(hot.astype(BF16), earlier, preferred_element_type=F32)
    slot_of = jnp.where(hot, rank, -1.0)

    def all_picks(slot_of):
        slots = jnp.arange(slot_count, dtype=F32)
        wide = (slot_of[:, :, None, :] == slots[None, None, :, None]).astype(BF16)
        return [
            wide[low : low + len(chunk)].reshape(len(chunk), experts * slot_count, tok_rows)
            for chunk, low in zip(CHUNKS, STARTS)
        ]


    stages = Stages(attn_in)
    cot, ffn = Gather(cotangent), Gather(None)
    d_sum, out_sum = Scatter(), Scatter()
    order = range(len(CHUNKS))
    cot_rows, cot_acts, kept = {}, {}, {}

    def advance(works=(), extra=(), **hops):
        tables = {"cot": cot, "ffn": ffn, "d": d_sum, "out": out_sum}
        sends = list(extra)
        spans = []
        for name, moves in hops.items():
            spans.append((tables[name], moves, len(sends)))
            sends += tables[name].sends(moves)
        got, made = stages.run(sends, works)
        for table, moves, low in spans:
            table.take(moves, got[low : low + len(moves)])
        return got[: len(extra)], made

    def cot_work(*chunks):
        made = [cot.chunk(i) for i in chunks]

        def work(picks_i, w_down_i, *args):
            blocks = []
            for i, (_, _, late), (values, crossing) in zip(chunks, made, args):
                blocks += Gather.complete(i, values, crossing, late)
            return cot_chunk(picks_i, w_down_i, blocks, slot_count)

        picks_i = picks[chunks[0]] if len(chunks) == 1 else jnp.concatenate([picks[i] for i in chunks], axis=0)
        return work, (picks_i, w_down) + tuple((values, crossing) for values, crossing, _ in made)

    def cot_done(chunks, made):
        for n, i in enumerate(chunks):
            cot_rows[i], cot_acts[i] = (made[0], n), (made[1], n)

    def main_work(i):
        values, crossing, late = ffn.chunk(i)

        def work(picks_i, gates_i, acts_i, gate_w, up_w, values, crossing):
            blocks = Gather.complete(i, values, crossing, late)
            return main_chunk(picks_i, gates_i, acts_i, cot_acts[i][1], gate_w, up_w, blocks, slot_count)

        gates_i = token_gates[STARTS[i] : STARTS[i] + len(CHUNKS[i])]
        return work, (picks[i], gates_i, cot_acts[i][0], w_gate, w_up, values, crossing)

    def out_work(*chunks):
        def work(picks_i, scaled_i, w_down_i):
            return out_chunk(picks_i, scaled_i, w_down_i, slot_count)

        return work, ([picks[i] for i in chunks], [kept[i][1] for i in chunks], w_down)

    (across, mate), ((cosine, sine), slot_of) = advance(
        [(turn_tables, (blocks_at,)), (to_groups, (slot_of,))],
        extra=[(attn_in, "y"), (attn_in, "c")],
        cot=[("z", (0, 0, 0)), ("x", (0, 0, 0))],
    )

    def project(block, mate, across, w_query, w_key, w_value):
        blocks = [block, mate, across, send(across, "c")]
        q_raw, k_raw, v_low, q_square, k_square = qkv(blocks, w_query, w_key, w_value)
        squares = token_sums(jnp.sum(q_square, axis=1), jnp.sum(k_square, axis=1))
        return blocks, q_raw, k_raw, v_low, squares

    _, (made,) = advance(
        [(project, (attn_in, mate, across, w_query, w_key, w_value))],
        cot=[("z", (1, 0, 0)), ("x", (1, 0, 0)), ("y", (0, 0, 0)), ("c", (0, 0, 0)), ("c", (1, 0, 0))],
    )
    seq_blocks, q_raw, k_raw, v_low, squares = made

    def columns_of(squares):
        scales = lax.rsqrt(squares / model_width + EPS)
        columns = jnp.stack([scales[0], scales[1], positions.astype(F32)], axis=1)
        return jnp.pad(columns, ((0, 0), (0, HDIM - columns.shape[1])))

    cols = columns_of(squares)
    _, (made,) = advance(
        [(attend_forward, (q_raw, k_raw, v_low, cols, q_gain, k_gain, cosine, sine, key_pos))],
        cot=[("z", (2, 0, 0)), ("x", (2, 0, 0)), ("y", (1, 0, 0)), ("c", (0, 1, 0)), ("c", (0, 0, 1))],
    )
    o_low, lse, q_rot, k_rot = made

    def project_back(o_low, w_out):
        parts = [
            jnp.dot(o_low[r * tok_rows : (r + 1) * tok_rows], w_out, preferred_element_type=F32).astype(BF16)
            for r in range(tensor_count)
        ]
        across = add_low(parts[2], send(parts[3], "c"))
        return add_wide(parts[0], send(parts[1], "c")) + send(across, "y").astype(F32)

    _, (attn_rows, picks) = advance(
        [(project_back, (o_low, w_out)), (all_picks, (slot_of,))],
        cot=[("x", (3, 0, 0)), ("c", (2, 0, 0)), ("c", (1, 1, 0))],
    )
    mixed = resid + attn_rows
    scale_two = rms_scale(mixed)
    mixed_norm = mixed * scale_two
    ffn_in = (mixed_norm * ffn_gain.astype(F32)).astype(BF16)
    ffn.held[0, 0, 0, 0] = ffn_in

    def route(ffn_in, w_router):
        logits = jnp.dot(ffn_in, w_router, preferred_element_type=F32)
        return jax.nn.softmax(logits, axis=-1)

    def join(*blocks):
        return jnp.concatenate(blocks, axis=0)

    _, (router_probs, made, gathered) = advance(
        [(route, (ffn_in, w_router)), cot_work(0), (join, tuple(seq_blocks))],
        ffn=[("z", (0, 0, 0)), ("x", (0, 0, 0)), ("y", (0, 0, 0))],
        cot=[("c", (1, 0, 1)), ("c", (2, 1, 0))],
    )
    cot_done((0,), made)
    _, (made, token_gates) = advance(
        [cot_work(1), (to_groups, (router_probs.T,))],
        ffn=[("z", (1, 0, 0)), ("x", (1, 0, 0)), ("y", (1, 0, 0))]
        + [("c", (0, 0, 0)), ("c", (0, 1, 0)), ("c", (1, 0, 0)), ("c", (0, 0, 1))],
    )
    cot_done((1,), made)
    _, (made,) = advance(
        [main_work(0)],
        ffn=[("z", (2, 0, 0)), ("x", (2, 0, 0)), ("c", (2, 0, 0))],
        cot=[("y", (2, 0, 0)), ("c", (3, 0, 0))],
    )
    kept[0], near, far = made[0], *made[1]
    _, (made,) = advance(
        [(core_sum, (near, far))],
        ffn=[("x", (3, 0, 0)), ("c", (1, 1, 0)), ("c", (1, 0, 1)), ("c", (2, 1, 0))],
        cot=[("y", (3, 0, 0))],
    )
    d_sum.put(0, made)
    _, (made,) = advance(
        [main_work(1)],
        ffn=[("y", (2, 0, 0))],
        cot=[("x", (0, 0, 1)), ("c", (3, 1, 0)), ("c", (2, 0, 1))],
    )
    kept[1], near, far = made[0], *made[1]
    _, (made, other) = advance(
        [(core_sum, (near, far)), cot_work(2)],
        ffn=[("y", (3, 0, 0)), ("c", (3, 0, 0)), ("c", (3, 1, 0))],
        cot=[("x", (1, 0, 1))],
    )
    d_sum.put(1, made)
    cot_done((2,), other)
    _, (made,) = advance(
        [main_work(2)],
        cot=[("x", (2, 0, 1)), ("y", (3, 1, 0)), ("c", (0, 1, 1)), ("c", (1, 1, 1))],
    )
    kept[2], near, far = made[0], *made[1]
    _, (made, other) = advance(
        [(core_sum, (near, far)), cot_work(3, 4)],
        ffn=[("x", (2, 0, 1)), ("y", (1, 1, 0))],
    )
    d_sum.put(2, made)
    cot_done((3, 4), other)
    _, (made,) = advance([main_work(3)], ffn=[("x", (3, 0, 1)), ("y", (0, 1, 0))])
    kept[3], near, far = made[0], *made[1]
    _, (made,) = advance([(core_sum, (near, far))], ffn=[("c", (0, 1, 1)), ("c", (3, 1, 1))])
    d_sum.put(3, made)

    _, (made,) = advance([main_work(4)], d=[("x", (1, 1, 1)), ("y", (2, 1, 1))])
    kept[4], near, far = made[0], *made[1]

    def return_probs(*d_probs):
        d_probs = jnp.concatenate(d_probs, axis=0)[position]
        arrived = lax.all_to_all(d_probs, BOTH, split_axis=0, concat_axis=0, tiled=True)
        arrived = arrived.reshape(group_count, tensor_count, experts, tok_rows)
        return jnp.sum(arrived, axis=1).reshape(expert_total, tok_rows).T

    outs = {}
    _, (made, outs[0], d_probs) = advance(
        [(core_sum, (near, far)), out_work(0), (return_probs, tuple(kept[i][4] for i in order))],
        d=[("x", (1, 1, 0)), ("y", (1, 0, 1))],
    )
    d_sum.put(4, made)
    _, (outs[1], made) = advance(
        [out_work(1), (core_sum, tuple(outs[0]))], d=[("x", (3, 1, 1)), ("y", (0, 1, 1))]
    )
    out_sum.put(0, made)
    _, (outs[2], made) = advance(
        [out_work(2), (core_sum, tuple(outs[1]))],
        d=[("x", (2, 1, 0)), ("y", (2, 0, 1)), ("z", (1, 0, 0))],
    )
    out_sum.put(1, made)
    _, (last_outs, made) = advance(
        [out_work(3, 4), (core_sum, tuple(outs[2]))],
        d=[("x", (3, 1, 0)), ("y", (3, 0, 1)), ("z", (2, 0, 0))],
    )
    out_sum.put(2, made)
    _, (made,) = advance(
        [(core_sum, tuple(last_outs))],
        d=[("x", (0, 1, 0)), ("y", (0, 0, 1)), ("z", (3, 0, 0))],
    )
    out_sum.put(3, made[:2])
    out_sum.put(4, made[2:])
    d_ffn = d_sum.total()

    d_result = cotangent.astype(F32)
    d_logits = (
        router_probs * (d_probs - jnp.sum(router_probs * d_probs, axis=-1, keepdims=True))
    ).astype(BF16)
    router_part = contract_rows(d_logits, ffn_in)
    d_ffn = d_ffn + times_transpose(d_logits, w_router)
    ffn_gain_part = jnp.sum(d_ffn * mixed_norm, axis=0)
    d_norm_two = d_ffn * ffn_gain.astype(F32)
    d_mixed = d_result + scale_two * (
        d_norm_two - mixed_norm * jnp.mean(d_norm_two * mixed_norm, axis=-1, keepdims=True)
    )
    d_attn = d_mixed.astype(BF16)
    router_sums = jnp.concatenate(
        [router_part, jnp.broadcast_to(ffn_gain_part[None, :], (8, model_width))], axis=0
    )

    (across, mate, other), _ = advance(
        extra=[(d_attn, "y"), (d_attn, "c"), (router_sums, "z1")], out=[("x", (1, 1, 1))]
    )
    router_sums = router_sums + other

    def attend_back(d_attn, mate, across, w_out, *rest):
        d_blocks = [d_attn, mate, across, send(across, "c")]
        d_attended = join(*[times_transpose(block, w_out).astype(BF16) for block in d_blocks])
        q_raw, k_raw, v_low, q_rot, k_rot, lse, cols = rest
        made = attend_backward(
            q_raw, k_raw, v_low, q_rot, k_rot, d_attended, lse, cols, q_gain, k_gain, cosine, sine, key_pos
        )
        return made, d_blocks

    _, (made,) = advance(
        [
            (
                attend_back,
                (d_attn, mate, across, w_out, q_raw, k_raw, v_low, q_rot, k_rot, lse, cols),
            )
        ],
        out=[("x", (3, 1, 1)), ("x", (1, 1, 0)), ("y", (2, 1, 1)), ("y", (0, 1, 1))],
    )
    (dq_hat, dk_hat, dv_raw, query_gain_part, key_gain_part, q_inner, k_inner), d_blocks = made

    def early_grads(o_low, gathered, dv_raw, *d_blocks):
        return (
            contract_rows(o_low, join(*d_blocks)).astype(BF16),
            contract_rows(gathered, dv_raw).astype(BF16),
        )


    def norm_back(q_raw, k_raw, cols, dq_hat, dk_hat, q_inner, k_inner):
        inner = token_sums(jnp.sum(q_inner, axis=1), jnp.sum(k_inner, axis=1)) / model_width
        raws = []
        for n, (raw, d_hat) in enumerate(((q_raw, dq_hat), (k_raw, dk_hat))):
            scale = cols[:, n : n + 1]
            raws.append((scale * (d_hat - raw * scale * inner[n][:, None])).astype(BF16))
        return raws

    (other,), ((dq_raw, dk_raw), made) = advance(
        [
            (norm_back, (q_raw, k_raw, cols, dq_hat, dk_hat, q_inner, k_inner)),
            (early_grads, (o_low, gathered, dv_raw) + tuple(d_blocks)),
        ],
        extra=[(router_sums, "z2")],
        out=[("x", (3, 1, 0)), ("y", (1, 0, 1))],
    )
    router_sums = router_sums + other

    grad_w_out, grad_value = lax.psum(made, "dp")

    def projections_back(gathered, dq_raw, dk_raw, dv_raw, w_query, w_key, w_value):
        grads = [contract_rows(gathered, part).astype(BF16) for part in (dk_raw, dq_raw)]
        total_term = times_transpose(dq_raw, w_query)
        total_term = total_term + times_transpose(dk_raw, w_key)
        total_term = (total_term + times_transpose(dv_raw, w_value)).astype(BF16)
        return grads, total_term

    (other,), (((grad_key, grad_query), total_term),) = advance(
        [(projections_back, (gathered, dq_raw, dk_raw, dv_raw, w_query, w_key, w_value))],
        extra=[(router_sums, "c")],
        out=[("x", (2, 1, 0)), ("y", (2, 0, 1)), ("z", (1, 0, 0))],
    )
    router_sums = router_sums + other

    key_sum, query_sum = DpSum(grad_key), DpSum(grad_query)

    def saved(n):
        return [kept[i][n] for i in order]

    def grads_of(first, last, earlier=None):
        all_cots = [cot_rows[i][0] for i in order]

        places = [cot_rows[i][1] for i in order]

        def work(*args):
            return expert_grads(*args[:5], places, first, last, args[5] if len(args) > 5 else None)

        args = (saved(0), all_cots, saved(1), saved(2), saved(3))
        return work, args if earlier is None else args + (earlier,)

    thirds = [experts * n // 3 for n in range(4)]
    parts = jnp.split(total_term, tensor_count, axis=0)
    (d_far, d_near, *got), _ = advance(
        extra=[(parts[3], "c"), (parts[1], "c")] + key_sum.split_x(),
        out=[("y", (3, 0, 1)), ("z", (2, 0, 0))],
    )
    key_sum.add_x(got)
    (d_across, *got), (made,) = advance(
        [grads_of(thirds[0], thirds[1])],
        extra=[(add_low(parts[2], d_far), "y")] + query_sum.split_x() + key_sum.split_z(),
    )
    query_sum.add_x(got[:1])
    key_sum.add_z(got[1:])
    d_attn_in = add_wide(parts[0], d_near, d_across)
    attn_gain_part = jnp.sum(d_attn_in * normed, axis=0)
    d_norm_one = d_attn_in * attn_gain.astype(F32)
    d_input = d_mixed + scale_one * (
        d_norm_one - normed * jnp.mean(d_norm_one * normed, axis=-1, keepdims=True)
    )
    got, (made,) = advance(
        [grads_of(thirds[1], thirds[2], made)], extra=key_sum.join_z(), out=[("x", (0, 1, 0)), ("y", (0, 0, 1))]
    )
    key_sum.took_z(got)
    (other, *got), ((grad_w_gate, grad_w_up, grad_w_down),) = advance(
        [grads_of(thirds[2], thirds[3], made)],
        extra=[(attn_gain_part, "c")] + key_sum.join_x() + query_sum.split_z(),
    )
    attn_gain_part = attn_gain_part + other
    key_sum.took_x(got[:1])
    query_sum.add_z(got[1:])
    (other, third, *got), _ = advance(
        extra=[(attn_gain_part, "y"), (router_sums, "x")] + query_sum.join_z(),
    )
    gain_parts = jnp.concatenate([attn_gain_part + other, query_gain_part[0], key_gain_part[0]])
    router_sums = router_sums + third
    query_sum.took_z(got)
    (other, third, *got), _ = advance(
        extra=[(gain_parts, "x"), (router_sums, "y")] + query_sum.join_x(), out=[("z", (3, 0, 0))]
    )
    query_sum.took_x(got)
    router_sums = router_sums + third
    gain_parts = gain_parts + other
    result = (mixed + out_sum.total()).astype(BF16)
    (next_z, far_z, last_z), ((result, d_input, grad_query, grad_key),) = advance(
        [
            (
                lambda *values: values,
                (result, d_input.astype(BF16), query_sum.result, key_sum.result),
            )
        ],
        extra=[(gain_parts, "u1"), (gain_parts, "u2"), (gain_parts, "u3")],
    )
    gain_sums = (gain_parts + far_z) + (next_z + last_z)
    return (
        result,
        d_input,
        grad_query,
        grad_key,
        grad_value.astype(F32),
        gain_sums[model_width : model_width + local_width],
        gain_sums[model_width + local_width :],
        grad_w_out.astype(F32),
        gain_sums[:model_width],
        router_sums[expert_total],
        router_sums[:expert_total].T,
        grad_w_gate,
        grad_w_up,
        grad_w_down,
    )


def local_sent(
    hidden_in,
    cotangent,
    seq_lengths,
    expert_ids,
    attn_gain,
    w_query,
    w_key,
    w_value,
    query_gain,
    key_gain,
    w_out,
    ffn_gain,
    w_router,
    w_gate,
    w_up,
    w_down,
):
    tensor_count = lax.axis_size("tensor")
    group_count = lax.axis_size("dp")
    device_total = tensor_count * group_count
    tok_rows, model_width = hidden_in.shape
    topk_count = expert_ids.shape[1]
    local_experts = w_gate.shape[0]
    expert_total = w_router.shape[1]
    slot_count = tok_rows * topk_count // expert_total
    per_group = local_experts * slot_count
    seq_len = tok_rows * tensor_count
    local_width = w_query.shape[1]
    head_width = HDIM
    local_heads = local_width // head_width
    block_rows = min(512, seq_len)
    block_count = seq_len // block_rows
    score_scale = head_width ** (-0.5)
    live_length = seq_lengths[0]
    cosine, sine_table = (table[:, None, :] for table in rope_tables(seq_len, head_width))
    key_pos = jnp.arange(seq_len)
    key_live = key_pos < live_length

    def send_out(rows_low):
        grouped_rows = rows_low.reshape(group_count, 1, per_group, model_width)
        copies = jnp.broadcast_to(
            grouped_rows, (group_count, tensor_count, per_group, model_width)
        ).reshape(device_total, per_group, model_width)
        arrived = lax.all_to_all(copies, ("dp", "tensor"), split_axis=0, concat_axis=0, tiled=True)
        return arrived.reshape(device_total, local_experts, slot_count, model_width)

    def send_back(parts_low):
        returned = lax.all_to_all(
            parts_low.reshape(device_total, per_group, model_width),
            ("dp", "tensor"),
            split_axis=0,
            concat_axis=0,
            tiled=True,
        )
        return jnp.sum(
            returned.reshape(group_count, tensor_count, per_group, model_width).astype(F32),
            axis=1,
        ).reshape(-1, model_width)

    resid = hidden_in.astype(F32)
    scale_one = rms_scale(resid)
    normed = resid * scale_one
    attn_in = (normed * attn_gain.astype(F32)).astype(BF16)
    gathered = lax.all_gather(attn_in, "tensor", axis=0, tiled=True)
    q_raw = jnp.dot(gathered, w_query, preferred_element_type=F32)
    k_raw = jnp.dot(gathered, w_key, preferred_element_type=F32)
    v_raw = jnp.dot(gathered, w_value, preferred_element_type=F32)
    q_square, k_square = lax.psum(
        (jnp.sum(q_raw * q_raw, axis=1), jnp.sum(k_raw * k_raw, axis=1)), "tensor"
    )
    q_rscale = lax.rsqrt(q_square / model_width + EPS)[:, None]
    k_rscale = lax.rsqrt(k_square / model_width + EPS)[:, None]
    query_hat = q_raw * q_rscale
    key_hat = k_raw * k_rscale
    q_gain = query_gain.astype(F32)
    k_gain = key_gain.astype(F32)
    q_rot = rotate(
        (query_hat * q_gain).reshape(seq_len, local_heads, head_width), cosine, sine_table
    ).astype(BF16)
    k_rot = rotate(
        (key_hat * k_gain).reshape(seq_len, local_heads, head_width), cosine, sine_table
    ).astype(BF16)
    v_low = v_raw.astype(BF16).reshape(seq_len, local_heads, head_width)
    starts = jnp.arange(block_count) * block_rows
    q_blocks = q_rot.reshape(block_count, block_rows, local_heads, head_width)

    def allowed_mask(row_start):
        q_pos = row_start + jnp.arange(block_rows)
        return ((key_pos[None, :] <= q_pos[:, None]) & key_live[None, :])[None]

    def attend(inputs):
        q_block, row_start = inputs
        scores = (
            jnp.einsum("qhd,khd->hqk", q_block, k_rot, preferred_element_type=F32)
            * score_scale
        )
        scores = jnp.where(allowed_mask(row_start), scores, -1e30)
        row_max = jnp.max(scores, axis=-1, keepdims=True)
        exp_scores = jnp.exp(scores - row_max)
        row_total = jnp.sum(exp_scores, axis=-1, keepdims=True)
        soft_low = (exp_scores / row_total).astype(BF16)
        attended = jnp.einsum("hqk,khd->qhd", soft_low, v_low, preferred_element_type=F32)
        return (attended, (row_max + jnp.log(row_total))[..., 0])

    o_blocks, lse_blocks = lax.map(attend, (q_blocks, starts))
    o_low = o_blocks.reshape(seq_len, local_width).astype(BF16)
    attn_rows = lax.psum_scatter(
        jnp.dot(o_low, w_out, preferred_element_type=F32),
        "tensor",
        scatter_dimension=0,
        tiled=True,
    )
    mixed = resid + attn_rows
    scale_two = rms_scale(mixed)
    mixed_norm = mixed * scale_two
    ffn_in = (mixed_norm * ffn_gain.astype(F32)).astype(BF16)
    logits = jnp.dot(ffn_in, w_router, preferred_element_type=F32)
    router_probs = jax.nn.softmax(logits, axis=-1)
    expert_hot = (expert_ids[:, :, None] == jnp.arange(expert_total)[None, None, :]).astype(
        F32
    )
    gate_values = jnp.einsum("tke,te->tk", expert_hot, router_probs)
    flat_ids = expert_ids.reshape(-1)
    sort_order = jnp.argsort(flat_ids, stable=True)
    inverse = jnp.argsort(sort_order)
    expert_in = send_out(ffn_in[sort_order // topk_count])
    gate_pre = jnp.einsum("secd,edf->secf", expert_in, w_gate, preferred_element_type=F32)
    up_pre = jnp.einsum("secd,edf->secf", expert_in, w_up, preferred_element_type=F32)
    silu_gate = jax.nn.silu(gate_pre)
    acts = (silu_gate * up_pre).astype(BF16)
    partial_value = jnp.einsum(
        "secf,efd->secd", acts, w_down, preferred_element_type=F32
    ).astype(BF16)
    out_sorted = send_back(partial_value)
    out_assign = out_sorted[inverse].reshape(tok_rows, topk_count, model_width)
    expert_mix = jnp.einsum("tk,tkd->td", gate_values, out_assign)
    result = mixed + expert_mix
    d_result = cotangent.astype(F32)
    d_gates = jnp.einsum("tkd,td->tk", out_assign, d_result)
    d_out = (
        (gate_values[:, :, None] * d_result[:, None, :])
        .astype(BF16)
        .reshape(-1, model_width)[sort_order]
    )
    d_arrived = send_out(d_out)
    d_acts = jnp.einsum("secd,efd->secf", d_arrived, w_down, preferred_element_type=F32)
    sigmoid_gate = jax.nn.sigmoid(gate_pre)
    d_gate_pre = (d_acts * up_pre * sigmoid_gate * (1.0 + gate_pre * (1.0 - sigmoid_gate))).astype(
        BF16
    )
    d_up_pre = (d_acts * silu_gate).astype(BF16)
    grad_w_down = jnp.einsum("secf,secd->efd", acts, d_arrived, preferred_element_type=F32)
    grad_w_gate = jnp.einsum(
        "secd,secf->edf", expert_in, d_gate_pre, preferred_element_type=F32
    )
    grad_w_up = jnp.einsum(
        "secd,secf->edf", expert_in, d_up_pre, preferred_element_type=F32
    )
    d_rows = (
        jnp.einsum("secf,edf->secd", d_gate_pre, w_gate, preferred_element_type=F32)
        + jnp.einsum("secf,edf->secd", d_up_pre, w_up, preferred_element_type=F32)
    ).astype(BF16)
    d_sorted = send_back(d_rows)
    d_ffn = jnp.sum(d_sorted[inverse].reshape(tok_rows, topk_count, model_width), axis=1)
    d_probs = jnp.einsum("tk,tke->te", d_gates, expert_hot)
    d_logits = (
        router_probs * (d_probs - jnp.sum(router_probs * d_probs, axis=-1, keepdims=True))
    ).astype(BF16)
    router_part = contract_rows(ffn_in, d_logits)
    d_ffn = d_ffn + times_transpose(d_logits, w_router)
    ffn_gain_part = jnp.sum(d_ffn * mixed_norm, axis=0)
    d_norm_two = d_ffn * ffn_gain.astype(F32)
    d_mixed = d_result + scale_two * (
        d_norm_two - mixed_norm * jnp.mean(d_norm_two * mixed_norm, axis=-1, keepdims=True)
    )
    d_attn = d_mixed.astype(BF16)
    d_attn_all = lax.all_gather(d_attn, "tensor", axis=0, tiled=True)
    grad_w_out = contract_rows(o_low, d_attn_all)
    d_attended = (
        times_transpose(d_attn_all, w_out)
        .astype(BF16)
        .reshape(block_count, block_rows, local_heads, head_width)
    )

    def attend_back(carry, inputs):
        dk_total, dv_total = carry
        q_block, do_block, lse_block, row_start = inputs
        scores = (
            jnp.einsum("qhd,khd->hqk", q_block, k_rot, preferred_element_type=F32)
            * score_scale
        )
        allowed = allowed_mask(row_start)
        scores = jnp.where(allowed, scores, -1e30)
        soft = jnp.where(allowed, jnp.exp(scores - lse_block[..., None]), 0.0)
        d_weights = jnp.einsum("qhd,khd->hqk", do_block, v_low, preferred_element_type=F32)
        d_scores = (soft * (d_weights - jnp.sum(soft * d_weights, axis=-1, keepdims=True))).astype(
            BF16
        )
        dq_block = (
            jnp.einsum("hqk,khd->qhd", d_scores, k_rot, preferred_element_type=F32)
            * score_scale
        )
        dk_total = (
            dk_total
            + jnp.einsum("hqk,qhd->khd", d_scores, q_block, preferred_element_type=F32)
            * score_scale
        )
        dv_total = dv_total + jnp.einsum(
            "hqk,qhd->khd", soft.astype(BF16), do_block, preferred_element_type=F32
        )
        return ((dk_total, dv_total), dq_block)

    zero_field = jnp.zeros((seq_len, local_heads, head_width), F32)
    (dk_rot, dv_full), dq_blocks = lax.scan(
        attend_back, (zero_field, zero_field), (q_blocks, d_attended, lse_blocks, starts)
    )
    dq_gain = unrotate(
        dq_blocks.reshape(seq_len, local_heads, head_width), cosine, sine_table
    ).reshape(seq_len, local_width)
    dk_gain = unrotate(dk_rot, cosine, sine_table).reshape(seq_len, local_width)
    query_gain_part = jnp.sum(dq_gain * query_hat, axis=0)
    key_gain_part = jnp.sum(dk_gain * key_hat, axis=0)
    dq_hat = dq_gain * q_gain
    dk_hat = dk_gain * k_gain
    q_inner, k_inner = lax.psum(
        (jnp.sum(dq_hat * query_hat, axis=1), jnp.sum(dk_hat * key_hat, axis=1)), "tensor"
    )
    dq_raw = (q_rscale * (dq_hat - query_hat * (q_inner / model_width)[:, None])).astype(
        BF16
    )
    dk_raw = (k_rscale * (dk_hat - key_hat * (k_inner / model_width)[:, None])).astype(BF16)
    dv_raw = dv_full.reshape(seq_len, local_width).astype(BF16)
    grad_query = contract_rows(gathered, dq_raw)
    grad_key = contract_rows(gathered, dk_raw)
    grad_value = contract_rows(gathered, dv_raw)
    total_term = times_transpose(dq_raw, w_query)
    total_term = total_term + times_transpose(dk_raw, w_key)
    d_attn_in = lax.psum_scatter(
        (total_term + times_transpose(dv_raw, w_value)).astype(BF16),
        "tensor",
        scatter_dimension=0,
        tiled=True,
    ).astype(F32)
    attn_gain_part = jnp.sum(d_attn_in * normed, axis=0)
    d_norm_one = d_attn_in * attn_gain.astype(F32)
    d_input = d_mixed + scale_one * (
        d_norm_one - normed * jnp.mean(d_norm_one * normed, axis=-1, keepdims=True)
    )
    dp_sums = (
        lax.psum(grad_query.astype(BF16), "dp").astype(F32),
        lax.psum(grad_key.astype(BF16), "dp").astype(F32),
        lax.psum(grad_value.astype(BF16), "dp").astype(F32),
        lax.psum(query_gain_part.astype(BF16), "dp").astype(F32),
        lax.psum(key_gain_part.astype(BF16), "dp").astype(F32),
        lax.psum(grad_w_out.astype(BF16), "dp").astype(F32),
    )
    shared = lax.psum((attn_gain_part, ffn_gain_part, router_part), ("dp", "tensor"))
    return (
        result.astype(BF16),
        d_input.astype(BF16),
        dp_sums[0],
        dp_sums[1],
        dp_sums[2],
        dp_sums[3],
        dp_sums[4],
        dp_sums[5],
        shared[0],
        shared[1],
        shared[2],
        grad_w_gate,
        grad_w_up,
        grad_w_down,
    )


def solution(mesh):
    rows, columns = P(BOTH, None), P(None, "tensor")
    gathered_plan = (mesh.shape["dp"], mesh.shape["tensor"]) == (2 * RING, 4)
    return jax.shard_map(
        local_gathered if gathered_plan else local_sent,
        mesh=mesh,
        in_specs=(
            rows,
            rows,
            P("dp"),
            rows,
            P(),
            columns,
            columns,
            columns,
            P("tensor"),
            P("tensor"),
            P("tensor", None),
            P(),
            P(),
            P("dp", None, "tensor"),
            P("dp", None, "tensor"),
            P("dp", "tensor", None),
        ),
        out_specs=(
            rows,
            rows,
            columns,
            columns,
            columns,
            P("tensor"),
            P("tensor"),
            P("tensor", None),
            P(),
            P(),
            P(),
            P("dp", None, "tensor"),
            P("dp", None, "tensor"),
            P("dp", "tensor", None),
        ),
        check_vma=False,
    )
```

```python
import functools
import math

import jax
import jax.numpy as jnp
from jax import lax
from jax.experimental import pallas as pl
from jax.experimental.pallas import tpu as pltpu
from jax.sharding import PartitionSpec as P

HDIM = 128
EPS = 1e-05
ROPE_BASE = 10000.0
BOTH = ("dp", "tensor")
F32 = jnp.float32
BF16 = jnp.bfloat16
VMEM_GRANT = 60 << 20
fence = lax.optimization_barrier


def rms_scale(values):
    return lax.rsqrt(jnp.mean(values * values, axis=-1, keepdims=True) + EPS)


def rope_tables(count, head_width):
    half_width = head_width // 2
    frequency = jnp.exp(
        -(jnp.arange(half_width, dtype=F32) * 2.0 / head_width) * math.log(ROPE_BASE)
    )
    angles = jnp.arange(count, dtype=F32)[:, None] * frequency[None, :]
    return (jnp.cos(angles), jnp.sin(angles))


def rotate(values_in, cosine, sine_table):
    half_width = values_in.shape[-1] // 2
    front_half = values_in[..., :half_width]
    back_half = values_in[..., half_width:]
    return jnp.concatenate(
        [
            front_half * cosine - back_half * sine_table,
            back_half * cosine + front_half * sine_table,
        ],
        axis=-1,
    )


def unrotate(grads_in, cosine, sine_table):
    return rotate(grads_in, cosine, -sine_table)


def contract_rows(left, right):
    return lax.dot_general(left, right, (((0,), (0,)), ((), ())), preferred_element_type=F32)


def times_transpose(left, right):
    return lax.dot_general(left, right, (((1,), (1,)), ((), ())), preferred_element_type=F32)


def add_low(*terms):
    total = terms[0].astype(F32)
    for term in terms[1:]:
        total = total + term.astype(F32)
    return total.astype(BF16)


def add_wide(*terms):
    total = terms[0].astype(F32)
    for term in terms[1:]:
        total = total + term.astype(F32)
    return total


RING = 4
COLUMNS = (
    ((0, 0, 0), (1, 0, 0), (0, 1, 0), (0, 0, 1)),
    ((2, 0, 0), (1, 1, 0), (1, 0, 1), (2, 1, 0)),
    ((3, 0, 0), (3, 1, 0), (2, 0, 1), (3, 0, 1)),
    ((1, 1, 1), (2, 1, 1)),
    ((0, 1, 1), (3, 1, 1)),
)
CHUNKS = tuple(tuple(chip + (dc,) for dc in (0, 1) for chip in chips) for chips in COLUMNS)
STARTS = tuple(sum(len(chunk) for chunk in CHUNKS[:i]) for i in range(len(CHUNKS)))
PLACES = tuple(place for chunk in CHUNKS for place in chunk)
MOVES = {
    "x": lambda z, x, y, c: (z, x ^ 1, y, c),
    "y": lambda z, x, y, c: (z, x, y ^ 1, c),
    "c": lambda z, x, y, c: (z, x, y, c ^ 1),
    "z": lambda z, x, y, c: ((z - 1) % RING, x, y, c),
    "u1": lambda z, x, y, c: ((z + 1) % RING, x, y, c),
    "u2": lambda z, x, y, c: ((z + 2) % RING, x, y, c),
    "u3": lambda z, x, y, c: ((z + 3) % RING, x, y, c),
    "z1": lambda z, x, y, c: (z ^ 1, x, y, c),
    "z2": lambda z, x, y, c: (z ^ 2, x, y, c),
}


def device_pairs(move):
    pairs = []
    for z in range(RING):
        for x in range(2):
            for y in range(2):
                for c in range(2):
                    tz, tx, ty, tc = move(z, x, y, c)
                    pairs.append(((z * 2 + x) * 4 + y * 2 + c, (tz * 2 + tx) * 4 + ty * 2 + tc))
    return pairs


def send(value, axis):
    return lax.ppermute(value, BOTH, device_pairs(MOVES[axis]))


def small_sum(value, axes):
    for axis in axes:
        value = value + send(value, axis)
    return value


def hop(axis, k, dx, dy):
    return {"z": ((k + 1) % RING, dx, dy), "x": (k, dx ^ 1, dy), "y": (k, dx, dy ^ 1)}[axis]


class Stages:
    def __init__(self, token):
        self.token = token

    def run(self, sends, works=()):
        values, args, _ = fence(([s[0] for s in sends], [w[1] for w in works], self.token))
        got, crossed = [], []
        for value, (_, axis) in zip(values, sends):
            if axis == "c" and len(crossed) >= 2:
                value, _ = fence((value, crossed[-2]))
            got.append(send(value, axis))
            if axis == "c":
                crossed.append(got[-1])
        made = [work(*arg) for (work, _), arg in zip(works, args)]
        got, made = fence((got, made))
        self.token = jax.tree.leaves((got, made))[0]
        return got, made


class Gather:
    def __init__(self, block):
        self.held = {(0, 0, 0, 0): block}

    def sends(self, hops):
        return [(self.held[chip + (0,)], axis) for axis, chip in hops]

    def take(self, hops, got):
        for (axis, chip), value in zip(hops, got):
            self.held[chip + (1,) if axis == "c" else hop(axis, *chip) + (0,)] = value

    def chunk(self, i):
        chunk = CHUNKS[i]
        late = [place for place in chunk if place not in self.held]
        values = [self.held[place] for place in chunk if place in self.held]
        return values, [self.held[place[:3] + (0,)] for place in late], late

    @staticmethod
    def complete(i, values, crossing, late):
        blocks = dict(zip([place for place in CHUNKS[i] if place not in late], values))
        done = []
        for place, value in zip(late, crossing):
            if len(done) >= 2:
                value, _ = fence((value, done[-2]))
            done.append(send(value, "c"))
            blocks[place] = done[-1]
        return [blocks[place] for place in CHUNKS[i]]


class Scatter:
    def __init__(self):
        self.held = {}

    def put(self, i, sums):
        for chip, value in zip(COLUMNS[i], sums):
            self.held.setdefault(chip, []).append(value)

    def sends(self, hops):
        groups = [self.held[chip] for _, chip in hops]
        added = [group for group in groups if len(group) > 1]
        sums = iter(block_sums(added) if added else ())
        return [(next(sums) if len(group) > 1 else group[0], axis) for group, (axis, _) in zip(groups, hops)]

    def take(self, hops, got):
        for (axis, chip), value in zip(hops, got):
            self.held.setdefault(hop(axis, *chip), []).append(value)

    def total(self):
        return add_wide(*self.held[0, 0, 0])


class DpSum:
    def __init__(self, value):
        group = lax.axis_index("dp")
        self.z, self.x = group // 2, group % 2
        self.value = value
        self.half, self.piece = value.shape[0] // 2, value.shape[0] // (2 * RING)

    def split_x(self):
        return [(lax.dynamic_slice_in_dim(self.value, (1 - self.x) * self.half, self.half), "x")]

    def add_x(self, got):
        self.sum = add_low(lax.dynamic_slice_in_dim(self.value, self.x * self.half, self.half), got[0])

    def split_z(self):
        return [
            (lax.dynamic_slice_in_dim(self.sum, ((self.z + d) % RING) * self.piece, self.piece), f"u{d}")
            for d in (1, 2, 3)
        ]

    def add_z(self, got):
        self.part = add_low(lax.dynamic_slice_in_dim(self.sum, self.z * self.piece, self.piece), *got)

    def reduce_z(self, half):
        low, high = self.z % 2, self.z // 2
        pieces = half.reshape((2, 2, self.piece) + half.shape[1:])
        for bit, axis, name in ((low, 1, "z1"), (high, 0, "z2")):
            mine = lax.dynamic_index_in_dim(pieces, bit, axis, keepdims=False)
            other = lax.dynamic_index_in_dim(pieces, 1 - bit, axis, keepdims=False)
            pieces = add_low(mine, send(other, name))
        return pieces

    def collect_z(self, part):
        low, high = self.z % 2, self.z // 2
        for bit, axis, name in ((high, 0, "z2"), (low, 1, "z1")):
            other = send(part, name)
            first, second = jnp.where(bit == 0, part, other), jnp.where(bit == 0, other, part)
            part = jnp.stack([first, second], axis=axis)
        return part.reshape((self.half,) + part.shape[3:])

    def join_z(self):
        return [(self.part, f"u{d}") for d in (1, 2, 3)]

    def took_z(self, got):
        stack = jnp.stack([self.part] + list(got))
        order = (self.z - jnp.arange(RING)) % RING
        self.whole_half = stack[order].reshape(self.half, -1)

    def join_x(self):
        return [(self.whole_half, "x")]

    def took_x(self, got):
        mine, other = self.whole_half, got[0]
        first = jnp.where(self.x == 0, mine, other)
        second = jnp.where(self.x == 0, other, mine)
        self.result = jnp.concatenate([first, second], axis=0).astype(F32)


def core_sum(near, far):
    return pair_sum(near, send(far, "c"))


def place_indices():
    group, member = lax.axis_index("dp"), lax.axis_index("tensor")
    z, x, y, c = group // 2, group % 2, member // 2, member % 2
    absolute = jnp.stack(
        [(((z + k) % RING) * 2 + (x ^ dx)) * 4 + (y ^ dy) * 2 + (c ^ dc) for k, dx, dy, dc in PLACES]
    )
    table = [0] * len(PLACES)
    for position, (k, dx, dy, dc) in enumerate(PLACES):
        table[((k * 2 + dx) * 2 + dy) * 2 + dc] = position
    numbers = jnp.arange(len(PLACES))
    other_z, other_x = numbers // 8, (numbers // 4) % 2
    other_y, other_c = (numbers // 2) % 2, numbers % 2
    offset = ((((other_z - z) % RING) * 2 + (other_x ^ x)) * 2 + (other_y ^ y)) * 2 + (other_c ^ c)
    return absolute, jnp.asarray(table, jnp.int32)[offset]


def nn(left, right):
    return lax.dot_general(left, right, (((1,), (0,)), ((), ())), preferred_element_type=F32)


def nt(left, right):
    return lax.dot_general(left, right, (((1,), (1,)), ((), ())), preferred_element_type=F32)


def pick_rows(picks_ref, blocks, rows_ref, slot_count, width):
    experts = rows_ref.shape[0]
    for b, block in enumerate(blocks):
        for low in range(0, block.shape[1], width):
            columns = pl.ds(low, width)
            picked = nn(picks_ref[b], block[:, columns]).astype(BF16)
            for e in range(experts):
                rows_ref[e, pl.ds(b * slot_count, slot_count), columns] = picked[
                    e * slot_count : (e + 1) * slot_count
                ]


def give_rows(picks_ref, rows_ref, blocks, slot_count, width, first=0):
    experts = rows_ref.shape[0]
    for b, block in enumerate(blocks):
        for low in range(0, block.shape[1], width):
            columns = pl.ds(low, width)
            slots = jnp.concatenate(
                [rows_ref[e, pl.ds(first + b * slot_count, slot_count), columns] for e in range(experts)],
                axis=0,
            )
            block[:, columns] = contract_rows(picks_ref[b], slots).astype(BF16)


def cot_kernel(count, slot_count, picks_ref, down_ref, *refs):
    blocks, (rows_out, acts_out, rows_ref) = refs[:count], refs[count:]
    e = pl.program_id(0)

    @pl.when(e == 0)
    def _():
        pick_rows(picks_ref, blocks, rows_ref, slot_count, 512)

    rows = rows_ref[e]
    rows_out[0] = rows
    acts_out[0] = nt(rows, down_ref[0])


def main_kernel(count, slot_count, picks_ref, gates_ref, acts_ref, gate_ref, up_ref, *refs):
    blocks = refs[:count]
    rows_out, scaled_out, d_gate_out, d_up_out, d_probs_out = refs[count : count + 5]
    near_out, far_out, rows_ref = refs[count + 5 :]
    results = [out.at[b] for out in (near_out, far_out) for b in range(count // 2)]
    e = pl.program_id(0)

    @pl.when(e == 0)
    def _():
        pick_rows(picks_ref, blocks, rows_ref, slot_count, 512)

    rows = rows_ref[e]
    rows_out[0] = rows
    pre, up = nn(rows, gate_ref[0]), nn(rows, up_ref[0])
    cot_acts = acts_ref[0]
    own_slots = pl.ds(pl.multiple_of(e * slot_count, slot_count), slot_count)
    own_picks = [picks_ref[b, own_slots, :].astype(F32) for b in range(count)]
    gate = jnp.concatenate(
        [
            jnp.sum(pick * gates_ref[b, pl.ds(e, 1), :], axis=1, keepdims=True)
            for b, pick in enumerate(own_picks)
        ],
        axis=0,
    )
    sig = jax.nn.sigmoid(pre)
    silu = pre * sig
    acts = silu * up
    scaled_out[0] = (gate * acts).astype(BF16)
    inner = jnp.sum(acts.astype(BF16).astype(F32) * cot_acts, axis=1, keepdims=True)
    for b, pick in enumerate(own_picks):
        here = inner[b * slot_count : (b + 1) * slot_count]
        d_probs_out[b, pl.ds(e, 1), :] = jnp.sum(pick * here, axis=0, keepdims=True)
    d_acts = gate * cot_acts
    d_pre = (d_acts * up * sig * (1.0 + pre * (1.0 - sig))).astype(BF16)
    d_up = (d_acts * silu).astype(BF16)
    d_gate_out[0] = d_pre
    d_up_out[0] = d_up
    rows_ref[e] = (nt(d_pre, gate_ref[0]) + nt(d_up, up_ref[0])).astype(BF16)

    @pl.when(e == pl.num_programs(0) - 1)
    def _():
        give_rows(picks_ref, rows_ref, results, slot_count, 512)


def out_kernel(parts, slot_count, *refs):
    picks, scaled, down_ref = refs[:parts], refs[parts : 2 * parts], refs[2 * parts]
    near_out, far_out, rows_ref = refs[2 * parts + 1 :]
    e = pl.program_id(0)
    rows = scaled[0][0] if parts == 1 else jnp.concatenate([part[0] for part in scaled], axis=0)
    rows_ref[e] = nn(rows, down_ref[0]).astype(BF16)

    @pl.when(e == pl.num_programs(0) - 1)
    def _():
        low, done = 0, 0
        for part in picks:
            count = part.shape[0]
            half = count // 2
            results = [out.at[done + b] for out in (near_out, far_out) for b in range(half)]
            give_rows(part, rows_ref, results, slot_count, 512, low)
            low, done = low + count * slot_count, done + half


def per_expert(*shape):
    return pl.BlockSpec((1,) + shape, lambda e: (e,) + (0,) * len(shape))


def resident(*shape):
    return pl.BlockSpec(shape, lambda e: (0,) * len(shape), pipeline_mode=pl.Buffered(1))


def cot_chunk(picks, w_down, blocks, slot_count):
    experts, hidden, width = w_down.shape
    count, tokens = len(blocks), blocks[0].shape[0]
    rows = count * slot_count
    return pl.pallas_call(
        functools.partial(cot_kernel, count, slot_count),
        grid=(experts,),
        in_specs=[resident(*picks.shape), per_expert(hidden, width)] + [resident(tokens, width)] * count,
        out_specs=[per_expert(rows, width), per_expert(rows, hidden)],
        out_shape=[
            jax.ShapeDtypeStruct((experts, rows, width), BF16),
            jax.ShapeDtypeStruct((experts, rows, hidden), F32),
        ],
        scratch_shapes=[pltpu.VMEM((experts, rows, width), BF16)],
        compiler_params=pltpu.CompilerParams(vmem_limit_bytes=VMEM_GRANT),
        cost_estimate=pl.CostEstimate(
            flops=2 * experts * rows * width * (hidden + tokens),
            bytes_accessed=2 * (count * tokens * width + experts * (rows + hidden) * width),
            transcendentals=0,
        ),
    )(picks, w_down, *blocks)


def main_chunk(picks, gates, cot_acts, acts_at, w_gate, w_up, blocks, slot_count):
    experts, width, hidden = w_gate.shape
    count, tokens = len(blocks), blocks[0].shape[0]
    rows = count * slot_count
    outs = pl.pallas_call(
        functools.partial(main_kernel, count, slot_count),
        grid=(experts,),
        in_specs=[
            resident(*picks.shape),
            resident(*gates.shape),
            pl.BlockSpec((1, rows, hidden), lambda e: (e, acts_at, 0)),
            per_expert(width, hidden),
            per_expert(width, hidden),
        ]
        + [resident(tokens, width)] * count,
        out_specs=[
            per_expert(rows, width),
            per_expert(rows, hidden),
            per_expert(rows, hidden),
            per_expert(rows, hidden),
            resident(*gates.shape),
        ]
        + [resident(count // 2, tokens, width)] * 2,
        out_shape=[
            jax.ShapeDtypeStruct((experts, rows, width), BF16),
            jax.ShapeDtypeStruct((experts, rows, hidden), BF16),
            jax.ShapeDtypeStruct((experts, rows, hidden), BF16),
            jax.ShapeDtypeStruct((experts, rows, hidden), BF16),
            jax.ShapeDtypeStruct(gates.shape, F32),
        ]
        + [jax.ShapeDtypeStruct((count // 2, tokens, width), BF16)] * 2,
        scratch_shapes=[pltpu.VMEM((experts, rows, width), BF16)],
        compiler_params=pltpu.CompilerParams(vmem_limit_bytes=VMEM_GRANT),
        cost_estimate=pl.CostEstimate(
            flops=2 * experts * rows * width * (4 * hidden + 2 * tokens),
            bytes_accessed=2 * (2 * count * tokens * width + experts * (rows + 2 * hidden) * width),
            transcendentals=experts * rows * hidden,
        ),
    )(picks, gates, cot_acts, w_gate, w_up, *blocks)
    return outs[:5], outs[5:]


def out_chunk(picks, scaled, w_down, slot_count):
    experts, hidden, width = w_down.shape
    tokens = picks[0].shape[2]
    count = sum(part.shape[0] for part in picks)
    rows = count * slot_count
    return pl.pallas_call(
        functools.partial(out_kernel, len(picks), slot_count),
        grid=(experts,),
        in_specs=[resident(*part.shape) for part in picks]
        + [per_expert(*part.shape[1:]) for part in scaled]
        + [per_expert(hidden, width)],
        out_specs=[resident(count // 2, tokens, width)] * 2,
        out_shape=[jax.ShapeDtypeStruct((count // 2, tokens, width), BF16)] * 2,
        scratch_shapes=[pltpu.VMEM((experts, rows, width), BF16)],
        compiler_params=pltpu.CompilerParams(vmem_limit_bytes=VMEM_GRANT),
        cost_estimate=pl.CostEstimate(
            flops=2 * experts * rows * width * (hidden + tokens),
            bytes_accessed=2 * (count * tokens * width + experts * (rows + hidden) * width),
            transcendentals=0,
        ),
    )(*picks, *scaled, w_down)


def grad_kernel(count, *refs):
    rows, cots, scaled, d_gate, d_up = (refs[i * count : (i + 1) * count] for i in range(5))
    gate_out, up_out, down_out = refs[-3:]

    def total(lefts, rights):
        value = None
        for left, right in zip(lefts, rights):
            term = contract_rows(left[0], right[0])
            value = term if value is None else value + term
        return value

    gate_out[0] = total(rows, d_gate)
    up_out[0] = total(rows, d_up)
    down_out[0] = total(scaled, cots)


def expert_grads(rows, cots, scaled, d_gate, d_up, cots_at, first, last, earlier=None, tile=512):
    count, experts, width = len(rows), rows[0].shape[0], rows[0].shape[2]
    hidden = scaled[0].shape[2]
    slots = sum(part.shape[1] for part in rows)
    wide = [pl.BlockSpec((1, part.shape[1], tile), lambda e, n: (first + e, 0, n)) for part in rows]
    wide_cots = [
        pl.BlockSpec((1, part.shape[1], tile), lambda e, n, at=at: (first + e, at, n))
        for part, at in zip(rows, cots_at)
    ]
    narrow = [pl.BlockSpec((1, part.shape[1], hidden), lambda e, n: (first + e, 0, 0)) for part in rows]
    tall = pl.BlockSpec((1, tile, hidden), lambda e, n: (first + e, n, 0))
    given = [] if earlier is None else list(earlier)
    return pl.pallas_call(
        functools.partial(grad_kernel, count),
        grid=(last - first, width // tile),
        in_specs=wide + wide_cots + narrow * 3 + [pl.BlockSpec(memory_space=pl.ANY)] * len(given),
        out_specs=[tall, tall, pl.BlockSpec((1, hidden, tile), lambda e, n: (first + e, 0, n))],
        out_shape=[
            jax.ShapeDtypeStruct((experts, width, hidden), F32),
            jax.ShapeDtypeStruct((experts, width, hidden), F32),
            jax.ShapeDtypeStruct((experts, hidden, width), F32),
        ],
        input_output_aliases={5 * count + i: i for i in range(len(given))},
        compiler_params=pltpu.CompilerParams(vmem_limit_bytes=VMEM_GRANT),
        cost_estimate=pl.CostEstimate(
            flops=6 * (last - first) * slots * width * hidden,
            bytes_accessed=(last - first) * (4 * slots * width + 12 * width * hidden),
            transcendentals=0,
        ),
    )(*rows, *cots, *scaled, *d_gate, *d_up, *given)


def sums_kernel(counts, *refs):
    terms, outs = refs[: sum(counts)], refs[sum(counts) :]
    for count, out in zip(counts, outs):
        value = terms[0][...].astype(F32)
        for term in terms[1:count]:
            value = value + term[...].astype(F32)
        out[...] = value.astype(BF16)
        terms = terms[count:]


def block_sums(groups, tile=64):
    rows, width = groups[0][0].shape
    counts = [len(group) for group in groups]
    block = pl.BlockSpec((tile, width), lambda i: (i, 0))
    return pl.pallas_call(
        functools.partial(sums_kernel, counts),
        grid=(rows // tile,),
        in_specs=[block] * sum(counts),
        out_specs=[block] * len(groups),
        out_shape=[jax.ShapeDtypeStruct((rows, width), BF16)] * len(groups),
        compiler_params=pltpu.CompilerParams(vmem_limit_bytes=VMEM_GRANT),
        cost_estimate=pl.CostEstimate(
            flops=sum(counts) * rows * width,
            bytes_accessed=2 * (sum(counts) + len(groups)) * rows * width,
            transcendentals=0,
        ),
    )(*[term for group in groups for term in group])


def qkv_kernel(*refs):
    blocks, (q_w, k_w, v_w, q_out, k_out, v_out, q_sq, k_sq) = refs[:-8], refs[-8:]
    lanes = q_sq.shape[1]
    rows = blocks[0].shape[0]
    for b, block in enumerate(blocks):
        here = pl.ds(b * rows, rows)
        for weight, out, squares in ((q_w, q_out, q_sq), (k_w, k_out, k_sq)):
            value = nn(block[...], weight[...])
            out[here, :] = value
            value = value * value
            total = value[:, :lanes]
            for low in range(lanes, value.shape[1], lanes):
                total = total + value[:, low : low + lanes]

            @pl.when(pl.program_id(0) == 0)
            def _(squares=squares, total=total):
                squares[here, :] = total

            @pl.when(pl.program_id(0) > 0)
            def _(squares=squares, total=total):
                squares[here, :] += total

        v_out[here, :] = nn(block[...], v_w[...]).astype(BF16)


def qkv(blocks, w_query, w_key, w_value, tile=256):
    rows, depth = blocks[0].shape
    width = w_query.shape[1]
    count = len(blocks) * rows
    weight = pl.BlockSpec((depth, tile), lambda n: (0, n))
    out = pl.BlockSpec((count, tile), lambda n: (0, n))
    return pl.pallas_call(
        qkv_kernel,
        grid=(width // tile,),
        in_specs=[resident(rows, depth)] * len(blocks) + [weight] * 3,
        out_specs=[out] * 3 + [resident(count, HDIM)] * 2,
        out_shape=[
            jax.ShapeDtypeStruct((count, width), F32),
            jax.ShapeDtypeStruct((count, width), F32),
            jax.ShapeDtypeStruct((count, width), BF16),
            jax.ShapeDtypeStruct((count, HDIM), F32),
            jax.ShapeDtypeStruct((count, HDIM), F32),
        ],
        compiler_params=pltpu.CompilerParams(vmem_limit_bytes=VMEM_GRANT),
        cost_estimate=pl.CostEstimate(
            flops=6 * count * depth * width,
            bytes_accessed=2 * count * depth + 6 * depth * width + 10 * count * width,
            transcendentals=0,
        ),
    )(*blocks, w_query, w_key, w_value)


def pair_kernel(near_ref, far_ref, *outs):
    for b, out in enumerate(outs):
        out[...] = (near_ref[b].astype(F32) + far_ref[b].astype(F32)).astype(BF16)


def pair_sum(near, far, tile=64):
    count, rows, width = near.shape
    stack = pl.BlockSpec((count, tile, width), lambda i: (0, i, 0))
    return pl.pallas_call(
        pair_kernel,
        grid=(rows // tile,),
        in_specs=[stack, stack],
        out_specs=[pl.BlockSpec((tile, width), lambda i: (i, 0))] * count,
        out_shape=[jax.ShapeDtypeStruct((rows, width), BF16)] * count,
        compiler_params=pltpu.CompilerParams(vmem_limit_bytes=VMEM_GRANT),
        cost_estimate=pl.CostEstimate(
            flops=count * rows * width, bytes_accessed=6 * count * rows * width, transcendentals=0
        ),
    )(near, far)


def turn(values, cosine, sine):
    return values * cosine + pltpu.roll(values, values.shape[1] // 2, 1) * sine


def attend_kernel(
    row_block, scale, q_ref, k_ref, v_ref, cols_ref, qg_ref, kg_ref, cos_ref, sin_ref, kpos_ref,
    out_ref, lse_ref, qrot_ref, krot_ref,
):
    cosine, sine = cos_ref[...], sin_ref[...]
    qrot_ref[...] = turn(q_ref[...] * cols_ref[:, 0:1] * qg_ref[...], cosine, sine).astype(BF16)
    krot_ref[...] = turn(k_ref[...] * cols_ref[:, 1:2] * kg_ref[...], cosine, sine).astype(BF16)
    for low in range(0, q_ref.shape[0], row_block):
        rows = pl.ds(low, row_block)
        scores = nt(qrot_ref[rows, :], krot_ref[...]) * scale
        scores = jnp.where(kpos_ref[...] <= cols_ref[rows, 2:3], scores, -1e30)
        top = jnp.max(scores, axis=1, keepdims=True)
        powers = jnp.exp(scores - top)
        total = jnp.sum(powers, axis=1, keepdims=True)
        soft = (powers * (1.0 / total)).astype(BF16)
        out_ref[rows, :] = nn(soft, v_ref[...]).astype(BF16)
        lse_ref[rows, :] = jnp.broadcast_to(top + jnp.log(total), (row_block, HDIM))


def attend_back_kernel(
    row_block, scale, q_ref, k_ref, v_ref, qrot_ref, krot_ref, do_ref, lse_ref, cols_ref, qg_ref, kg_ref,
    cos_ref, sin_ref, kpos_ref,
    dq_ref, dk_ref, dv_ref, qgain_ref, kgain_ref, qin_ref, kin_ref, dq_acc, dk_acc, dv_acc,
):
    for low in range(0, q_ref.shape[0], row_block):
        rows = pl.ds(low, row_block)
        query, d_out = qrot_ref[rows, :], do_ref[rows, :]
        scores = nt(query, krot_ref[...]) * scale
        soft = jnp.where(kpos_ref[...] <= cols_ref[rows, 2:3], jnp.exp(scores - lse_ref[rows, 0:1]), 0.0)
        d_weights = nt(d_out, v_ref[...])
        spread = soft * d_weights
        mean = jnp.sum(spread, axis=1, keepdims=True)
        d_scores = (spread - soft * mean).astype(BF16)
        dq_acc[rows, :] = nn(d_scores, krot_ref[...]) * scale
        d_keys = contract_rows(d_scores, query)
        d_values = contract_rows(soft.astype(BF16), d_out)
        if low:
            dk_acc[...] += d_keys
            dv_acc[...] += d_values
        else:
            dk_acc[...] = d_keys
            dv_acc[...] = d_values
    dv_ref[...] = dv_acc[...].astype(BF16)
    cosine, sine = cos_ref[...], -sin_ref[...]
    for lane, raw_ref, gain_ref, grad, hat_ref, gain_out, inner_out in (
        (0, q_ref, qg_ref, dq_acc[...], dq_ref, qgain_ref, qin_ref),
        (1, k_ref, kg_ref, dk_acc[...] * scale, dk_ref, kgain_ref, kin_ref),
    ):
        hat = raw_ref[...] * cols_ref[:, lane : lane + 1]
        turned = turn(grad, cosine, sine)
        gain_out[...] = jnp.sum(turned * hat, axis=0, keepdims=True)
        d_hat = turned * gain_ref[...]
        hat_ref[...] = d_hat
        inner = d_hat * hat

        @pl.when(pl.program_id(0) == 0)
        def _(inner=inner, inner_out=inner_out):
            inner_out[...] = inner

        @pl.when(pl.program_id(0) > 0)
        def _(inner=inner, inner_out=inner_out):
            inner_out[...] += inner


def head_columns(rows):
    return pl.BlockSpec((rows, HDIM), lambda h: (0, h))


def whole(*shape):
    return pl.BlockSpec(shape, lambda h: (0,) * len(shape))


def attend_forward(q_raw, k_raw, v_low, cols, q_gain, k_gain, cosine, sine, kpos):
    seq_len, width = q_raw.shape
    heads = width // HDIM
    part, one = head_columns(seq_len), head_columns(1)
    return pl.pallas_call(
        functools.partial(attend_kernel, min(256, seq_len), HDIM ** (-0.5)),
        grid=(heads,),
        in_specs=[part, part, part, whole(seq_len, HDIM), one, one]
        + [whole(seq_len, HDIM), whole(seq_len, HDIM), whole(1, seq_len)],
        out_specs=[part, part, part, part],
        out_shape=[
            jax.ShapeDtypeStruct((seq_len, width), BF16),
            jax.ShapeDtypeStruct((seq_len, width), F32),
            jax.ShapeDtypeStruct((seq_len, width), BF16),
            jax.ShapeDtypeStruct((seq_len, width), BF16),
        ],
        compiler_params=pltpu.CompilerParams(vmem_limit_bytes=VMEM_GRANT),
        cost_estimate=pl.CostEstimate(
            flops=4 * seq_len * seq_len * width,
            bytes_accessed=20 * seq_len * width,
            transcendentals=heads * seq_len * seq_len,
        ),
    )(q_raw, k_raw, v_low, cols, q_gain, k_gain, cosine, sine, kpos)


def attend_backward(
    q_raw, k_raw, v_low, q_rot, k_rot, d_out, lse, cols, q_gain, k_gain, cosine, sine, kpos
):
    seq_len, width = q_raw.shape
    heads = width // HDIM
    part, one = head_columns(seq_len), head_columns(1)
    return pl.pallas_call(
        functools.partial(attend_back_kernel, min(256, seq_len), HDIM ** (-0.5)),
        grid=(heads,),
        in_specs=[part, part, part, part, part, part, part, whole(seq_len, HDIM), one, one]
        + [whole(seq_len, HDIM), whole(seq_len, HDIM), whole(1, seq_len)],
        out_specs=[part, part, part, one, one, whole(seq_len, HDIM), whole(seq_len, HDIM)],
        out_shape=[
            jax.ShapeDtypeStruct((seq_len, width), F32),
            jax.ShapeDtypeStruct((seq_len, width), F32),
            jax.ShapeDtypeStruct((seq_len, width), BF16),
            jax.ShapeDtypeStruct((1, width), F32),
            jax.ShapeDtypeStruct((1, width), F32),
            jax.ShapeDtypeStruct((seq_len, HDIM), F32),
            jax.ShapeDtypeStruct((seq_len, HDIM), F32),
        ],
        scratch_shapes=[pltpu.VMEM((seq_len, HDIM), F32)] * 3,
        compiler_params=pltpu.CompilerParams(vmem_limit_bytes=VMEM_GRANT),
        cost_estimate=pl.CostEstimate(
            flops=10 * seq_len * seq_len * width,
            bytes_accessed=32 * seq_len * width,
            transcendentals=heads * seq_len * seq_len,
        ),
    )(q_raw, k_raw, v_low, q_rot, k_rot, d_out, lse, cols, q_gain, k_gain, cosine, sine, kpos)


def local_gathered(
    hidden_in,
    cotangent,
    seq_lengths,
    expert_ids,
    attn_gain,
    w_query,
    w_key,
    w_value,
    query_gain,
    key_gain,
    w_out,
    ffn_gain,
    w_router,
    w_gate,
    w_up,
    w_down,
):
    tensor_count = lax.axis_size("tensor")
    group_count = lax.axis_size("dp")
    tok_rows, model_width = hidden_in.shape
    topk = expert_ids.shape[1]
    expert_total = w_router.shape[1]
    experts = w_gate.shape[0]
    slot_count = tok_rows * topk // expert_total
    devices = len(PLACES)
    seq_len = tok_rows * tensor_count
    local_width = w_query.shape[1]
    half_width = HDIM // 2
    live_length = seq_lengths[0]
    absolute, position = place_indices()

    member = lax.axis_index("tensor")
    blocks_at = member ^ jnp.arange(tensor_count)

    def turn_tables(blocks_at):
        cosine, sine = (
            table.reshape(tensor_count, tok_rows, half_width)[blocks_at].reshape(seq_len, half_width)
            for table in rope_tables(seq_len, HDIM)
        )
        return jnp.concatenate([cosine, cosine], axis=1), jnp.concatenate([-sine, sine], axis=1)

    positions = (blocks_at[:, None] * tok_rows + jnp.arange(tok_rows)[None, :]).reshape(-1)
    never = 2 * seq_len
    key_pos = jnp.where(positions < live_length, positions, never).astype(F32)[None, :]

    def token_sums(*values):
        stacked = jnp.stack([value.reshape(tensor_count, tok_rows) for value in values])
        summed = lax.psum(stacked[:, blocks_at], "tensor")
        return summed[:, blocks_at].reshape(len(values), seq_len)

    def to_groups(by_expert):
        copies = jnp.broadcast_to(
            by_expert.reshape(group_count, 1, experts, tok_rows),
            (group_count, tensor_count, experts, tok_rows),
        ).reshape(devices, experts, tok_rows)
        return lax.all_to_all(copies, BOTH, split_axis=0, concat_axis=0, tiled=True)[absolute]

    resid = hidden_in.astype(F32)
    scale_one = rms_scale(resid)
    normed = resid * scale_one
    attn_in = (normed * attn_gain.astype(F32)).astype(BF16)
    q_gain = query_gain.astype(F32)[None, :]
    k_gain = key_gain.astype(F32)[None, :]

    hot = jnp.any(expert_ids.T[None, :, :] == jnp.arange(expert_total)[:, None, None], axis=1)
    earlier = jnp.triu(jnp.ones((tok_rows, tok_rows), F32), 1).astype(BF16)
    rank = jnp.dot(hot.astype(BF16), earlier, preferred_element_type=F32)
    slot_of = jnp.where(hot, rank, -1.0)

    def all_picks(slot_of):
        slots = jnp.arange(slot_count, dtype=F32)
        wide = (slot_of[:, :, None, :] == slots[None, None, :, None]).astype(BF16)
        return [
            wide[low : low + len(chunk)].reshape(len(chunk), experts * slot_count, tok_rows)
            for chunk, low in zip(CHUNKS, STARTS)
        ]


    stages = Stages(attn_in)
    cot, ffn = Gather(cotangent), Gather(None)
    d_sum, out_sum = Scatter(), Scatter()
    order = range(len(CHUNKS))
    cot_rows, cot_acts, kept = {}, {}, {}

    def advance(works=(), extra=(), **hops):
        tables = {"cot": cot, "ffn": ffn, "d": d_sum, "out": out_sum}
        sends = list(extra)
        spans = []
        for name, moves in hops.items():
            spans.append((tables[name], moves, len(sends)))
            sends += tables[name].sends(moves)
        got, made = stages.run(sends, works)
        for table, moves, low in spans:
            table.take(moves, got[low : low + len(moves)])
        return got[: len(extra)], made

    def cot_work(*chunks):
        made = [cot.chunk(i) for i in chunks]

        def work(picks_i, w_down_i, *args):
            blocks = []
            for i, (_, _, late), (values, crossing) in zip(chunks, made, args):
                blocks += Gather.complete(i, values, crossing, late)
            return cot_chunk(picks_i, w_down_i, blocks, slot_count)

        picks_i = picks[chunks[0]] if len(chunks) == 1 else jnp.concatenate([picks[i] for i in chunks], axis=0)
        return work, (picks_i, w_down) + tuple((values, crossing) for values, crossing, _ in made)

    def cot_done(chunks, made):
        for n, i in enumerate(chunks):
            cot_rows[i], cot_acts[i] = (made[0], n), (made[1], n)

    def main_work(i):
        values, crossing, late = ffn.chunk(i)

        def work(picks_i, gates_i, acts_i, gate_w, up_w, values, crossing):
            blocks = Gather.complete(i, values, crossing, late)
            return main_chunk(picks_i, gates_i, acts_i, cot_acts[i][1], gate_w, up_w, blocks, slot_count)

        gates_i = token_gates[STARTS[i] : STARTS[i] + len(CHUNKS[i])]
        return work, (picks[i], gates_i, cot_acts[i][0], w_gate, w_up, values, crossing)

    def out_work(*chunks):
        def work(picks_i, scaled_i, w_down_i):
            return out_chunk(picks_i, scaled_i, w_down_i, slot_count)

        return work, ([picks[i] for i in chunks], [kept[i][1] for i in chunks], w_down)

    (across, mate), ((cosine, sine), slot_of) = advance(
        [(turn_tables, (blocks_at,)), (to_groups, (slot_of,))],
        extra=[(attn_in, "y"), (attn_in, "c")],
        cot=[("z", (0, 0, 0)), ("x", (0, 0, 0))],
    )

    def project(block, mate, across, w_query, w_key, w_value):
        blocks = [block, mate, across, send(across, "c")]
        q_raw, k_raw, v_low, q_square, k_square = qkv(blocks, w_query, w_key, w_value)
        squares = token_sums(jnp.sum(q_square, axis=1), jnp.sum(k_square, axis=1))
        return blocks, q_raw, k_raw, v_low, squares

    _, (made,) = advance(
        [(project, (attn_in, mate, across, w_query, w_key, w_value))],
        cot=[("z", (1, 0, 0)), ("x", (1, 0, 0)), ("y", (0, 0, 0)), ("c", (0, 0, 0)), ("c", (1, 0, 0))],
    )
    seq_blocks, q_raw, k_raw, v_low, squares = made

    def columns_of(squares):
        scales = lax.rsqrt(squares / model_width + EPS)
        columns = jnp.stack([scales[0], scales[1], positions.astype(F32)], axis=1)
        return jnp.pad(columns, ((0, 0), (0, HDIM - columns.shape[1])))

    cols = columns_of(squares)
    _, (made,) = advance(
        [(attend_forward, (q_raw, k_raw, v_low, cols, q_gain, k_gain, cosine, sine, key_pos))],
        cot=[("z", (2, 0, 0)), ("x", (2, 0, 0)), ("y", (1, 0, 0)), ("c", (0, 1, 0)), ("c", (0, 0, 1))],
    )
    o_low, lse, q_rot, k_rot = made

    def project_back(o_low, w_out):
        parts = [
            jnp.dot(o_low[r * tok_rows : (r + 1) * tok_rows], w_out, preferred_element_type=F32).astype(BF16)
            for r in range(tensor_count)
        ]
        across = add_low(parts[2], send(parts[3], "c"))
        return add_wide(parts[0], send(parts[1], "c")) + send(across, "y").astype(F32)

    _, (attn_rows, picks) = advance(
        [(project_back, (o_low, w_out)), (all_picks, (slot_of,))],
        cot=[("x", (3, 0, 0)), ("c", (2, 0, 0)), ("c", (1, 1, 0))],
    )
    mixed = resid + attn_rows
    scale_two = rms_scale(mixed)
    mixed_norm = mixed * scale_two
    ffn_in = (mixed_norm * ffn_gain.astype(F32)).astype(BF16)
    ffn.held[0, 0, 0, 0] = ffn_in

    def route(ffn_in, w_router):
        logits = jnp.dot(ffn_in, w_router, preferred_element_type=F32)
        return jax.nn.softmax(logits, axis=-1)

    def join(*blocks):
        return jnp.concatenate(blocks, axis=0)

    _, (router_probs, made, gathered) = advance(
        [(route, (ffn_in, w_router)), cot_work(0), (join, tuple(seq_blocks))],
        ffn=[("z", (0, 0, 0)), ("x", (0, 0, 0)), ("y", (0, 0, 0))],
        cot=[("c", (1, 0, 1)), ("c", (2, 1, 0))],
    )
    cot_done((0,), made)
    _, (made, token_gates) = advance(
        [cot_work(1), (to_groups, (router_probs.T,))],
        ffn=[("z", (1, 0, 0)), ("x", (1, 0, 0)), ("y", (1, 0, 0))]
        + [("c", (0, 0, 0)), ("c", (0, 1, 0)), ("c", (1, 0, 0)), ("c", (0, 0, 1))],
    )
    cot_done((1,), made)
    _, (made,) = advance(
        [main_work(0)],
        ffn=[("z", (2, 0, 0)), ("x", (2, 0, 0)), ("c", (2, 0, 0))],
        cot=[("y", (2, 0, 0)), ("c", (3, 0, 0))],
    )
    kept[0], near, far = made[0], *made[1]
    _, (made,) = advance(
        [(core_sum, (near, far))],
        ffn=[("x", (3, 0, 0)), ("c", (1, 1, 0)), ("c", (1, 0, 1)), ("c", (2, 1, 0))],
        cot=[("y", (3, 0, 0))],
    )
    d_sum.put(0, made)
    _, (made,) = advance(
        [main_work(1)],
        ffn=[("y", (2, 0, 0))],
        cot=[("x", (0, 0, 1)), ("c", (3, 1, 0)), ("c", (2, 0, 1))],
    )
    kept[1], near, far = made[0], *made[1]
    _, (made, other) = advance(
        [(core_sum, (near, far)), cot_work(2)],
        ffn=[("y", (3, 0, 0)), ("c", (3, 0, 0)), ("c", (3, 1, 0))],
        cot=[("x", (1, 0, 1))],
    )
    d_sum.put(1, made)
    cot_done((2,), other)
    _, (made,) = advance(
        [main_work(2)],
        cot=[("x", (2, 0, 1)), ("y", (3, 1, 0)), ("c", (0, 1, 1)), ("c", (1, 1, 1))],
    )
    kept[2], near, far = made[0], *made[1]
    _, (made, other) = advance(
        [(core_sum, (near, far)), cot_work(3, 4)],
        ffn=[("x", (2, 0, 1)), ("y", (1, 1, 0))],
    )
    d_sum.put(2, made)
    cot_done((3, 4), other)
    _, (made,) = advance([main_work(3)], ffn=[("x", (3, 0, 1)), ("y", (0, 1, 0))])
    kept[3], near, far = made[0], *made[1]
    _, (made,) = advance([(core_sum, (near, far))], ffn=[("c", (0, 1, 1)), ("c", (3, 1, 1))])
    d_sum.put(3, made)

    _, (made,) = advance([main_work(4)], d=[("x", (1, 1, 1)), ("y", (2, 1, 1))])
    kept[4], near, far = made[0], *made[1]

    def return_probs(*d_probs):
        d_probs = jnp.concatenate(d_probs, axis=0)[position]
        arrived = lax.all_to_all(d_probs, BOTH, split_axis=0, concat_axis=0, tiled=True)
        arrived = arrived.reshape(group_count, tensor_count, experts, tok_rows)
        return jnp.sum(arrived, axis=1).reshape(expert_total, tok_rows).T

    outs = {}
    _, (made, outs[0], d_probs) = advance(
        [(core_sum, (near, far)), out_work(0), (return_probs, tuple(kept[i][4] for i in order))],
        d=[("x", (1, 1, 0)), ("y", (1, 0, 1))],
    )
    d_sum.put(4, made)
    _, (outs[1], made) = advance(
        [out_work(1), (core_sum, tuple(outs[0]))], d=[("x", (3, 1, 1)), ("y", (0, 1, 1))]
    )
    out_sum.put(0, made)
    _, (outs[2], made) = advance(
        [out_work(2), (core_sum, tuple(outs[1]))],
        d=[("x", (2, 1, 0)), ("y", (2, 0, 1)), ("z", (1, 0, 0))],
    )
    out_sum.put(1, made)
    _, (last_outs, made) = advance(
        [out_work(3, 4), (core_sum, tuple(outs[2]))],
        d=[("x", (3, 1, 0)), ("y", (3, 0, 1)), ("z", (2, 0, 0))],
    )
    out_sum.put(2, made)
    def saved(n):
        return [kept[i][n] for i in order]

    def grads_of(first, last, earlier=None):
        all_cots = [cot_rows[i][0] for i in order]

        places = [cot_rows[i][1] for i in order]

        def work(*args):
            return expert_grads(*args[:5], places, first, last, args[5] if len(args) > 5 else None)

        args = (saved(0), all_cots, saved(1), saved(2), saved(3))
        return work, args if earlier is None else args + (earlier,)

    thirds = [experts * n // 3 for n in range(4)]
    _, (made, weight_grads) = advance(
        [(core_sum, tuple(last_outs)), grads_of(thirds[0], thirds[1])],
        d=[("x", (0, 1, 0)), ("y", (0, 0, 1)), ("z", (3, 0, 0))],
    )
    out_sum.put(3, made[:2])
    out_sum.put(4, made[2:])
    d_ffn = d_sum.total()

    d_result = cotangent.astype(F32)
    d_logits = (
        router_probs * (d_probs - jnp.sum(router_probs * d_probs, axis=-1, keepdims=True))
    ).astype(BF16)
    router_part = contract_rows(d_logits, ffn_in)
    d_ffn = d_ffn + times_transpose(d_logits, w_router)
    ffn_gain_part = jnp.sum(d_ffn * mixed_norm, axis=0)
    d_norm_two = d_ffn * ffn_gain.astype(F32)
    d_mixed = d_result + scale_two * (
        d_norm_two - mixed_norm * jnp.mean(d_norm_two * mixed_norm, axis=-1, keepdims=True)
    )
    d_attn = d_mixed.astype(BF16)
    router_sums = jnp.concatenate(
        [router_part, jnp.broadcast_to(ffn_gain_part[None, :], (16, model_width))], axis=0
    ).astype(BF16)

    (across, mate, other), (weight_grads,) = advance(
        [grads_of(thirds[1], thirds[2], weight_grads)],
        extra=[(d_attn, "y"), (d_attn, "c"), (router_sums, "z1")],
        out=[("x", (1, 1, 1))],
    )
    router_sums = add_low(router_sums, other)

    def attend_back(d_attn, mate, across, w_out, o_low, *rest):
        d_blocks = [d_attn, mate, across, send(across, "c")]
        d_attended = join(*[times_transpose(block, w_out).astype(BF16) for block in d_blocks])
        q_raw, k_raw, v_low, q_rot, k_rot, lse, cols = rest
        *made, q_inner, k_inner = attend_backward(
            q_raw, k_raw, v_low, q_rot, k_rot, d_attended, lse, cols, q_gain, k_gain, cosine, sine, key_pos
        )
        inner = token_sums(jnp.sum(q_inner, axis=1), jnp.sum(k_inner, axis=1)) / model_width
        return made, inner, contract_rows(o_low, join(*d_blocks)).astype(BF16)

    _, (made,) = advance(
        [
            (
                attend_back,
                (d_attn, mate, across, w_out, o_low, q_raw, k_raw, v_low, q_rot, k_rot, lse, cols),
            )
        ],
        out=[("x", (3, 1, 1)), ("x", (1, 1, 0)), ("y", (2, 1, 1)), ("y", (1, 0, 1))],
    )
    (dq_hat, dk_hat, dv_raw, query_gain_part, key_gain_part), inner, grad_w_out = made

    def value_grad(gathered, dv_raw):
        return contract_rows(gathered, dv_raw).astype(BF16)

    def norm_back(q_raw, k_raw, cols, dq_hat, dk_hat, inner):
        raws = []
        for n, (raw, d_hat) in enumerate(((q_raw, dq_hat), (k_raw, dk_hat))):
            scale = cols[:, n : n + 1]
            raws.append((scale * (d_hat - raw * scale * inner[n][:, None])).astype(BF16))
        return raws

    out_weight = DpSum(grad_w_out)
    (other, *got), ((dq_raw, dk_raw), grad_value, (grad_w_gate, grad_w_up, grad_w_down)) = advance(
        [
            (norm_back, (q_raw, k_raw, cols, dq_hat, dk_hat, inner)),
            (value_grad, (gathered, dv_raw)),
            grads_of(thirds[2], thirds[3], weight_grads),
        ],
        extra=[(router_sums, "z2")] + out_weight.split_x(),
        out=[("x", (2, 1, 0)), ("y", (2, 0, 1)), ("z", (1, 0, 0))],
    )
    router_sums = add_low(router_sums, other)
    out_weight.add_x(got)
    value_weight = DpSum(grad_value)

    def projections_back(gathered, dq_raw, dk_raw, dv_raw, w_query, w_key, w_value):
        grads = [contract_rows(gathered, part).astype(BF16) for part in (dk_raw, dq_raw)]
        total_term = times_transpose(dq_raw, w_query)
        total_term = total_term + times_transpose(dk_raw, w_key)
        total_term = (total_term + times_transpose(dv_raw, w_value)).astype(BF16)
        return grads, total_term

    got, (((grad_key, grad_query), total_term), out_piece) = advance(
        [
            (projections_back, (gathered, dq_raw, dk_raw, dv_raw, w_query, w_key, w_value)),
            (out_weight.reduce_z, (out_weight.sum,)),
        ],
        extra=value_weight.split_x(),
        out=[("x", (3, 1, 0)), ("y", (3, 0, 1)), ("z", (2, 0, 0))],
    )
    value_weight.add_x(got)
    key_weight, query_weight = DpSum(grad_key), DpSum(grad_query)
    parts = jnp.split(total_term, tensor_count, axis=0)
    (d_other, other, *got), (value_piece,) = advance(
        [(value_weight.reduce_z, (value_weight.sum,))],
        extra=[(jnp.concatenate([parts[1], parts[3]], axis=0), "c"), (router_sums, "c")] + key_weight.split_x(),
        out=[("y", (0, 1, 1))],
    )
    router_sums = add_low(router_sums, other)
    key_weight.add_x(got)
    out_weight.part, value_weight.part = out_piece, value_piece
    (d_across, *got), _ = advance(
        extra=[(add_low(parts[2], d_other[tok_rows:]), "y")] + query_weight.split_x() + out_weight.join_z(),
    )
    query_weight.add_x(got[:1])
    out_weight.took_z(got[1:])
    d_attn_in = add_wide(parts[0], d_other[:tok_rows], d_across)
    attn_gain_part = jnp.sum(d_attn_in * normed, axis=0)
    d_norm_one = d_attn_in * attn_gain.astype(F32)
    d_input = d_mixed + scale_one * (
        d_norm_one - normed * jnp.mean(d_norm_one * normed, axis=-1, keepdims=True)
    )
    got, (d_input,) = advance(
        [(lambda value: value, (d_input.astype(BF16),))],
        extra=out_weight.join_x() + value_weight.join_z(),
        out=[("y", (0, 0, 1))],
    )
    out_weight.took_x(got[:1])
    value_weight.took_z(got[1:])
    (other, *got), (grad_w_out,) = advance(
        [(lambda value: value, (out_weight.result,))],
        extra=[(attn_gain_part, "c")] + value_weight.join_x() + key_weight.split_z(),
    )
    attn_gain_part = attn_gain_part + other
    value_weight.took_x(got[:1])
    key_weight.add_z(got[1:])
    (other, *got), (grad_value,) = advance(
        [(lambda value: value, (value_weight.result,))],
        extra=[(attn_gain_part, "y")] + query_weight.split_z(),
        out=[("x", (0, 1, 0))],
    )
    query_weight.add_z(got)
    gain_parts = jnp.concatenate([attn_gain_part + other, query_gain_part[0], key_gain_part[0]])
    (other, third, *got), _ = advance(
        extra=[(gain_parts, "x"), (router_sums, "y")] + key_weight.join_z(),
    )
    gain_parts = gain_parts + other
    router_sums = add_low(router_sums, third)
    key_weight.took_z(got)
    (other, *got), _ = advance(
        extra=[(router_sums, "x")] + key_weight.join_x() + query_weight.join_z(),
    )
    router_sums = add_wide(router_sums, other)
    key_weight.took_x(got[:1])
    query_weight.took_z(got[1:])
    (next_z, far_z, last_z, *got), (grad_key, router_sums) = advance(
        [(lambda value: value, (key_weight.result,)), (lambda value: value, (router_sums,))],
        extra=[(gain_parts, "u1"), (gain_parts, "u2"), (gain_parts, "u3")] + query_weight.join_x(),
        out=[("z", (3, 0, 0))],
    )
    gain_sums = (gain_parts + far_z) + (next_z + last_z)
    query_weight.took_x(got)
    grad_query = query_weight.result
    result = (mixed + out_sum.total()).astype(BF16)
    return (
        result,
        d_input,
        grad_query,
        grad_key,
        grad_value,
        gain_sums[model_width : model_width + local_width],
        gain_sums[model_width + local_width :],
        grad_w_out,
        gain_sums[:model_width],
        router_sums[expert_total],
        router_sums[:expert_total].T,
        grad_w_gate,
        grad_w_up,
        grad_w_down,
    )


def local_sent(
    hidden_in,
    cotangent,
    seq_lengths,
    expert_ids,
    attn_gain,
    w_query,
    w_key,
    w_value,
    query_gain,
    key_gain,
    w_out,
    ffn_gain,
    w_router,
    w_gate,
    w_up,
    w_down,
):
    tensor_count = lax.axis_size("tensor")
    group_count = lax.axis_size("dp")
    device_total = tensor_count * group_count
    tok_rows, model_width = hidden_in.shape
    topk_count = expert_ids.shape[1]
    local_experts = w_gate.shape[0]
    expert_total = w_router.shape[1]
    slot_count = tok_rows * topk_count // expert_total
    per_group = local_experts * slot_count
    seq_len = tok_rows * tensor_count
    local_width = w_query.shape[1]
    head_width = HDIM
    local_heads = local_width // head_width
    block_rows = min(512, seq_len)
    block_count = seq_len // block_rows
    score_scale = head_width ** (-0.5)
    live_length = seq_lengths[0]
    cosine, sine_table = (table[:, None, :] for table in rope_tables(seq_len, head_width))
    key_pos = jnp.arange(seq_len)
    key_live = key_pos < live_length

    def send_out(rows_low):
        grouped_rows = rows_low.reshape(group_count, 1, per_group, model_width)
        copies = jnp.broadcast_to(
            grouped_rows, (group_count, tensor_count, per_group, model_width)
        ).reshape(device_total, per_group, model_width)
        arrived = lax.all_to_all(copies, ("dp", "tensor"), split_axis=0, concat_axis=0, tiled=True)
        return arrived.reshape(device_total, local_experts, slot_count, model_width)

    def send_back(parts_low):
        returned = lax.all_to_all(
            parts_low.reshape(device_total, per_group, model_width),
            ("dp", "tensor"),
            split_axis=0,
            concat_axis=0,
            tiled=True,
        )
        return jnp.sum(
            returned.reshape(group_count, tensor_count, per_group, model_width).astype(F32),
            axis=1,
        ).reshape(-1, model_width)

    resid = hidden_in.astype(F32)
    scale_one = rms_scale(resid)
    normed = resid * scale_one
    attn_in = (normed * attn_gain.astype(F32)).astype(BF16)
    gathered = lax.all_gather(attn_in, "tensor", axis=0, tiled=True)
    q_raw = jnp.dot(gathered, w_query, preferred_element_type=F32)
    k_raw = jnp.dot(gathered, w_key, preferred_element_type=F32)
    v_raw = jnp.dot(gathered, w_value, preferred_element_type=F32)
    q_square, k_square = lax.psum(
        (jnp.sum(q_raw * q_raw, axis=1), jnp.sum(k_raw * k_raw, axis=1)), "tensor"
    )
    q_rscale = lax.rsqrt(q_square / model_width + EPS)[:, None]
    k_rscale = lax.rsqrt(k_square / model_width + EPS)[:, None]
    query_hat = q_raw * q_rscale
    key_hat = k_raw * k_rscale
    q_gain = query_gain.astype(F32)
    k_gain = key_gain.astype(F32)
    q_rot = rotate(
        (query_hat * q_gain).reshape(seq_len, local_heads, head_width), cosine, sine_table
    ).astype(BF16)
    k_rot = rotate(
        (key_hat * k_gain).reshape(seq_len, local_heads, head_width), cosine, sine_table
    ).astype(BF16)
    v_low = v_raw.astype(BF16).reshape(seq_len, local_heads, head_width)
    starts = jnp.arange(block_count) * block_rows
    q_blocks = q_rot.reshape(block_count, block_rows, local_heads, head_width)

    def allowed_mask(row_start):
        q_pos = row_start + jnp.arange(block_rows)
        return ((key_pos[None, :] <= q_pos[:, None]) & key_live[None, :])[None]

    def attend(inputs):
        q_block, row_start = inputs
        scores = (
            jnp.einsum("qhd,khd->hqk", q_block, k_rot, preferred_element_type=F32)
            * score_scale
        )
        scores = jnp.where(allowed_mask(row_start), scores, -1e30)
        row_max = jnp.max(scores, axis=-1, keepdims=True)
        exp_scores = jnp.exp(scores - row_max)
        row_total = jnp.sum(exp_scores, axis=-1, keepdims=True)
        soft_low = (exp_scores / row_total).astype(BF16)
        attended = jnp.einsum("hqk,khd->qhd", soft_low, v_low, preferred_element_type=F32)
        return (attended, (row_max + jnp.log(row_total))[..., 0])

    o_blocks, lse_blocks = lax.map(attend, (q_blocks, starts))
    o_low = o_blocks.reshape(seq_len, local_width).astype(BF16)
    attn_rows = lax.psum_scatter(
        jnp.dot(o_low, w_out, preferred_element_type=F32),
        "tensor",
        scatter_dimension=0,
        tiled=True,
    )
    mixed = resid + attn_rows
    scale_two = rms_scale(mixed)
    mixed_norm = mixed * scale_two
    ffn_in = (mixed_norm * ffn_gain.astype(F32)).astype(BF16)
    logits = jnp.dot(ffn_in, w_router, preferred_element_type=F32)
    router_probs = jax.nn.softmax(logits, axis=-1)
    expert_hot = (expert_ids[:, :, None] == jnp.arange(expert_total)[None, None, :]).astype(
        F32
    )
    gate_values = jnp.einsum("tke,te->tk", expert_hot, router_probs)
    flat_ids = expert_ids.reshape(-1)
    sort_order = jnp.argsort(flat_ids, stable=True)
    inverse = jnp.argsort(sort_order)
    expert_in = send_out(ffn_in[sort_order // topk_count])
    gate_pre = jnp.einsum("secd,edf->secf", expert_in, w_gate, preferred_element_type=F32)
    up_pre = jnp.einsum("secd,edf->secf", expert_in, w_up, preferred_element_type=F32)
    silu_gate = jax.nn.silu(gate_pre)
    acts = (silu_gate * up_pre).astype(BF16)
    partial_value = jnp.einsum(
        "secf,efd->secd", acts, w_down, preferred_element_type=F32
    ).astype(BF16)
    out_sorted = send_back(partial_value)
    out_assign = out_sorted[inverse].reshape(tok_rows, topk_count, model_width)
    expert_mix = jnp.einsum("tk,tkd->td", gate_values, out_assign)
    result = mixed + expert_mix
    d_result = cotangent.astype(F32)
    d_gates = jnp.einsum("tkd,td->tk", out_assign, d_result)
    d_out = (
        (gate_values[:, :, None] * d_result[:, None, :])
        .astype(BF16)
        .reshape(-1, model_width)[sort_order]
    )
    d_arrived = send_out(d_out)
    d_acts = jnp.einsum("secd,efd->secf", d_arrived, w_down, preferred_element_type=F32)
    sigmoid_gate = jax.nn.sigmoid(gate_pre)
    d_gate_pre = (d_acts * up_pre * sigmoid_gate * (1.0 + gate_pre * (1.0 - sigmoid_gate))).astype(
        BF16
    )
    d_up_pre = (d_acts * silu_gate).astype(BF16)
    grad_w_down = jnp.einsum("secf,secd->efd", acts, d_arrived, preferred_element_type=F32)
    grad_w_gate = jnp.einsum(
        "secd,secf->edf", expert_in, d_gate_pre, preferred_element_type=F32
    )
    grad_w_up = jnp.einsum(
        "secd,secf->edf", expert_in, d_up_pre, preferred_element_type=F32
    )
    d_rows = (
        jnp.einsum("secf,edf->secd", d_gate_pre, w_gate, preferred_element_type=F32)
        + jnp.einsum("secf,edf->secd", d_up_pre, w_up, preferred_element_type=F32)
    ).astype(BF16)
    d_sorted = send_back(d_rows)
    d_ffn = jnp.sum(d_sorted[inverse].reshape(tok_rows, topk_count, model_width), axis=1)
    d_probs = jnp.einsum("tk,tke->te", d_gates, expert_hot)
    d_logits = (
        router_probs * (d_probs - jnp.sum(router_probs * d_probs, axis=-1, keepdims=True))
    ).astype(BF16)
    router_part = contract_rows(ffn_in, d_logits)
    d_ffn = d_ffn + times_transpose(d_logits, w_router)
    ffn_gain_part = jnp.sum(d_ffn * mixed_norm, axis=0)
    d_norm_two = d_ffn * ffn_gain.astype(F32)
    d_mixed = d_result + scale_two * (
        d_norm_two - mixed_norm * jnp.mean(d_norm_two * mixed_norm, axis=-1, keepdims=True)
    )
    d_attn = d_mixed.astype(BF16)
    d_attn_all = lax.all_gather(d_attn, "tensor", axis=0, tiled=True)
    grad_w_out = contract_rows(o_low, d_attn_all)
    d_attended = (
        times_transpose(d_attn_all, w_out)
        .astype(BF16)
        .reshape(block_count, block_rows, local_heads, head_width)
    )

    def attend_back(carry, inputs):
        dk_total, dv_total = carry
        q_block, do_block, lse_block, row_start = inputs
        scores = (
            jnp.einsum("qhd,khd->hqk", q_block, k_rot, preferred_element_type=F32)
            * score_scale
        )
        allowed = allowed_mask(row_start)
        scores = jnp.where(allowed, scores, -1e30)
        soft = jnp.where(allowed, jnp.exp(scores - lse_block[..., None]), 0.0)
        d_weights = jnp.einsum("qhd,khd->hqk", do_block, v_low, preferred_element_type=F32)
        d_scores = (soft * (d_weights - jnp.sum(soft * d_weights, axis=-1, keepdims=True))).astype(
            BF16
        )
        dq_block = (
            jnp.einsum("hqk,khd->qhd", d_scores, k_rot, preferred_element_type=F32)
            * score_scale
        )
        dk_total = (
            dk_total
            + jnp.einsum("hqk,qhd->khd", d_scores, q_block, preferred_element_type=F32)
            * score_scale
        )
        dv_total = dv_total + jnp.einsum(
            "hqk,qhd->khd", soft.astype(BF16), do_block, preferred_element_type=F32
        )
        return ((dk_total, dv_total), dq_block)

    zero_field = jnp.zeros((seq_len, local_heads, head_width), F32)
    (dk_rot, dv_full), dq_blocks = lax.scan(
        attend_back, (zero_field, zero_field), (q_blocks, d_attended, lse_blocks, starts)
    )
    dq_gain = unrotate(
        dq_blocks.reshape(seq_len, local_heads, head_width), cosine, sine_table
    ).reshape(seq_len, local_width)
    dk_gain = unrotate(dk_rot, cosine, sine_table).reshape(seq_len, local_width)
    query_gain_part = jnp.sum(dq_gain * query_hat, axis=0)
    key_gain_part = jnp.sum(dk_gain * key_hat, axis=0)
    dq_hat = dq_gain * q_gain
    dk_hat = dk_gain * k_gain
    q_inner, k_inner = lax.psum(
        (jnp.sum(dq_hat * query_hat, axis=1), jnp.sum(dk_hat * key_hat, axis=1)), "tensor"
    )
    dq_raw = (q_rscale * (dq_hat - query_hat * (q_inner / model_width)[:, None])).astype(
        BF16
    )
    dk_raw = (k_rscale * (dk_hat - key_hat * (k_inner / model_width)[:, None])).astype(BF16)
    dv_raw = dv_full.reshape(seq_len, local_width).astype(BF16)
    grad_query = contract_rows(gathered, dq_raw)
    grad_key = contract_rows(gathered, dk_raw)
    grad_value = contract_rows(gathered, dv_raw)
    total_term = times_transpose(dq_raw, w_query)
    total_term = total_term + times_transpose(dk_raw, w_key)
    d_attn_in = lax.psum_scatter(
        (total_term + times_transpose(dv_raw, w_value)).astype(BF16),
        "tensor",
        scatter_dimension=0,
        tiled=True,
    ).astype(F32)
    attn_gain_part = jnp.sum(d_attn_in * normed, axis=0)
    d_norm_one = d_attn_in * attn_gain.astype(F32)
    d_input = d_mixed + scale_one * (
        d_norm_one - normed * jnp.mean(d_norm_one * normed, axis=-1, keepdims=True)
    )
    dp_sums = (
        lax.psum(grad_query.astype(BF16), "dp").astype(F32),
        lax.psum(grad_key.astype(BF16), "dp").astype(F32),
        lax.psum(grad_value.astype(BF16), "dp").astype(F32),
        lax.psum(query_gain_part.astype(BF16), "dp").astype(F32),
        lax.psum(key_gain_part.astype(BF16), "dp").astype(F32),
        lax.psum(grad_w_out.astype(BF16), "dp").astype(F32),
    )
    shared = lax.psum((attn_gain_part, ffn_gain_part, router_part), ("dp", "tensor"))
    return (
        result.astype(BF16),
        d_input.astype(BF16),
        dp_sums[0],
        dp_sums[1],
        dp_sums[2],
        dp_sums[3],
        dp_sums[4],
        dp_sums[5],
        shared[0],
        shared[1],
        shared[2],
        grad_w_gate,
        grad_w_up,
        grad_w_down,
    )


def solution(mesh):
    rows, columns = P(BOTH, None), P(None, "tensor")
    gathered_plan = (mesh.shape["dp"], mesh.shape["tensor"]) == (2 * RING, 4)
    return jax.shard_map(
        local_gathered if gathered_plan else local_sent,
        mesh=mesh,
        in_specs=(
            rows,
            rows,
            P("dp"),
            rows,
            P(),
            columns,
            columns,
            columns,
            P("tensor"),
            P("tensor"),
            P("tensor", None),
            P(),
            P(),
            P("dp", None, "tensor"),
            P("dp", None, "tensor"),
            P("dp", "tensor", None),
        ),
        out_specs=(
            rows,
            rows,
            columns,
            columns,
            columns,
            P("tensor"),
            P("tensor"),
            P("tensor", None),
            P(),
            P(),
            P(),
            P("dp", None, "tensor"),
            P("dp", None, "tensor"),
            P("dp", "tensor", None),
        ),
        check_vma=False,
    )
```

```python
import functools
import math

import jax
import jax.numpy as jnp
from jax import lax
from jax.experimental import pallas as pl
from jax.experimental.pallas import tpu as pltpu
from jax.sharding import PartitionSpec as P

HDIM = 128
EPS = 1e-05
ROPE_BASE = 10000.0
BOTH = ("dp", "tensor")
F32 = jnp.float32
BF16 = jnp.bfloat16
VMEM_GRANT = 60 << 20
fence = lax.optimization_barrier


def rms_scale(values):
    return lax.rsqrt(jnp.mean(values * values, axis=-1, keepdims=True) + EPS)


def rope_tables(count, head_width):
    half_width = head_width // 2
    frequency = jnp.exp(
        -(jnp.arange(half_width, dtype=F32) * 2.0 / head_width) * math.log(ROPE_BASE)
    )
    angles = jnp.arange(count, dtype=F32)[:, None] * frequency[None, :]
    return (jnp.cos(angles), jnp.sin(angles))


def rotate(values_in, cosine, sine_table):
    half_width = values_in.shape[-1] // 2
    front_half = values_in[..., :half_width]
    back_half = values_in[..., half_width:]
    return jnp.concatenate(
        [
            front_half * cosine - back_half * sine_table,
            back_half * cosine + front_half * sine_table,
        ],
        axis=-1,
    )


def unrotate(grads_in, cosine, sine_table):
    return rotate(grads_in, cosine, -sine_table)


def contract_rows(left, right):
    return lax.dot_general(left, right, (((0,), (0,)), ((), ())), preferred_element_type=F32)


def times_transpose(left, right):
    return lax.dot_general(left, right, (((1,), (1,)), ((), ())), preferred_element_type=F32)


def add_low(*terms):
    total = terms[0].astype(F32)
    for term in terms[1:]:
        total = total + term.astype(F32)
    return total.astype(BF16)


def add_wide(*terms):
    total = terms[0].astype(F32)
    for term in terms[1:]:
        total = total + term.astype(F32)
    return total


RING = 4
COLUMNS = (
    ((0, 0, 0), (1, 0, 0), (0, 1, 0), (0, 0, 1)),
    ((2, 0, 0), (1, 1, 0), (1, 0, 1), (2, 1, 0)),
    ((3, 0, 0), (3, 1, 0), (2, 0, 1), (3, 0, 1)),
    ((1, 1, 1), (2, 1, 1)),
    ((0, 1, 1), (3, 1, 1)),
)
CHUNKS = tuple(tuple(chip + (dc,) for dc in (0, 1) for chip in chips) for chips in COLUMNS)
STARTS = tuple(sum(len(chunk) for chunk in CHUNKS[:i]) for i in range(len(CHUNKS)))
PLACES = tuple(place for chunk in CHUNKS for place in chunk)
MOVES = {
    "x": lambda z, x, y, c: (z, x ^ 1, y, c),
    "y": lambda z, x, y, c: (z, x, y ^ 1, c),
    "c": lambda z, x, y, c: (z, x, y, c ^ 1),
    "z": lambda z, x, y, c: ((z - 1) % RING, x, y, c),
    "u1": lambda z, x, y, c: ((z + 1) % RING, x, y, c),
    "u2": lambda z, x, y, c: ((z + 2) % RING, x, y, c),
    "u3": lambda z, x, y, c: ((z + 3) % RING, x, y, c),
    "z1": lambda z, x, y, c: (z ^ 1, x, y, c),
    "z2": lambda z, x, y, c: (z ^ 2, x, y, c),
}


def device_pairs(move):
    pairs = []
    for z in range(RING):
        for x in range(2):
            for y in range(2):
                for c in range(2):
                    tz, tx, ty, tc = move(z, x, y, c)
                    pairs.append(((z * 2 + x) * 4 + y * 2 + c, (tz * 2 + tx) * 4 + ty * 2 + tc))
    return pairs


def send(value, axis):
    return lax.ppermute(value, BOTH, device_pairs(MOVES[axis]))


def small_sum(value, axes):
    for axis in axes:
        value = value + send(value, axis)
    return value


def hop(axis, k, dx, dy):
    return {"z": ((k + 1) % RING, dx, dy), "x": (k, dx ^ 1, dy), "y": (k, dx, dy ^ 1)}[axis]


class Stages:
    def __init__(self, token):
        self.token = token

    def run(self, sends, works=()):
        values, args, _ = fence(([s[0] for s in sends], [w[1] for w in works], self.token))
        got, crossed = [], []
        for value, (_, axis) in zip(values, sends):
            if axis == "c" and len(crossed) >= 2:
                value, _ = fence((value, crossed[-2]))
            got.append(send(value, axis))
            if axis == "c":
                crossed.append(got[-1])
        made = [work(*arg) for (work, _), arg in zip(works, args)]
        got, made = fence((got, made))
        self.token = jax.tree.leaves((got, made))[0]
        return got, made


class Gather:
    def __init__(self, block):
        self.held = {(0, 0, 0, 0): block}

    def sends(self, hops):
        return [(self.held[chip + (0,)], axis) for axis, chip in hops]

    def take(self, hops, got):
        for (axis, chip), value in zip(hops, got):
            self.held[chip + (1,) if axis == "c" else hop(axis, *chip) + (0,)] = value

    def chunk(self, i):
        chunk = CHUNKS[i]
        late = [place for place in chunk if place not in self.held]
        values = [self.held[place] for place in chunk if place in self.held]
        return values, [self.held[place[:3] + (0,)] for place in late], late

    @staticmethod
    def complete(i, values, crossing, late):
        blocks = dict(zip([place for place in CHUNKS[i] if place not in late], values))
        done = []
        for place, value in zip(late, crossing):
            if len(done) >= 2:
                value, _ = fence((value, done[-2]))
            done.append(send(value, "c"))
            blocks[place] = done[-1]
        return [blocks[place] for place in CHUNKS[i]]


class Scatter:
    def __init__(self):
        self.held = {}

    def put(self, i, sums):
        for chip, value in zip(COLUMNS[i], sums):
            self.held.setdefault(chip, []).append(value)

    def sends(self, hops):
        groups = [self.held[chip] for _, chip in hops]
        added = [group for group in groups if len(group) > 1]
        sums = iter(block_sums(added) if added else ())
        return [(next(sums) if len(group) > 1 else group[0], axis) for group, (axis, _) in zip(groups, hops)]

    def take(self, hops, got):
        for (axis, chip), value in zip(hops, got):
            self.held.setdefault(hop(axis, *chip), []).append(value)

    def total(self):
        return add_wide(*self.held[0, 0, 0])


class DpSum:
    def __init__(self, value):
        group = lax.axis_index("dp")
        self.z, self.x = group // 2, group % 2
        self.value = value
        self.half, self.piece = value.shape[0] // 2, value.shape[0] // (2 * RING)

    def split_x(self):
        return [(lax.dynamic_slice_in_dim(self.value, (1 - self.x) * self.half, self.half), "x")]

    def add_x(self, got):
        self.sum = add_low(lax.dynamic_slice_in_dim(self.value, self.x * self.half, self.half), got[0])

    def split_z(self):
        return [
            (lax.dynamic_slice_in_dim(self.sum, ((self.z + d) % RING) * self.piece, self.piece), f"u{d}")
            for d in (1, 2, 3)
        ]

    def add_z(self, got):
        self.part = add_low(lax.dynamic_slice_in_dim(self.sum, self.z * self.piece, self.piece), *got)

    def reduce_z(self, half):
        low, high = self.z % 2, self.z // 2
        pieces = half.reshape((2, 2, self.piece) + half.shape[1:])
        for bit, axis, name in ((low, 1, "z1"), (high, 0, "z2")):
            mine = lax.dynamic_index_in_dim(pieces, bit, axis, keepdims=False)
            other = lax.dynamic_index_in_dim(pieces, 1 - bit, axis, keepdims=False)
            pieces = add_low(mine, send(other, name))
        return pieces

    def collect_z(self, part):
        low, high = self.z % 2, self.z // 2
        for bit, axis, name in ((high, 0, "z2"), (low, 1, "z1")):
            other = send(part, name)
            first, second = jnp.where(bit == 0, part, other), jnp.where(bit == 0, other, part)
            part = jnp.stack([first, second], axis=axis)
        return part.reshape((self.half,) + part.shape[3:])

    def join_z(self):
        return [(self.part, f"u{d}") for d in (1, 2, 3)]

    def took_z(self, got):
        stack = jnp.stack([self.part] + list(got))
        order = (self.z - jnp.arange(RING)) % RING
        self.whole_half = stack[order].reshape(self.half, -1)

    def join_x(self):
        return [(self.whole_half, "x")]

    def took_x(self, got):
        mine, other = self.whole_half, got[0]
        first = jnp.where(self.x == 0, mine, other)
        second = jnp.where(self.x == 0, other, mine)
        self.result = jnp.concatenate([first, second], axis=0).astype(F32)


def core_sum(near, far):
    return pair_sum(near, send(far, "c"))


def place_indices():
    group, member = lax.axis_index("dp"), lax.axis_index("tensor")
    z, x, y, c = group // 2, group % 2, member // 2, member % 2
    absolute = jnp.stack(
        [(((z + k) % RING) * 2 + (x ^ dx)) * 4 + (y ^ dy) * 2 + (c ^ dc) for k, dx, dy, dc in PLACES]
    )
    table = [0] * len(PLACES)
    for position, (k, dx, dy, dc) in enumerate(PLACES):
        table[((k * 2 + dx) * 2 + dy) * 2 + dc] = position
    numbers = jnp.arange(len(PLACES))
    other_z, other_x = numbers // 8, (numbers // 4) % 2
    other_y, other_c = (numbers // 2) % 2, numbers % 2
    offset = ((((other_z - z) % RING) * 2 + (other_x ^ x)) * 2 + (other_y ^ y)) * 2 + (other_c ^ c)
    return absolute, jnp.asarray(table, jnp.int32)[offset]


def nn(left, right):
    return lax.dot_general(left, right, (((1,), (0,)), ((), ())), preferred_element_type=F32)


def nt(left, right):
    return lax.dot_general(left, right, (((1,), (1,)), ((), ())), preferred_element_type=F32)


def pick_rows(picks_ref, blocks, rows_ref, slot_count, width):
    experts = rows_ref.shape[0]
    for b, block in enumerate(blocks):
        for low in range(0, block.shape[1], width):
            columns = pl.ds(low, width)
            picked = nn(picks_ref[b], block[:, columns]).astype(BF16)
            for e in range(experts):
                rows_ref[e, pl.ds(b * slot_count, slot_count), columns] = picked[
                    e * slot_count : (e + 1) * slot_count
                ]


def give_rows(picks_ref, rows_ref, blocks, slot_count, width, first=0):
    experts = rows_ref.shape[0]
    for b, block in enumerate(blocks):
        for low in range(0, block.shape[1], width):
            columns = pl.ds(low, width)
            slots = jnp.concatenate(
                [rows_ref[e, pl.ds(first + b * slot_count, slot_count), columns] for e in range(experts)],
                axis=0,
            )
            block[:, columns] = contract_rows(picks_ref[b], slots).astype(BF16)


def cot_kernel(count, slot_count, picks_ref, down_ref, *refs):
    blocks, (rows_out, acts_out, rows_ref) = refs[:count], refs[count:]
    e = pl.program_id(0)

    @pl.when(e == 0)
    def _():
        pick_rows(picks_ref, blocks, rows_ref, slot_count, 512)

    rows = rows_ref[e]
    rows_out[0] = rows
    acts_out[0] = nt(rows, down_ref[0])


def main_kernel(count, slot_count, picks_ref, gates_ref, acts_ref, gate_ref, up_ref, *refs):
    blocks = refs[:count]
    rows_out, scaled_out, d_gate_out, d_up_out, d_probs_out = refs[count : count + 5]
    near_out, far_out, rows_ref = refs[count + 5 :]
    results = [out.at[b] for out in (near_out, far_out) for b in range(count // 2)]
    e = pl.program_id(0)

    @pl.when(e == 0)
    def _():
        pick_rows(picks_ref, blocks, rows_ref, slot_count, 512)

    rows = rows_ref[e]
    rows_out[0] = rows
    pre, up = nn(rows, gate_ref[0]), nn(rows, up_ref[0])
    cot_acts = acts_ref[0]
    own_slots = pl.ds(pl.multiple_of(e * slot_count, slot_count), slot_count)
    own_picks = [picks_ref[b, own_slots, :].astype(F32) for b in range(count)]
    gate = jnp.concatenate(
        [
            jnp.sum(pick * gates_ref[b, pl.ds(e, 1), :], axis=1, keepdims=True)
            for b, pick in enumerate(own_picks)
        ],
        axis=0,
    )
    sig = jax.nn.sigmoid(pre)
    silu = pre * sig
    acts = silu * up
    scaled_out[0] = (gate * acts).astype(BF16)
    inner = jnp.sum(acts.astype(BF16).astype(F32) * cot_acts, axis=1, keepdims=True)
    for b, pick in enumerate(own_picks):
        here = inner[b * slot_count : (b + 1) * slot_count]
        d_probs_out[b, pl.ds(e, 1), :] = jnp.sum(pick * here, axis=0, keepdims=True)
    d_acts = gate * cot_acts
    d_pre = (d_acts * up * sig * (1.0 + pre * (1.0 - sig))).astype(BF16)
    d_up = (d_acts * silu).astype(BF16)
    d_gate_out[0] = d_pre
    d_up_out[0] = d_up
    rows_ref[e] = (nt(d_pre, gate_ref[0]) + nt(d_up, up_ref[0])).astype(BF16)

    @pl.when(e == pl.num_programs(0) - 1)
    def _():
        give_rows(picks_ref, rows_ref, results, slot_count, 512)


def out_kernel(parts, slot_count, *refs):
    picks, scaled, down_ref = refs[:parts], refs[parts : 2 * parts], refs[2 * parts]
    near_out, far_out, rows_ref = refs[2 * parts + 1 :]
    e = pl.program_id(0)
    rows = scaled[0][0] if parts == 1 else jnp.concatenate([part[0] for part in scaled], axis=0)
    rows_ref[e] = nn(rows, down_ref[0]).astype(BF16)

    @pl.when(e == pl.num_programs(0) - 1)
    def _():
        low, done = 0, 0
        for part in picks:
            count = part.shape[0]
            half = count // 2
            results = [out.at[done + b] for out in (near_out, far_out) for b in range(half)]
            give_rows(part, rows_ref, results, slot_count, 512, low)
            low, done = low + count * slot_count, done + half


def per_expert(*shape):
    return pl.BlockSpec((1,) + shape, lambda e: (e,) + (0,) * len(shape))


def resident(*shape):
    return pl.BlockSpec(shape, lambda e: (0,) * len(shape), pipeline_mode=pl.Buffered(1))


def cot_chunk(picks, w_down, blocks, slot_count):
    experts, hidden, width = w_down.shape
    count, tokens = len(blocks), blocks[0].shape[0]
    rows = count * slot_count
    return pl.pallas_call(
        functools.partial(cot_kernel, count, slot_count),
        grid=(experts,),
        in_specs=[resident(*picks.shape), per_expert(hidden, width)] + [resident(tokens, width)] * count,
        out_specs=[per_expert(rows, width), per_expert(rows, hidden)],
        out_shape=[
            jax.ShapeDtypeStruct((experts, rows, width), BF16),
            jax.ShapeDtypeStruct((experts, rows, hidden), F32),
        ],
        scratch_shapes=[pltpu.VMEM((experts, rows, width), BF16)],
        compiler_params=pltpu.CompilerParams(vmem_limit_bytes=VMEM_GRANT),
        cost_estimate=pl.CostEstimate(
            flops=2 * experts * rows * width * (hidden + tokens),
            bytes_accessed=2 * (count * tokens * width + experts * (rows + hidden) * width),
            transcendentals=0,
        ),
    )(picks, w_down, *blocks)


def main_chunk(picks, gates, cot_acts, acts_at, w_gate, w_up, blocks, slot_count):
    experts, width, hidden = w_gate.shape
    count, tokens = len(blocks), blocks[0].shape[0]
    rows = count * slot_count
    outs = pl.pallas_call(
        functools.partial(main_kernel, count, slot_count),
        grid=(experts,),
        in_specs=[
            resident(*picks.shape),
            resident(*gates.shape),
            pl.BlockSpec((1, rows, hidden), lambda e: (e, acts_at, 0)),
            per_expert(width, hidden),
            per_expert(width, hidden),
        ]
        + [resident(tokens, width)] * count,
        out_specs=[
            per_expert(rows, width),
            per_expert(rows, hidden),
            per_expert(rows, hidden),
            per_expert(rows, hidden),
            resident(*gates.shape),
        ]
        + [resident(count // 2, tokens, width)] * 2,
        out_shape=[
            jax.ShapeDtypeStruct((experts, rows, width), BF16),
            jax.ShapeDtypeStruct((experts, rows, hidden), BF16),
            jax.ShapeDtypeStruct((experts, rows, hidden), BF16),
            jax.ShapeDtypeStruct((experts, rows, hidden), BF16),
            jax.ShapeDtypeStruct(gates.shape, F32),
        ]
        + [jax.ShapeDtypeStruct((count // 2, tokens, width), BF16)] * 2,
        scratch_shapes=[pltpu.VMEM((experts, rows, width), BF16)],
        compiler_params=pltpu.CompilerParams(vmem_limit_bytes=VMEM_GRANT),
        cost_estimate=pl.CostEstimate(
            flops=2 * experts * rows * width * (4 * hidden + 2 * tokens),
            bytes_accessed=2 * (2 * count * tokens * width + experts * (rows + 2 * hidden) * width),
            transcendentals=experts * rows * hidden,
        ),
    )(picks, gates, cot_acts, w_gate, w_up, *blocks)
    return outs[:5], outs[5:]


def out_chunk(picks, scaled, w_down, slot_count):
    experts, hidden, width = w_down.shape
    tokens = picks[0].shape[2]
    count = sum(part.shape[0] for part in picks)
    rows = count * slot_count
    return pl.pallas_call(
        functools.partial(out_kernel, len(picks), slot_count),
        grid=(experts,),
        in_specs=[resident(*part.shape) for part in picks]
        + [per_expert(*part.shape[1:]) for part in scaled]
        + [per_expert(hidden, width)],
        out_specs=[resident(count // 2, tokens, width)] * 2,
        out_shape=[jax.ShapeDtypeStruct((count // 2, tokens, width), BF16)] * 2,
        scratch_shapes=[pltpu.VMEM((experts, rows, width), BF16)],
        compiler_params=pltpu.CompilerParams(vmem_limit_bytes=VMEM_GRANT),
        cost_estimate=pl.CostEstimate(
            flops=2 * experts * rows * width * (hidden + tokens),
            bytes_accessed=2 * (count * tokens * width + experts * (rows + hidden) * width),
            transcendentals=0,
        ),
    )(*picks, *scaled, w_down)


def grad_kernel(count, *refs):
    rows, cots, scaled, d_gate, d_up = (refs[i * count : (i + 1) * count] for i in range(5))
    gate_out, up_out, down_out = refs[-3:]

    def total(lefts, rights):
        value = None
        for left, right in zip(lefts, rights):
            term = contract_rows(left[0], right[0])
            value = term if value is None else value + term
        return value

    gate_out[0] = total(rows, d_gate)
    up_out[0] = total(rows, d_up)
    down_out[0] = total(scaled, cots)


def expert_grads(rows, cots, scaled, d_gate, d_up, cots_at, first, last, earlier=None, tile=512):
    count, experts, width = len(rows), rows[0].shape[0], rows[0].shape[2]
    hidden = scaled[0].shape[2]
    slots = sum(part.shape[1] for part in rows)
    wide = [pl.BlockSpec((1, part.shape[1], tile), lambda e, n: (first + e, 0, n)) for part in rows]
    wide_cots = [
        pl.BlockSpec((1, part.shape[1], tile), lambda e, n, at=at: (first + e, at, n))
        for part, at in zip(rows, cots_at)
    ]
    narrow = [pl.BlockSpec((1, part.shape[1], hidden), lambda e, n: (first + e, 0, 0)) for part in rows]
    tall = pl.BlockSpec((1, tile, hidden), lambda e, n: (first + e, n, 0))
    given = [] if earlier is None else list(earlier)
    return pl.pallas_call(
        functools.partial(grad_kernel, count),
        grid=(last - first, width // tile),
        in_specs=wide + wide_cots + narrow * 3 + [pl.BlockSpec(memory_space=pl.ANY)] * len(given),
        out_specs=[tall, tall, pl.BlockSpec((1, hidden, tile), lambda e, n: (first + e, 0, n))],
        out_shape=[
            jax.ShapeDtypeStruct((experts, width, hidden), F32),
            jax.ShapeDtypeStruct((experts, width, hidden), F32),
            jax.ShapeDtypeStruct((experts, hidden, width), F32),
        ],
        input_output_aliases={5 * count + i: i for i in range(len(given))},
        compiler_params=pltpu.CompilerParams(vmem_limit_bytes=VMEM_GRANT),
        cost_estimate=pl.CostEstimate(
            flops=6 * (last - first) * slots * width * hidden,
            bytes_accessed=(last - first) * (4 * slots * width + 12 * width * hidden),
            transcendentals=0,
        ),
    )(*rows, *cots, *scaled, *d_gate, *d_up, *given)


def sums_kernel(counts, *refs):
    terms, outs = refs[: sum(counts)], refs[sum(counts) :]
    for count, out in zip(counts, outs):
        value = terms[0][...].astype(F32)
        for term in terms[1:count]:
            value = value + term[...].astype(F32)
        out[...] = value.astype(BF16)
        terms = terms[count:]


def block_sums(groups, tile=64):
    rows, width = groups[0][0].shape
    counts = [len(group) for group in groups]
    block = pl.BlockSpec((tile, width), lambda i: (i, 0))
    return pl.pallas_call(
        functools.partial(sums_kernel, counts),
        grid=(rows // tile,),
        in_specs=[block] * sum(counts),
        out_specs=[block] * len(groups),
        out_shape=[jax.ShapeDtypeStruct((rows, width), BF16)] * len(groups),
        compiler_params=pltpu.CompilerParams(vmem_limit_bytes=VMEM_GRANT),
        cost_estimate=pl.CostEstimate(
            flops=sum(counts) * rows * width,
            bytes_accessed=2 * (sum(counts) + len(groups)) * rows * width,
            transcendentals=0,
        ),
    )(*[term for group in groups for term in group])


def qkv_kernel(*refs):
    blocks, (q_w, k_w, v_w, q_out, k_out, v_out, q_sq, k_sq) = refs[:-8], refs[-8:]
    lanes = q_sq.shape[1]
    rows = blocks[0].shape[0]
    for b, block in enumerate(blocks):
        here = pl.ds(b * rows, rows)
        for weight, out, squares in ((q_w, q_out, q_sq), (k_w, k_out, k_sq)):
            value = nn(block[...], weight[...])
            out[here, :] = value
            value = value * value
            total = value[:, :lanes]
            for low in range(lanes, value.shape[1], lanes):
                total = total + value[:, low : low + lanes]

            @pl.when(pl.program_id(0) == 0)
            def _(squares=squares, total=total):
                squares[here, :] = total

            @pl.when(pl.program_id(0) > 0)
            def _(squares=squares, total=total):
                squares[here, :] += total

        v_out[here, :] = nn(block[...], v_w[...]).astype(BF16)


def qkv(blocks, w_query, w_key, w_value, tile=256):
    rows, depth = blocks[0].shape
    width = w_query.shape[1]
    count = len(blocks) * rows
    weight = pl.BlockSpec((depth, tile), lambda n: (0, n))
    out = pl.BlockSpec((count, tile), lambda n: (0, n))
    return pl.pallas_call(
        qkv_kernel,
        grid=(width // tile,),
        in_specs=[resident(rows, depth)] * len(blocks) + [weight] * 3,
        out_specs=[out] * 3 + [resident(count, HDIM)] * 2,
        out_shape=[
            jax.ShapeDtypeStruct((count, width), F32),
            jax.ShapeDtypeStruct((count, width), F32),
            jax.ShapeDtypeStruct((count, width), BF16),
            jax.ShapeDtypeStruct((count, HDIM), F32),
            jax.ShapeDtypeStruct((count, HDIM), F32),
        ],
        compiler_params=pltpu.CompilerParams(vmem_limit_bytes=VMEM_GRANT),
        cost_estimate=pl.CostEstimate(
            flops=6 * count * depth * width,
            bytes_accessed=2 * count * depth + 6 * depth * width + 10 * count * width,
            transcendentals=0,
        ),
    )(*blocks, w_query, w_key, w_value)


def pair_kernel(near_ref, far_ref, *outs):
    for b, out in enumerate(outs):
        out[...] = (near_ref[b].astype(F32) + far_ref[b].astype(F32)).astype(BF16)


def pair_sum(near, far, tile=64):
    count, rows, width = near.shape
    stack = pl.BlockSpec((count, tile, width), lambda i: (0, i, 0))
    return pl.pallas_call(
        pair_kernel,
        grid=(rows // tile,),
        in_specs=[stack, stack],
        out_specs=[pl.BlockSpec((tile, width), lambda i: (i, 0))] * count,
        out_shape=[jax.ShapeDtypeStruct((rows, width), BF16)] * count,
        compiler_params=pltpu.CompilerParams(vmem_limit_bytes=VMEM_GRANT),
        cost_estimate=pl.CostEstimate(
            flops=count * rows * width, bytes_accessed=6 * count * rows * width, transcendentals=0
        ),
    )(near, far)


def turn(values, cosine, sine):
    return values * cosine + pltpu.roll(values, values.shape[1] // 2, 1) * sine


def attend_kernel(
    row_block, scale, q_ref, k_ref, v_ref, cols_ref, qg_ref, kg_ref, cos_ref, sin_ref, kpos_ref,
    out_ref, lse_ref, qrot_ref, krot_ref,
):
    cosine, sine = cos_ref[...], sin_ref[...]
    qrot_ref[...] = turn(q_ref[...] * cols_ref[:, 0:1] * qg_ref[...], cosine, sine).astype(BF16)
    krot_ref[...] = turn(k_ref[...] * cols_ref[:, 1:2] * kg_ref[...], cosine, sine).astype(BF16)
    for low in range(0, q_ref.shape[0], row_block):
        rows = pl.ds(low, row_block)
        scores = nt(qrot_ref[rows, :], krot_ref[...]) * scale
        scores = jnp.where(kpos_ref[...] <= cols_ref[rows, 2:3], scores, -1e30)
        top = jnp.max(scores, axis=1, keepdims=True)
        powers = jnp.exp(scores - top)
        total = jnp.sum(powers, axis=1, keepdims=True)
        soft = (powers * (1.0 / total)).astype(BF16)
        out_ref[rows, :] = nn(soft, v_ref[...]).astype(BF16)
        lse_ref[rows, :] = jnp.broadcast_to(top + jnp.log(total), (row_block, HDIM))


def attend_back_kernel(
    row_block, scale, q_ref, k_ref, v_ref, qrot_ref, krot_ref, do_ref, lse_ref, cols_ref, qg_ref, kg_ref,
    cos_ref, sin_ref, kpos_ref,
    dq_ref, dk_ref, dv_ref, qgain_ref, kgain_ref, qin_ref, kin_ref, dq_acc, dk_acc, dv_acc,
):
    for low in range(0, q_ref.shape[0], row_block):
        rows = pl.ds(low, row_block)
        query, d_out = qrot_ref[rows, :], do_ref[rows, :]
        scores = nt(query, krot_ref[...]) * scale
        soft = jnp.where(kpos_ref[...] <= cols_ref[rows, 2:3], jnp.exp(scores - lse_ref[rows, 0:1]), 0.0)
        d_weights = nt(d_out, v_ref[...])
        spread = soft * d_weights
        mean = jnp.sum(spread, axis=1, keepdims=True)
        d_scores = (spread - soft * mean).astype(BF16)
        dq_acc[rows, :] = nn(d_scores, krot_ref[...]) * scale
        d_keys = contract_rows(d_scores, query)
        d_values = contract_rows(soft.astype(BF16), d_out)
        if low:
            dk_acc[...] += d_keys
            dv_acc[...] += d_values
        else:
            dk_acc[...] = d_keys
            dv_acc[...] = d_values
    dv_ref[...] = dv_acc[...].astype(BF16)
    cosine, sine = cos_ref[...], -sin_ref[...]
    for lane, raw_ref, gain_ref, grad, hat_ref, gain_out, inner_out in (
        (0, q_ref, qg_ref, dq_acc[...], dq_ref, qgain_ref, qin_ref),
        (1, k_ref, kg_ref, dk_acc[...] * scale, dk_ref, kgain_ref, kin_ref),
    ):
        hat = raw_ref[...] * cols_ref[:, lane : lane + 1]
        turned = turn(grad, cosine, sine)
        gain_out[...] = jnp.sum(turned * hat, axis=0, keepdims=True)
        d_hat = turned * gain_ref[...]
        hat_ref[...] = d_hat
        inner = d_hat * hat

        @pl.when(pl.program_id(0) == 0)
        def _(inner=inner, inner_out=inner_out):
            inner_out[...] = inner

        @pl.when(pl.program_id(0) > 0)
        def _(inner=inner, inner_out=inner_out):
            inner_out[...] += inner


def head_columns(rows):
    return pl.BlockSpec((rows, HDIM), lambda h: (0, h))


def whole(*shape):
    return pl.BlockSpec(shape, lambda h: (0,) * len(shape))


def attend_forward(q_raw, k_raw, v_low, cols, q_gain, k_gain, cosine, sine, kpos):
    seq_len, width = q_raw.shape
    heads = width // HDIM
    part, one = head_columns(seq_len), head_columns(1)
    return pl.pallas_call(
        functools.partial(attend_kernel, min(256, seq_len), HDIM ** (-0.5)),
        grid=(heads,),
        in_specs=[part, part, part, whole(seq_len, HDIM), one, one]
        + [whole(seq_len, HDIM), whole(seq_len, HDIM), whole(1, seq_len)],
        out_specs=[part, part, part, part],
        out_shape=[
            jax.ShapeDtypeStruct((seq_len, width), BF16),
            jax.ShapeDtypeStruct((seq_len, width), F32),
            jax.ShapeDtypeStruct((seq_len, width), BF16),
            jax.ShapeDtypeStruct((seq_len, width), BF16),
        ],
        compiler_params=pltpu.CompilerParams(vmem_limit_bytes=VMEM_GRANT),
        cost_estimate=pl.CostEstimate(
            flops=4 * seq_len * seq_len * width,
            bytes_accessed=20 * seq_len * width,
            transcendentals=heads * seq_len * seq_len,
        ),
    )(q_raw, k_raw, v_low, cols, q_gain, k_gain, cosine, sine, kpos)


def attend_backward(
    q_raw, k_raw, v_low, q_rot, k_rot, d_out, lse, cols, q_gain, k_gain, cosine, sine, kpos
):
    seq_len, width = q_raw.shape
    heads = width // HDIM
    part, one = head_columns(seq_len), head_columns(1)
    return pl.pallas_call(
        functools.partial(attend_back_kernel, min(256, seq_len), HDIM ** (-0.5)),
        grid=(heads,),
        in_specs=[part, part, part, part, part, part, part, whole(seq_len, HDIM), one, one]
        + [whole(seq_len, HDIM), whole(seq_len, HDIM), whole(1, seq_len)],
        out_specs=[part, part, part, one, one, whole(seq_len, HDIM), whole(seq_len, HDIM)],
        out_shape=[
            jax.ShapeDtypeStruct((seq_len, width), F32),
            jax.ShapeDtypeStruct((seq_len, width), F32),
            jax.ShapeDtypeStruct((seq_len, width), BF16),
            jax.ShapeDtypeStruct((1, width), F32),
            jax.ShapeDtypeStruct((1, width), F32),
            jax.ShapeDtypeStruct((seq_len, HDIM), F32),
            jax.ShapeDtypeStruct((seq_len, HDIM), F32),
        ],
        scratch_shapes=[pltpu.VMEM((seq_len, HDIM), F32)] * 3,
        compiler_params=pltpu.CompilerParams(vmem_limit_bytes=VMEM_GRANT),
        cost_estimate=pl.CostEstimate(
            flops=10 * seq_len * seq_len * width,
            bytes_accessed=32 * seq_len * width,
            transcendentals=heads * seq_len * seq_len,
        ),
    )(q_raw, k_raw, v_low, q_rot, k_rot, d_out, lse, cols, q_gain, k_gain, cosine, sine, kpos)


def local_gathered(
    hidden_in,
    cotangent,
    seq_lengths,
    expert_ids,
    attn_gain,
    w_query,
    w_key,
    w_value,
    query_gain,
    key_gain,
    w_out,
    ffn_gain,
    w_router,
    w_gate,
    w_up,
    w_down,
):
    tensor_count = lax.axis_size("tensor")
    group_count = lax.axis_size("dp")
    tok_rows, model_width = hidden_in.shape
    topk = expert_ids.shape[1]
    expert_total = w_router.shape[1]
    experts = w_gate.shape[0]
    slot_count = tok_rows * topk // expert_total
    devices = len(PLACES)
    seq_len = tok_rows * tensor_count
    local_width = w_query.shape[1]
    half_width = HDIM // 2
    live_length = seq_lengths[0]
    absolute, position = place_indices()

    member = lax.axis_index("tensor")
    blocks_at = member ^ jnp.arange(tensor_count)

    def turn_tables(blocks_at):
        cosine, sine = (
            table.reshape(tensor_count, tok_rows, half_width)[blocks_at].reshape(seq_len, half_width)
            for table in rope_tables(seq_len, HDIM)
        )
        return jnp.concatenate([cosine, cosine], axis=1), jnp.concatenate([-sine, sine], axis=1)

    positions = (blocks_at[:, None] * tok_rows + jnp.arange(tok_rows)[None, :]).reshape(-1)
    never = 2 * seq_len
    key_pos = jnp.where(positions < live_length, positions, never).astype(F32)[None, :]

    def token_sums(*values):
        stacked = jnp.stack([value.reshape(tensor_count, tok_rows) for value in values])
        summed = lax.psum(stacked[:, blocks_at], "tensor")
        return summed[:, blocks_at].reshape(len(values), seq_len)

    def to_groups(by_expert):
        copies = jnp.broadcast_to(
            by_expert.reshape(group_count, 1, experts, tok_rows),
            (group_count, tensor_count, experts, tok_rows),
        ).reshape(devices, experts, tok_rows)
        return lax.all_to_all(copies, BOTH, split_axis=0, concat_axis=0, tiled=True)[absolute]

    resid = hidden_in.astype(F32)
    scale_one = rms_scale(resid)
    normed = resid * scale_one
    attn_in = (normed * attn_gain.astype(F32)).astype(BF16)
    q_gain = query_gain.astype(F32)[None, :]
    k_gain = key_gain.astype(F32)[None, :]

    hot = jnp.any(expert_ids.T[None, :, :] == jnp.arange(expert_total)[:, None, None], axis=1)
    earlier = jnp.triu(jnp.ones((tok_rows, tok_rows), F32), 1).astype(BF16)
    rank = jnp.dot(hot.astype(BF16), earlier, preferred_element_type=F32)
    slot_of = jnp.where(hot, rank, -1.0)

    def all_picks(slot_of):
        slots = jnp.arange(slot_count, dtype=F32)
        wide = (slot_of[:, :, None, :] == slots[None, None, :, None]).astype(BF16)
        return [
            wide[low : low + len(chunk)].reshape(len(chunk), experts * slot_count, tok_rows)
            for chunk, low in zip(CHUNKS, STARTS)
        ]


    stages = Stages(attn_in)
    cot, ffn = Gather(cotangent), Gather(None)
    d_sum, out_sum = Scatter(), Scatter()
    order = range(len(CHUNKS))
    cot_rows, cot_acts, kept = {}, {}, {}

    def advance(works=(), extra=(), **hops):
        tables = {"cot": cot, "ffn": ffn, "d": d_sum, "out": out_sum}
        sends = list(extra)
        spans = []
        for name, moves in hops.items():
            spans.append((tables[name], moves, len(sends)))
            sends += tables[name].sends(moves)
        got, made = stages.run(sends, works)
        for table, moves, low in spans:
            table.take(moves, got[low : low + len(moves)])
        return got[: len(extra)], made

    def cot_work(*chunks):
        made = [cot.chunk(i) for i in chunks]

        def work(picks_i, w_down_i, *args):
            blocks = []
            for i, (_, _, late), (values, crossing) in zip(chunks, made, args):
                blocks += Gather.complete(i, values, crossing, late)
            return cot_chunk(picks_i, w_down_i, blocks, slot_count)

        picks_i = picks[chunks[0]] if len(chunks) == 1 else jnp.concatenate([picks[i] for i in chunks], axis=0)
        return work, (picks_i, w_down) + tuple((values, crossing) for values, crossing, _ in made)

    def cot_done(chunks, made):
        for n, i in enumerate(chunks):
            cot_rows[i], cot_acts[i] = (made[0], n), (made[1], n)

    def main_work(i):
        values, crossing, late = ffn.chunk(i)

        def work(picks_i, gates_i, acts_i, gate_w, up_w, values, crossing):
            blocks = Gather.complete(i, values, crossing, late)
            return main_chunk(picks_i, gates_i, acts_i, cot_acts[i][1], gate_w, up_w, blocks, slot_count)

        gates_i = token_gates[STARTS[i] : STARTS[i] + len(CHUNKS[i])]
        return work, (picks[i], gates_i, cot_acts[i][0], w_gate, w_up, values, crossing)

    def out_work(*chunks):
        def work(picks_i, scaled_i, w_down_i):
            return out_chunk(picks_i, scaled_i, w_down_i, slot_count)

        return work, ([picks[i] for i in chunks], [kept[i][1] for i in chunks], w_down)

    (across, mate), ((cosine, sine), slot_of) = advance(
        [(turn_tables, (blocks_at,)), (to_groups, (slot_of,))],
        extra=[(attn_in, "y"), (attn_in, "c")],
        cot=[("z", (0, 0, 0)), ("x", (0, 0, 0))],
    )

    def project(block, mate, across, w_query, w_key, w_value):
        blocks = [block, mate, across, send(across, "c")]
        q_raw, k_raw, v_low, q_square, k_square = qkv(blocks, w_query, w_key, w_value)
        squares = token_sums(jnp.sum(q_square, axis=1), jnp.sum(k_square, axis=1))
        return blocks, q_raw, k_raw, v_low, squares

    _, (made,) = advance(
        [(project, (attn_in, mate, across, w_query, w_key, w_value))],
        cot=[("z", (1, 0, 0)), ("x", (1, 0, 0)), ("y", (0, 0, 0)), ("c", (0, 0, 0)), ("c", (1, 0, 0))],
    )
    seq_blocks, q_raw, k_raw, v_low, squares = made

    def columns_of(squares):
        scales = lax.rsqrt(squares / model_width + EPS)
        columns = jnp.stack([scales[0], scales[1], positions.astype(F32)], axis=1)
        return jnp.pad(columns, ((0, 0), (0, HDIM - columns.shape[1])))

    cols = columns_of(squares)
    _, (made,) = advance(
        [(attend_forward, (q_raw, k_raw, v_low, cols, q_gain, k_gain, cosine, sine, key_pos))],
        cot=[("z", (2, 0, 0)), ("x", (2, 0, 0)), ("y", (1, 0, 0)), ("c", (0, 1, 0)), ("c", (0, 0, 1))],
    )
    o_low, lse, q_rot, k_rot = made

    def project_back(o_low, w_out):
        parts = [
            jnp.dot(o_low[r * tok_rows : (r + 1) * tok_rows], w_out, preferred_element_type=F32).astype(BF16)
            for r in range(tensor_count)
        ]
        across = add_low(parts[2], send(parts[3], "c"))
        return add_wide(parts[0], send(parts[1], "c")) + send(across, "y").astype(F32)

    _, (attn_rows, picks) = advance(
        [(project_back, (o_low, w_out)), (all_picks, (slot_of,))],
        cot=[("x", (3, 0, 0)), ("c", (2, 0, 0)), ("c", (1, 1, 0))],
    )
    mixed = resid + attn_rows
    scale_two = rms_scale(mixed)
    mixed_norm = mixed * scale_two
    ffn_in = (mixed_norm * ffn_gain.astype(F32)).astype(BF16)
    ffn.held[0, 0, 0, 0] = ffn_in

    def route(ffn_in, w_router):
        logits = jnp.dot(ffn_in, w_router, preferred_element_type=F32)
        return jax.nn.softmax(logits, axis=-1)

    def join(*blocks):
        return jnp.concatenate(blocks, axis=0)

    _, (router_probs, made, gathered) = advance(
        [(route, (ffn_in, w_router)), cot_work(0), (join, tuple(seq_blocks))],
        ffn=[("z", (0, 0, 0)), ("x", (0, 0, 0)), ("y", (0, 0, 0))],
        cot=[("c", (1, 0, 1)), ("c", (2, 1, 0))],
    )
    cot_done((0,), made)
    _, (made, token_gates) = advance(
        [cot_work(1), (to_groups, (router_probs.T,))],
        ffn=[("z", (1, 0, 0)), ("x", (1, 0, 0)), ("y", (1, 0, 0))]
        + [("c", (0, 0, 0)), ("c", (0, 1, 0)), ("c", (1, 0, 0)), ("c", (0, 0, 1))],
    )
    cot_done((1,), made)
    _, (made,) = advance(
        [main_work(0)],
        ffn=[("z", (2, 0, 0)), ("x", (2, 0, 0)), ("c", (2, 0, 0))],
        cot=[("y", (2, 0, 0)), ("c", (3, 0, 0))],
    )
    kept[0], near, far = made[0], *made[1]
    _, (made,) = advance(
        [(core_sum, (near, far))],
        ffn=[("x", (3, 0, 0)), ("c", (1, 1, 0)), ("c", (1, 0, 1)), ("c", (2, 1, 0))],
        cot=[("y", (3, 0, 0))],
    )
    d_sum.put(0, made)
    _, (made,) = advance(
        [main_work(1)],
        ffn=[("y", (2, 0, 0))],
        cot=[("x", (0, 0, 1)), ("c", (3, 1, 0)), ("c", (2, 0, 1))],
    )
    kept[1], near, far = made[0], *made[1]
    _, (made, other) = advance(
        [(core_sum, (near, far)), cot_work(2)],
        ffn=[("y", (3, 0, 0)), ("c", (3, 0, 0)), ("c", (3, 1, 0))],
        cot=[("x", (1, 0, 1))],
    )
    d_sum.put(1, made)
    cot_done((2,), other)
    _, (made,) = advance(
        [main_work(2)],
        cot=[("x", (2, 0, 1)), ("y", (3, 1, 0)), ("c", (0, 1, 1)), ("c", (1, 1, 1))],
    )
    kept[2], near, far = made[0], *made[1]
    _, (made, other) = advance(
        [(core_sum, (near, far)), cot_work(3, 4)],
        ffn=[("x", (2, 0, 1)), ("y", (1, 1, 0))],
    )
    d_sum.put(2, made)
    cot_done((3, 4), other)
    _, (made,) = advance([main_work(3)], ffn=[("x", (3, 0, 1)), ("y", (0, 1, 0))])
    kept[3], near, far = made[0], *made[1]
    _, (made,) = advance([(core_sum, (near, far))], ffn=[("c", (0, 1, 1)), ("c", (3, 1, 1))])
    d_sum.put(3, made)

    _, (made,) = advance([main_work(4)], d=[("x", (1, 1, 1)), ("y", (2, 1, 1))])
    kept[4], near, far = made[0], *made[1]

    def return_probs(*d_probs):
        d_probs = jnp.concatenate(d_probs, axis=0)[position]
        arrived = lax.all_to_all(d_probs, BOTH, split_axis=0, concat_axis=0, tiled=True)
        arrived = arrived.reshape(group_count, tensor_count, experts, tok_rows)
        return jnp.sum(arrived, axis=1).reshape(expert_total, tok_rows).T

    outs = {}
    _, (made, outs[0], d_probs) = advance(
        [(core_sum, (near, far)), out_work(0), (return_probs, tuple(kept[i][4] for i in order))],
        d=[("x", (1, 1, 0)), ("y", (1, 0, 1))],
    )
    d_sum.put(4, made)
    _, (outs[1], made) = advance(
        [out_work(1), (core_sum, tuple(outs[0]))], d=[("x", (3, 1, 1)), ("y", (0, 1, 1))]
    )
    out_sum.put(0, made)
    _, (outs[2], made) = advance(
        [out_work(2), (core_sum, tuple(outs[1]))],
        d=[("x", (2, 1, 0)), ("y", (2, 0, 1)), ("z", (1, 0, 0))],
    )
    out_sum.put(1, made)
    _, (last_outs, made) = advance(
        [out_work(3, 4), (core_sum, tuple(outs[2]))],
        d=[("x", (3, 1, 0)), ("y", (3, 0, 1)), ("z", (2, 0, 0))],
    )
    out_sum.put(2, made)
    def saved(n):
        return [kept[i][n] for i in order]

    def grads_of(first, last, earlier=None):
        all_cots = [cot_rows[i][0] for i in order]

        places = [cot_rows[i][1] for i in order]

        def work(*args):
            return expert_grads(*args[:5], places, first, last, args[5] if len(args) > 5 else None)

        args = (saved(0), all_cots, saved(1), saved(2), saved(3))
        return work, args if earlier is None else args + (earlier,)

    thirds = [experts * n // 3 for n in range(4)]
    _, (made, weight_grads) = advance(
        [(core_sum, tuple(last_outs)), grads_of(thirds[0], thirds[1])],
        d=[("x", (0, 1, 0)), ("y", (0, 0, 1)), ("z", (3, 0, 0))],
    )
    out_sum.put(3, made[:2])
    out_sum.put(4, made[2:])
    d_ffn = d_sum.total()

    d_result = cotangent.astype(F32)
    d_logits = (
        router_probs * (d_probs - jnp.sum(router_probs * d_probs, axis=-1, keepdims=True))
    ).astype(BF16)
    router_part = contract_rows(d_logits, ffn_in)
    d_ffn = d_ffn + times_transpose(d_logits, w_router)
    ffn_gain_part = jnp.sum(d_ffn * mixed_norm, axis=0)
    d_norm_two = d_ffn * ffn_gain.astype(F32)
    d_mixed = d_result + scale_two * (
        d_norm_two - mixed_norm * jnp.mean(d_norm_two * mixed_norm, axis=-1, keepdims=True)
    )
    d_attn = d_mixed.astype(BF16)
    router_sums = jnp.concatenate(
        [router_part, jnp.broadcast_to(ffn_gain_part[None, :], (16, model_width))], axis=0
    ).astype(BF16)

    (across, mate, other), (weight_grads,) = advance(
        [grads_of(thirds[1], thirds[2], weight_grads)],
        extra=[(d_attn, "y"), (d_attn, "c"), (router_sums, "z1")],
        out=[("x", (1, 1, 1))],
    )
    router_sums = add_low(router_sums, other)

    def attend_back(d_attn, mate, across, w_out, o_low, *rest):
        d_blocks = [d_attn, mate, across, send(across, "c")]
        d_attended = join(*[times_transpose(block, w_out).astype(BF16) for block in d_blocks])
        q_raw, k_raw, v_low, q_rot, k_rot, lse, cols = rest
        *made, q_inner, k_inner = attend_backward(
            q_raw, k_raw, v_low, q_rot, k_rot, d_attended, lse, cols, q_gain, k_gain, cosine, sine, key_pos
        )
        inner = token_sums(jnp.sum(q_inner, axis=1), jnp.sum(k_inner, axis=1)) / model_width
        return made, inner, contract_rows(o_low, join(*d_blocks)).astype(BF16)

    _, (made,) = advance(
        [
            (
                attend_back,
                (d_attn, mate, across, w_out, o_low, q_raw, k_raw, v_low, q_rot, k_rot, lse, cols),
            )
        ],
        out=[("x", (3, 1, 1)), ("x", (1, 1, 0)), ("y", (2, 1, 1)), ("y", (1, 0, 1))],
    )
    (dq_hat, dk_hat, dv_raw, query_gain_part, key_gain_part), inner, grad_w_out = made

    def value_grad(gathered, dv_raw):
        return contract_rows(gathered, dv_raw).astype(BF16)

    def norm_back(q_raw, k_raw, cols, dq_hat, dk_hat, inner):
        raws = []
        for n, (raw, d_hat) in enumerate(((q_raw, dq_hat), (k_raw, dk_hat))):
            scale = cols[:, n : n + 1]
            raws.append((scale * (d_hat - raw * scale * inner[n][:, None])).astype(BF16))
        return raws

    out_weight = DpSum(grad_w_out)
    (other, *got), ((dq_raw, dk_raw), grad_value, (grad_w_gate, grad_w_up, grad_w_down)) = advance(
        [
            (norm_back, (q_raw, k_raw, cols, dq_hat, dk_hat, inner)),
            (value_grad, (gathered, dv_raw)),
            grads_of(thirds[2], thirds[3], weight_grads),
        ],
        extra=[(router_sums, "z2")] + out_weight.split_x(),
        out=[("x", (2, 1, 0)), ("y", (2, 0, 1)), ("z", (1, 0, 0))],
    )
    router_sums = add_low(router_sums, other)
    out_weight.add_x(got)
    value_weight = DpSum(grad_value)

    def projections_back(gathered, dq_raw, dk_raw, dv_raw, w_query, w_key, w_value):
        grads = [contract_rows(gathered, part).astype(BF16) for part in (dk_raw, dq_raw)]
        total_term = times_transpose(dq_raw, w_query)
        total_term = total_term + times_transpose(dk_raw, w_key)
        total_term = (total_term + times_transpose(dv_raw, w_value)).astype(BF16)
        return grads, total_term

    got, (((grad_key, grad_query), total_term), out_piece) = advance(
        [
            (projections_back, (gathered, dq_raw, dk_raw, dv_raw, w_query, w_key, w_value)),
            (out_weight.reduce_z, (out_weight.sum,)),
        ],
        extra=value_weight.split_x(),
        out=[("x", (3, 1, 0)), ("y", (3, 0, 1)), ("z", (2, 0, 0))],
    )
    value_weight.add_x(got)
    key_weight, query_weight = DpSum(grad_key), DpSum(grad_query)
    parts = jnp.split(total_term, tensor_count, axis=0)
    (d_other, other, *got), (value_piece,) = advance(
        [(value_weight.reduce_z, (value_weight.sum,))],
        extra=[(jnp.concatenate([parts[1], parts[3]], axis=0), "c"), (router_sums, "c")] + key_weight.split_x(),
        out=[("y", (0, 1, 1))],
    )
    router_sums = add_low(router_sums, other)
    key_weight.add_x(got)
    out_weight.part = out_piece
    (d_across, *got), _ = advance(
        extra=[(add_low(parts[2], d_other[tok_rows:]), "y")] + query_weight.split_x() + out_weight.join_z(),
    )
    query_weight.add_x(got[:1])
    out_weight.took_z(got[1:])
    d_attn_in = add_wide(parts[0], d_other[:tok_rows], d_across)
    attn_gain_part = jnp.sum(d_attn_in * normed, axis=0)
    d_norm_one = d_attn_in * attn_gain.astype(F32)
    d_input = d_mixed + scale_one * (
        d_norm_one - normed * jnp.mean(d_norm_one * normed, axis=-1, keepdims=True)
    )
    (other, third, *got), (value_weight.whole_half, d_input) = advance(
        [
            (value_weight.collect_z, (value_piece,)),
            (lambda value: value, (d_input.astype(BF16),)),
        ],
        extra=[(attn_gain_part, "c"), (router_sums, "y")] + out_weight.join_x(),
        out=[("y", (0, 0, 1))],
    )
    router_sums = add_low(router_sums, third)
    attn_gain_part = attn_gain_part + other
    out_weight.took_x(got)
    (other, *got), (key_piece, grad_w_out) = advance(
        [
            (key_weight.reduce_z, (key_weight.sum,)),
            (lambda value: value, (out_weight.result,)),
        ],
        extra=[(attn_gain_part, "y")] + value_weight.join_x(),
    )
    value_weight.took_x(got)
    gain_parts = jnp.concatenate([attn_gain_part + other, query_gain_part[0], key_gain_part[0]])
    (other, third), (query_piece, grad_value) = advance(
        [
            (query_weight.reduce_z, (query_weight.sum,)),
            (lambda value: value, (value_weight.result,)),
        ],
        extra=[(gain_parts, "x"), (router_sums, "x")],
        out=[("x", (0, 1, 0))],
    )
    gain_parts = gain_parts + other
    router_sums = add_wide(router_sums, third)
    (next_z, far_z, last_z), (key_weight.whole_half,) = advance(
        [(key_weight.collect_z, (key_piece,))],
        extra=[(gain_parts, "u1"), (gain_parts, "u2"), (gain_parts, "u3")],
    )
    gain_sums = (gain_parts + far_z) + (next_z + last_z)
    got, (query_weight.whole_half, gain_sums, router_sums) = advance(
        [
            (query_weight.collect_z, (query_piece,)),
            (lambda value: value, (gain_sums,)),
            (lambda value: value, (router_sums,)),
        ],
        extra=key_weight.join_x(),
    )
    key_weight.took_x(got)
    got, (grad_key,) = advance(
        [(lambda value: value, (key_weight.result,))],
        extra=query_weight.join_x(),
        out=[("z", (3, 0, 0))],
    )
    query_weight.took_x(got)
    grad_query = query_weight.result
    result = (mixed + out_sum.total()).astype(BF16)
    return (
        result,
        d_input,
        grad_query,
        grad_key,
        grad_value,
        gain_sums[model_width : model_width + local_width],
        gain_sums[model_width + local_width :],
        grad_w_out,
        gain_sums[:model_width],
        router_sums[expert_total],
        router_sums[:expert_total].T,
        grad_w_gate,
        grad_w_up,
        grad_w_down,
    )


def local_sent(
    hidden_in,
    cotangent,
    seq_lengths,
    expert_ids,
    attn_gain,
    w_query,
    w_key,
    w_value,
    query_gain,
    key_gain,
    w_out,
    ffn_gain,
    w_router,
    w_gate,
    w_up,
    w_down,
):
    tensor_count = lax.axis_size("tensor")
    group_count = lax.axis_size("dp")
    device_total = tensor_count * group_count
    tok_rows, model_width = hidden_in.shape
    topk_count = expert_ids.shape[1]
    local_experts = w_gate.shape[0]
    expert_total = w_router.shape[1]
    slot_count = tok_rows * topk_count // expert_total
    per_group = local_experts * slot_count
    seq_len = tok_rows * tensor_count
    local_width = w_query.shape[1]
    head_width = HDIM
    local_heads = local_width // head_width
    block_rows = min(512, seq_len)
    block_count = seq_len // block_rows
    score_scale = head_width ** (-0.5)
    live_length = seq_lengths[0]
    cosine, sine_table = (table[:, None, :] for table in rope_tables(seq_len, head_width))
    key_pos = jnp.arange(seq_len)
    key_live = key_pos < live_length

    def send_out(rows_low):
        grouped_rows = rows_low.reshape(group_count, 1, per_group, model_width)
        copies = jnp.broadcast_to(
            grouped_rows, (group_count, tensor_count, per_group, model_width)
        ).reshape(device_total, per_group, model_width)
        arrived = lax.all_to_all(copies, ("dp", "tensor"), split_axis=0, concat_axis=0, tiled=True)
        return arrived.reshape(device_total, local_experts, slot_count, model_width)

    def send_back(parts_low):
        returned = lax.all_to_all(
            parts_low.reshape(device_total, per_group, model_width),
            ("dp", "tensor"),
            split_axis=0,
            concat_axis=0,
            tiled=True,
        )
        return jnp.sum(
            returned.reshape(group_count, tensor_count, per_group, model_width).astype(F32),
            axis=1,
        ).reshape(-1, model_width)

    resid = hidden_in.astype(F32)
    scale_one = rms_scale(resid)
    normed = resid * scale_one
    attn_in = (normed * attn_gain.astype(F32)).astype(BF16)
    gathered = lax.all_gather(attn_in, "tensor", axis=0, tiled=True)
    q_raw = jnp.dot(gathered, w_query, preferred_element_type=F32)
    k_raw = jnp.dot(gathered, w_key, preferred_element_type=F32)
    v_raw = jnp.dot(gathered, w_value, preferred_element_type=F32)
    q_square, k_square = lax.psum(
        (jnp.sum(q_raw * q_raw, axis=1), jnp.sum(k_raw * k_raw, axis=1)), "tensor"
    )
    q_rscale = lax.rsqrt(q_square / model_width + EPS)[:, None]
    k_rscale = lax.rsqrt(k_square / model_width + EPS)[:, None]
    query_hat = q_raw * q_rscale
    key_hat = k_raw * k_rscale
    q_gain = query_gain.astype(F32)
    k_gain = key_gain.astype(F32)
    q_rot = rotate(
        (query_hat * q_gain).reshape(seq_len, local_heads, head_width), cosine, sine_table
    ).astype(BF16)
    k_rot = rotate(
        (key_hat * k_gain).reshape(seq_len, local_heads, head_width), cosine, sine_table
    ).astype(BF16)
    v_low = v_raw.astype(BF16).reshape(seq_len, local_heads, head_width)
    starts = jnp.arange(block_count) * block_rows
    q_blocks = q_rot.reshape(block_count, block_rows, local_heads, head_width)

    def allowed_mask(row_start):
        q_pos = row_start + jnp.arange(block_rows)
        return ((key_pos[None, :] <= q_pos[:, None]) & key_live[None, :])[None]

    def attend(inputs):
        q_block, row_start = inputs
        scores = (
            jnp.einsum("qhd,khd->hqk", q_block, k_rot, preferred_element_type=F32)
            * score_scale
        )
        scores = jnp.where(allowed_mask(row_start), scores, -1e30)
        row_max = jnp.max(scores, axis=-1, keepdims=True)
        exp_scores = jnp.exp(scores - row_max)
        row_total = jnp.sum(exp_scores, axis=-1, keepdims=True)
        soft_low = (exp_scores / row_total).astype(BF16)
        attended = jnp.einsum("hqk,khd->qhd", soft_low, v_low, preferred_element_type=F32)
        return (attended, (row_max + jnp.log(row_total))[..., 0])

    o_blocks, lse_blocks = lax.map(attend, (q_blocks, starts))
    o_low = o_blocks.reshape(seq_len, local_width).astype(BF16)
    attn_rows = lax.psum_scatter(
        jnp.dot(o_low, w_out, preferred_element_type=F32),
        "tensor",
        scatter_dimension=0,
        tiled=True,
    )
    mixed = resid + attn_rows
    scale_two = rms_scale(mixed)
    mixed_norm = mixed * scale_two
    ffn_in = (mixed_norm * ffn_gain.astype(F32)).astype(BF16)
    logits = jnp.dot(ffn_in, w_router, preferred_element_type=F32)
    router_probs = jax.nn.softmax(logits, axis=-1)
    expert_hot = (expert_ids[:, :, None] == jnp.arange(expert_total)[None, None, :]).astype(
        F32
    )
    gate_values = jnp.einsum("tke,te->tk", expert_hot, router_probs)
    flat_ids = expert_ids.reshape(-1)
    sort_order = jnp.argsort(flat_ids, stable=True)
    inverse = jnp.argsort(sort_order)
    expert_in = send_out(ffn_in[sort_order // topk_count])
    gate_pre = jnp.einsum("secd,edf->secf", expert_in, w_gate, preferred_element_type=F32)
    up_pre = jnp.einsum("secd,edf->secf", expert_in, w_up, preferred_element_type=F32)
    silu_gate = jax.nn.silu(gate_pre)
    acts = (silu_gate * up_pre).astype(BF16)
    partial_value = jnp.einsum(
        "secf,efd->secd", acts, w_down, preferred_element_type=F32
    ).astype(BF16)
    out_sorted = send_back(partial_value)
    out_assign = out_sorted[inverse].reshape(tok_rows, topk_count, model_width)
    expert_mix = jnp.einsum("tk,tkd->td", gate_values, out_assign)
    result = mixed + expert_mix
    d_result = cotangent.astype(F32)
    d_gates = jnp.einsum("tkd,td->tk", out_assign, d_result)
    d_out = (
        (gate_values[:, :, None] * d_result[:, None, :])
        .astype(BF16)
        .reshape(-1, model_width)[sort_order]
    )
    d_arrived = send_out(d_out)
    d_acts = jnp.einsum("secd,efd->secf", d_arrived, w_down, preferred_element_type=F32)
    sigmoid_gate = jax.nn.sigmoid(gate_pre)
    d_gate_pre = (d_acts * up_pre * sigmoid_gate * (1.0 + gate_pre * (1.0 - sigmoid_gate))).astype(
        BF16
    )
    d_up_pre = (d_acts * silu_gate).astype(BF16)
    grad_w_down = jnp.einsum("secf,secd->efd", acts, d_arrived, preferred_element_type=F32)
    grad_w_gate = jnp.einsum(
        "secd,secf->edf", expert_in, d_gate_pre, preferred_element_type=F32
    )
    grad_w_up = jnp.einsum(
        "secd,secf->edf", expert_in, d_up_pre, preferred_element_type=F32
    )
    d_rows = (
        jnp.einsum("secf,edf->secd", d_gate_pre, w_gate, preferred_element_type=F32)
        + jnp.einsum("secf,edf->secd", d_up_pre, w_up, preferred_element_type=F32)
    ).astype(BF16)
    d_sorted = send_back(d_rows)
    d_ffn = jnp.sum(d_sorted[inverse].reshape(tok_rows, topk_count, model_width), axis=1)
    d_probs = jnp.einsum("tk,tke->te", d_gates, expert_hot)
    d_logits = (
        router_probs * (d_probs - jnp.sum(router_probs * d_probs, axis=-1, keepdims=True))
    ).astype(BF16)
    router_part = contract_rows(ffn_in, d_logits)
    d_ffn = d_ffn + times_transpose(d_logits, w_router)
    ffn_gain_part = jnp.sum(d_ffn * mixed_norm, axis=0)
    d_norm_two = d_ffn * ffn_gain.astype(F32)
    d_mixed = d_result + scale_two * (
        d_norm_two - mixed_norm * jnp.mean(d_norm_two * mixed_norm, axis=-1, keepdims=True)
    )
    d_attn = d_mixed.astype(BF16)
    d_attn_all = lax.all_gather(d_attn, "tensor", axis=0, tiled=True)
    grad_w_out = contract_rows(o_low, d_attn_all)
    d_attended = (
        times_transpose(d_attn_all, w_out)
        .astype(BF16)
        .reshape(block_count, block_rows, local_heads, head_width)
    )

    def attend_back(carry, inputs):
        dk_total, dv_total = carry
        q_block, do_block, lse_block, row_start = inputs
        scores = (
            jnp.einsum("qhd,khd->hqk", q_block, k_rot, preferred_element_type=F32)
            * score_scale
        )
        allowed = allowed_mask(row_start)
        scores = jnp.where(allowed, scores, -1e30)
        soft = jnp.where(allowed, jnp.exp(scores - lse_block[..., None]), 0.0)
        d_weights = jnp.einsum("qhd,khd->hqk", do_block, v_low, preferred_element_type=F32)
        d_scores = (soft * (d_weights - jnp.sum(soft * d_weights, axis=-1, keepdims=True))).astype(
            BF16
        )
        dq_block = (
            jnp.einsum("hqk,khd->qhd", d_scores, k_rot, preferred_element_type=F32)
            * score_scale
        )
        dk_total = (
            dk_total
            + jnp.einsum("hqk,qhd->khd", d_scores, q_block, preferred_element_type=F32)
            * score_scale
        )
        dv_total = dv_total + jnp.einsum(
            "hqk,qhd->khd", soft.astype(BF16), do_block, preferred_element_type=F32
        )
        return ((dk_total, dv_total), dq_block)

    zero_field = jnp.zeros((seq_len, local_heads, head_width), F32)
    (dk_rot, dv_full), dq_blocks = lax.scan(
        attend_back, (zero_field, zero_field), (q_blocks, d_attended, lse_blocks, starts)
    )
    dq_gain = unrotate(
        dq_blocks.reshape(seq_len, local_heads, head_width), cosine, sine_table
    ).reshape(seq_len, local_width)
    dk_gain = unrotate(dk_rot, cosine, sine_table).reshape(seq_len, local_width)
    query_gain_part = jnp.sum(dq_gain * query_hat, axis=0)
    key_gain_part = jnp.sum(dk_gain * key_hat, axis=0)
    dq_hat = dq_gain * q_gain
    dk_hat = dk_gain * k_gain
    q_inner, k_inner = lax.psum(
        (jnp.sum(dq_hat * query_hat, axis=1), jnp.sum(dk_hat * key_hat, axis=1)), "tensor"
    )
    dq_raw = (q_rscale * (dq_hat - query_hat * (q_inner / model_width)[:, None])).astype(
        BF16
    )
    dk_raw = (k_rscale * (dk_hat - key_hat * (k_inner / model_width)[:, None])).astype(BF16)
    dv_raw = dv_full.reshape(seq_len, local_width).astype(BF16)
    grad_query = contract_rows(gathered, dq_raw)
    grad_key = contract_rows(gathered, dk_raw)
    grad_value = contract_rows(gathered, dv_raw)
    total_term = times_transpose(dq_raw, w_query)
    total_term = total_term + times_transpose(dk_raw, w_key)
    d_attn_in = lax.psum_scatter(
        (total_term + times_transpose(dv_raw, w_value)).astype(BF16),
        "tensor",
        scatter_dimension=0,
        tiled=True,
    ).astype(F32)
    attn_gain_part = jnp.sum(d_attn_in * normed, axis=0)
    d_norm_one = d_attn_in * attn_gain.astype(F32)
    d_input = d_mixed + scale_one * (
        d_norm_one - normed * jnp.mean(d_norm_one * normed, axis=-1, keepdims=True)
    )
    dp_sums = (
        lax.psum(grad_query.astype(BF16), "dp").astype(F32),
        lax.psum(grad_key.astype(BF16), "dp").astype(F32),
        lax.psum(grad_value.astype(BF16), "dp").astype(F32),
        lax.psum(query_gain_part.astype(BF16), "dp").astype(F32),
        lax.psum(key_gain_part.astype(BF16), "dp").astype(F32),
        lax.psum(grad_w_out.astype(BF16), "dp").astype(F32),
    )
    shared = lax.psum((attn_gain_part, ffn_gain_part, router_part), ("dp", "tensor"))
    return (
        result.astype(BF16),
        d_input.astype(BF16),
        dp_sums[0],
        dp_sums[1],
        dp_sums[2],
        dp_sums[3],
        dp_sums[4],
        dp_sums[5],
        shared[0],
        shared[1],
        shared[2],
        grad_w_gate,
        grad_w_up,
        grad_w_down,
    )


def solution(mesh):
    rows, columns = P(BOTH, None), P(None, "tensor")
    gathered_plan = (mesh.shape["dp"], mesh.shape["tensor"]) == (2 * RING, 4)
    return jax.shard_map(
        local_gathered if gathered_plan else local_sent,
        mesh=mesh,
        in_specs=(
            rows,
            rows,
            P("dp"),
            rows,
            P(),
            columns,
            columns,
            columns,
            P("tensor"),
            P("tensor"),
            P("tensor", None),
            P(),
            P(),
            P("dp", None, "tensor"),
            P("dp", None, "tensor"),
            P("dp", "tensor", None),
        ),
        out_specs=(
            rows,
            rows,
            columns,
            columns,
            columns,
            P("tensor"),
            P("tensor"),
            P("tensor", None),
            P(),
            P(),
            P(),
            P("dp", None, "tensor"),
            P("dp", None, "tensor"),
            P("dp", "tensor", None),
        ),
        check_vma=False,
    )
```

```python
import functools
import math

import jax
import jax.numpy as jnp
from jax import lax
from jax.experimental import pallas as pl
from jax.experimental.pallas import tpu as pltpu
from jax.sharding import PartitionSpec as P

HDIM = 128
EPS = 1e-05
ROPE_BASE = 10000.0
BOTH = ("dp", "tensor")
F32 = jnp.float32
BF16 = jnp.bfloat16
VMEM_GRANT = 60 << 20
fence = lax.optimization_barrier


def rms_scale(values):
    return lax.rsqrt(jnp.mean(values * values, axis=-1, keepdims=True) + EPS)


def rope_tables(count, head_width):
    half_width = head_width // 2
    frequency = jnp.exp(
        -(jnp.arange(half_width, dtype=F32) * 2.0 / head_width) * math.log(ROPE_BASE)
    )
    angles = jnp.arange(count, dtype=F32)[:, None] * frequency[None, :]
    return (jnp.cos(angles), jnp.sin(angles))


def rotate(values_in, cosine, sine_table):
    half_width = values_in.shape[-1] // 2
    front_half = values_in[..., :half_width]
    back_half = values_in[..., half_width:]
    return jnp.concatenate(
        [
            front_half * cosine - back_half * sine_table,
            back_half * cosine + front_half * sine_table,
        ],
        axis=-1,
    )


def unrotate(grads_in, cosine, sine_table):
    return rotate(grads_in, cosine, -sine_table)


def contract_rows(left, right):
    return lax.dot_general(left, right, (((0,), (0,)), ((), ())), preferred_element_type=F32)


def times_transpose(left, right):
    return lax.dot_general(left, right, (((1,), (1,)), ((), ())), preferred_element_type=F32)


def add_low(*terms):
    total = terms[0].astype(F32)
    for term in terms[1:]:
        total = total + term.astype(F32)
    return total.astype(BF16)


def add_wide(*terms):
    total = terms[0].astype(F32)
    for term in terms[1:]:
        total = total + term.astype(F32)
    return total


RING = 4
COLUMNS = (
    ((0, 0, 0), (1, 0, 0), (0, 1, 0), (0, 0, 1)),
    ((2, 0, 0), (1, 1, 0), (1, 0, 1), (2, 1, 0)),
    ((3, 0, 0), (3, 1, 0), (2, 0, 1), (3, 0, 1)),
    ((1, 1, 1), (2, 1, 1)),
    ((0, 1, 1), (3, 1, 1)),
)
CHUNKS = tuple(tuple(chip + (dc,) for dc in (0, 1) for chip in chips) for chips in COLUMNS)
STARTS = tuple(sum(len(chunk) for chunk in CHUNKS[:i]) for i in range(len(CHUNKS)))
PLACES = tuple(place for chunk in CHUNKS for place in chunk)
MOVES = {
    "x": lambda z, x, y, c: (z, x ^ 1, y, c),
    "y": lambda z, x, y, c: (z, x, y ^ 1, c),
    "c": lambda z, x, y, c: (z, x, y, c ^ 1),
    "z": lambda z, x, y, c: ((z - 1) % RING, x, y, c),
    "u1": lambda z, x, y, c: ((z + 1) % RING, x, y, c),
    "u2": lambda z, x, y, c: ((z + 2) % RING, x, y, c),
    "u3": lambda z, x, y, c: ((z + 3) % RING, x, y, c),
    "z1": lambda z, x, y, c: (z ^ 1, x, y, c),
    "z2": lambda z, x, y, c: (z ^ 2, x, y, c),
}


def device_pairs(move):
    pairs = []
    for z in range(RING):
        for x in range(2):
            for y in range(2):
                for c in range(2):
                    tz, tx, ty, tc = move(z, x, y, c)
                    pairs.append(((z * 2 + x) * 4 + y * 2 + c, (tz * 2 + tx) * 4 + ty * 2 + tc))
    return pairs


def send(value, axis):
    return lax.ppermute(value, BOTH, device_pairs(MOVES[axis]))


def small_sum(value, axes):
    for axis in axes:
        value = value + send(value, axis)
    return value


def hop(axis, k, dx, dy):
    return {"z": ((k + 1) % RING, dx, dy), "x": (k, dx ^ 1, dy), "y": (k, dx, dy ^ 1)}[axis]


class Stages:
    def __init__(self, token):
        self.token = token

    def run(self, sends, works=()):
        values, args, _ = fence(([s[0] for s in sends], [w[1] for w in works], self.token))
        got, crossed = [], []
        for value, (_, axis) in zip(values, sends):
            if axis == "c" and len(crossed) >= 2:
                value, _ = fence((value, crossed[-2]))
            got.append(send(value, axis))
            if axis == "c":
                crossed.append(got[-1])
        made = [work(*arg) for (work, _), arg in zip(works, args)]
        got, made = fence((got, made))
        self.token = jax.tree.leaves((got, made))[0]
        return got, made


class Gather:
    def __init__(self, block):
        self.held = {(0, 0, 0, 0): block}

    def sends(self, hops):
        return [(self.held[chip + (0,)], axis) for axis, chip in hops]

    def take(self, hops, got):
        for (axis, chip), value in zip(hops, got):
            self.held[chip + (1,) if axis == "c" else hop(axis, *chip) + (0,)] = value

    def chunk(self, i):
        chunk = CHUNKS[i]
        late = [place for place in chunk if place not in self.held]
        values = [self.held[place] for place in chunk if place in self.held]
        return values, [self.held[place[:3] + (0,)] for place in late], late

    @staticmethod
    def complete(i, values, crossing, late):
        blocks = dict(zip([place for place in CHUNKS[i] if place not in late], values))
        done = []
        for place, value in zip(late, crossing):
            if len(done) >= 2:
                value, _ = fence((value, done[-2]))
            done.append(send(value, "c"))
            blocks[place] = done[-1]
        return [blocks[place] for place in CHUNKS[i]]


class Scatter:
    def __init__(self):
        self.held = {}

    def put(self, i, sums):
        for chip, value in zip(COLUMNS[i], sums):
            self.held.setdefault(chip, []).append(value)

    def sends(self, hops):
        groups = [self.held[chip] for _, chip in hops]
        added = [group for group in groups if len(group) > 1]
        sums = iter(block_sums(added) if added else ())
        return [(next(sums) if len(group) > 1 else group[0], axis) for group, (axis, _) in zip(groups, hops)]

    def take(self, hops, got):
        for (axis, chip), value in zip(hops, got):
            self.held.setdefault(hop(axis, *chip), []).append(value)

    def total(self):
        return add_wide(*self.held[0, 0, 0])


class DpSum:
    def __init__(self, value):
        group = lax.axis_index("dp")
        self.z, self.x = group // 2, group % 2
        self.value = value
        self.half, self.piece = value.shape[0] // 2, value.shape[0] // (2 * RING)

    def split_x(self):
        return [(lax.dynamic_slice_in_dim(self.value, (1 - self.x) * self.half, self.half), "x")]

    def add_x(self, got):
        self.sum = add_low(lax.dynamic_slice_in_dim(self.value, self.x * self.half, self.half), got[0])

    def split_z(self):
        return [
            (lax.dynamic_slice_in_dim(self.sum, ((self.z + d) % RING) * self.piece, self.piece), f"u{d}")
            for d in (1, 2, 3)
        ]

    def add_z(self, got):
        self.part = add_low(lax.dynamic_slice_in_dim(self.sum, self.z * self.piece, self.piece), *got)

    def reduce_z(self, half):
        low, high = self.z % 2, self.z // 2
        pieces = half.reshape((2, 2, self.piece) + half.shape[1:])
        for bit, axis, name in ((low, 1, "z1"), (high, 0, "z2")):
            mine = lax.dynamic_index_in_dim(pieces, bit, axis, keepdims=False)
            other = lax.dynamic_index_in_dim(pieces, 1 - bit, axis, keepdims=False)
            pieces = add_low(mine, send(other, name))
        return pieces

    def collect_z(self, part):
        low, high = self.z % 2, self.z // 2
        for bit, axis, name in ((high, 0, "z2"), (low, 1, "z1")):
            other = send(part, name)
            first, second = jnp.where(bit == 0, part, other), jnp.where(bit == 0, other, part)
            part = jnp.stack([first, second], axis=axis)
        return part.reshape((self.half,) + part.shape[3:])

    def join_z(self):
        return [(self.part, f"u{d}") for d in (1, 2, 3)]

    def took_z(self, got):
        stack = jnp.stack([self.part] + list(got))
        order = (self.z - jnp.arange(RING)) % RING
        self.whole_half = stack[order].reshape(self.half, -1)

    def join_x(self):
        return [(self.whole_half, "x")]

    def took_x(self, got):
        mine, other = self.whole_half, got[0]
        first = jnp.where(self.x == 0, mine, other)
        second = jnp.where(self.x == 0, other, mine)
        self.result = jnp.concatenate([first, second], axis=0).astype(F32)


def core_sum(near, far):
    return pair_sum(near, send(far, "c"))


def place_indices():
    group, member = lax.axis_index("dp"), lax.axis_index("tensor")
    z, x, y, c = group // 2, group % 2, member // 2, member % 2
    absolute = jnp.stack(
        [(((z + k) % RING) * 2 + (x ^ dx)) * 4 + (y ^ dy) * 2 + (c ^ dc) for k, dx, dy, dc in PLACES]
    )
    table = [0] * len(PLACES)
    for position, (k, dx, dy, dc) in enumerate(PLACES):
        table[((k * 2 + dx) * 2 + dy) * 2 + dc] = position
    numbers = jnp.arange(len(PLACES))
    other_z, other_x = numbers // 8, (numbers // 4) % 2
    other_y, other_c = (numbers // 2) % 2, numbers % 2
    offset = ((((other_z - z) % RING) * 2 + (other_x ^ x)) * 2 + (other_y ^ y)) * 2 + (other_c ^ c)
    return absolute, jnp.asarray(table, jnp.int32)[offset]


def nn(left, right):
    return lax.dot_general(left, right, (((1,), (0,)), ((), ())), preferred_element_type=F32)


def nt(left, right):
    return lax.dot_general(left, right, (((1,), (1,)), ((), ())), preferred_element_type=F32)


def pick_rows(picks_ref, blocks, buffer, arrived, rows_ref, slot_count, width):
    experts = rows_ref.shape[0]
    copies = [pltpu.make_async_copy(block, buffer.at[b], arrived.at[b]) for b, block in enumerate(blocks)]
    for copy in copies:
        copy.start()
    for b, copy in enumerate(copies):
        copy.wait()
        for low in range(0, buffer.shape[2], width):
            columns = pl.ds(low, width)
            picked = nn(picks_ref[b], buffer[b, :, columns]).astype(BF16)
            for e in range(experts):
                rows_ref[e, pl.ds(b * slot_count, slot_count), columns] = picked[
                    e * slot_count : (e + 1) * slot_count
                ]


def give_rows(groups, rows_ref, buffer, left, slot_count, width):
    experts = rows_ref.shape[0]
    copies, n = [], 0
    for picks_ref, targets in groups:
        for b, target in enumerate(targets):
            for low in range(0, buffer.shape[2], width):
                columns = pl.ds(low, width)
                slots = jnp.concatenate(
                    [rows_ref[e, pl.ds(n * slot_count, slot_count), columns] for e in range(experts)], axis=0
                )
                buffer[n, :, columns] = contract_rows(picks_ref[b], slots).astype(BF16)
            copies.append(pltpu.make_async_copy(buffer.at[n], target, left.at[n]))
            copies[-1].start()
            n += 1
    for copy in copies:
        copy.wait()


def halves_of(outs, first, count):
    return [out.at[first + b] for out in outs for b in range(count // 2)]


def cot_kernel(count, slot_count, picks_ref, down_ref, *refs):
    blocks, (rows_out, acts_out, rows_ref, buffer, arrived, left) = refs[:count], refs[count:]
    e = pl.program_id(0)

    @pl.when(e == 0)
    def _():
        pick_rows(picks_ref, blocks, buffer, arrived, rows_ref, slot_count, 512)

    out = pltpu.make_async_copy(rows_ref, rows_out, left.at[0])

    @pl.when(e == 0)
    def _():
        out.start()

    acts_out[0] = nt(rows_ref[e], down_ref[0])

    @pl.when(e == pl.num_programs(0) - 1)
    def _():
        out.wait()


def main_kernel(count, slot_count, picks_ref, gates_ref, acts_ref, gate_ref, up_ref, *refs):
    blocks = refs[:count]
    rows_out, scaled_out, d_gate_out, d_up_out, d_probs_out = refs[count : count + 5]
    near_out, far_out, rows_ref, d_rows_ref, buffer, arrived, left, copied = refs[count + 5 :]
    e = pl.program_id(0)

    @pl.when(e == 0)
    def _():
        pick_rows(picks_ref, blocks, buffer, arrived, rows_ref, slot_count, 512)

    out = pltpu.make_async_copy(rows_ref, rows_out, copied.at[0])

    @pl.when(e == 0)
    def _():
        out.start()

    rows = rows_ref[e]
    pre, up = nn(rows, gate_ref[0]), nn(rows, up_ref[0])
    cot_acts = acts_ref[0]
    own_slots = pl.ds(pl.multiple_of(e * slot_count, slot_count), slot_count)
    own_picks = [picks_ref[b, own_slots, :].astype(F32) for b in range(count)]
    gate = jnp.concatenate(
        [
            jnp.sum(pick * gates_ref[b, pl.ds(e, 1), :], axis=1, keepdims=True)
            for b, pick in enumerate(own_picks)
        ],
        axis=0,
    )
    sig = jax.nn.sigmoid(pre)
    silu = pre * sig
    acts = silu * up
    scaled_out[0] = (gate * acts).astype(BF16)
    inner = jnp.sum(acts.astype(BF16).astype(F32) * cot_acts, axis=1, keepdims=True)
    for b, pick in enumerate(own_picks):
        here = inner[b * slot_count : (b + 1) * slot_count]
        d_probs_out[b, pl.ds(e, 1), :] = jnp.sum(pick * here, axis=0, keepdims=True)
    d_acts = gate * cot_acts
    d_pre = (d_acts * up * sig * (1.0 + pre * (1.0 - sig))).astype(BF16)
    d_up = (d_acts * silu).astype(BF16)
    d_gate_out[0] = d_pre
    d_up_out[0] = d_up
    d_rows_ref[e] = (nt(d_pre, gate_ref[0]) + nt(d_up, up_ref[0])).astype(BF16)

    @pl.when(e == pl.num_programs(0) - 1)
    def _():
        targets = halves_of((near_out, far_out), 0, count)
        give_rows([(picks_ref, targets)], d_rows_ref, buffer, left, slot_count, 512)
        out.wait()


def out_kernel(parts, slot_count, *refs):
    picks, scaled, down_ref = refs[:parts], refs[parts : 2 * parts], refs[2 * parts]
    near_out, far_out, rows_ref, buffer, left = refs[2 * parts + 1 :]
    e = pl.program_id(0)
    rows = scaled[0][0] if parts == 1 else jnp.concatenate([part[0] for part in scaled], axis=0)
    rows_ref[e] = nn(rows, down_ref[0]).astype(BF16)

    @pl.when(e == pl.num_programs(0) - 1)
    def _():
        groups, done = [], 0
        for part in picks:
            groups.append((part, halves_of((near_out, far_out), done, part.shape[0])))
            done += part.shape[0] // 2
        give_rows(groups, rows_ref, buffer, left, slot_count, 512)


def per_expert(*shape):
    return pl.BlockSpec((1,) + shape, lambda e: (e,) + (0,) * len(shape))


def in_place(count):
    return [pl.BlockSpec(memory_space=pl.ANY)] * count


def resident(*shape):
    return pl.BlockSpec(shape, lambda e: (0,) * len(shape), pipeline_mode=pl.Buffered(1))


def cot_chunk(picks, w_down, blocks, slot_count):
    experts, hidden, width = w_down.shape
    count, tokens = len(blocks), blocks[0].shape[0]
    rows = count * slot_count
    return pl.pallas_call(
        functools.partial(cot_kernel, count, slot_count),
        grid=(experts,),
        in_specs=[resident(*picks.shape), per_expert(hidden, width)] + in_place(count),
        out_specs=in_place(1) + [per_expert(rows, hidden)],
        out_shape=[
            jax.ShapeDtypeStruct((experts, rows, width), BF16),
            jax.ShapeDtypeStruct((experts, rows, hidden), F32),
        ],
        scratch_shapes=[
            pltpu.VMEM((experts, rows, width), BF16),
            pltpu.VMEM((count, tokens, width), BF16),
            pltpu.SemaphoreType.DMA((count,)),
            pltpu.SemaphoreType.DMA((1,)),
        ],
        compiler_params=pltpu.CompilerParams(vmem_limit_bytes=VMEM_GRANT),
        cost_estimate=pl.CostEstimate(
            flops=2 * experts * rows * width * (hidden + tokens),
            bytes_accessed=2 * (count * tokens * width + experts * (rows + hidden) * width),
            transcendentals=0,
        ),
    )(picks, w_down, *blocks)


def main_chunk(picks, gates, cot_acts, acts_at, w_gate, w_up, blocks, slot_count):
    experts, width, hidden = w_gate.shape
    count, tokens = len(blocks), blocks[0].shape[0]
    rows = count * slot_count
    outs = pl.pallas_call(
        functools.partial(main_kernel, count, slot_count),
        grid=(experts,),
        in_specs=[
            resident(*picks.shape),
            resident(*gates.shape),
            pl.BlockSpec((1, rows, hidden), lambda e: (e, acts_at, 0)),
            per_expert(width, hidden),
            per_expert(width, hidden),
        ]
        + in_place(count),
        out_specs=in_place(1)
        + [
            per_expert(rows, hidden),
            per_expert(rows, hidden),
            per_expert(rows, hidden),
            resident(*gates.shape),
        ]
        + in_place(2),
        out_shape=[
            jax.ShapeDtypeStruct((experts, rows, width), BF16),
            jax.ShapeDtypeStruct((experts, rows, hidden), BF16),
            jax.ShapeDtypeStruct((experts, rows, hidden), BF16),
            jax.ShapeDtypeStruct((experts, rows, hidden), BF16),
            jax.ShapeDtypeStruct(gates.shape, F32),
        ]
        + [jax.ShapeDtypeStruct((count // 2, tokens, width), BF16)] * 2,
        scratch_shapes=[
            pltpu.VMEM((experts, rows, width), BF16),
            pltpu.VMEM((experts, rows, width), BF16),
            pltpu.VMEM((count, tokens, width), BF16),
            pltpu.SemaphoreType.DMA((count,)),
            pltpu.SemaphoreType.DMA((count,)),
            pltpu.SemaphoreType.DMA((1,)),
        ],
        compiler_params=pltpu.CompilerParams(vmem_limit_bytes=VMEM_GRANT),
        cost_estimate=pl.CostEstimate(
            flops=2 * experts * rows * width * (4 * hidden + 2 * tokens),
            bytes_accessed=2 * (2 * count * tokens * width + experts * (rows + 2 * hidden) * width),
            transcendentals=experts * rows * hidden,
        ),
    )(picks, gates, cot_acts, w_gate, w_up, *blocks)
    return outs[:5], outs[5:]


def out_chunk(picks, scaled, w_down, slot_count):
    experts, hidden, width = w_down.shape
    tokens = picks[0].shape[2]
    count = sum(part.shape[0] for part in picks)
    rows = count * slot_count
    return pl.pallas_call(
        functools.partial(out_kernel, len(picks), slot_count),
        grid=(experts,),
        in_specs=[resident(*part.shape) for part in picks]
        + [per_expert(*part.shape[1:]) for part in scaled]
        + [per_expert(hidden, width)],
        out_specs=in_place(2),
        out_shape=[jax.ShapeDtypeStruct((count // 2, tokens, width), BF16)] * 2,
        scratch_shapes=[
            pltpu.VMEM((experts, rows, width), BF16),
            pltpu.VMEM((count, tokens, width), BF16),
            pltpu.SemaphoreType.DMA((count,)),
        ],
        compiler_params=pltpu.CompilerParams(vmem_limit_bytes=VMEM_GRANT),
        cost_estimate=pl.CostEstimate(
            flops=2 * experts * rows * width * (hidden + tokens),
            bytes_accessed=2 * (count * tokens * width + experts * (rows + hidden) * width),
            transcendentals=0,
        ),
    )(*picks, *scaled, w_down)


def grad_kernel(count, *refs):
    rows, cots, scaled, d_gate, d_up = (refs[i * count : (i + 1) * count] for i in range(5))
    gate_out, up_out, down_out = refs[-3:]

    def total(lefts, rights):
        value = None
        for left, right in zip(lefts, rights):
            term = contract_rows(left[0], right[0])
            value = term if value is None else value + term
        return value

    gate_out[0] = total(rows, d_gate)
    up_out[0] = total(rows, d_up)
    down_out[0] = total(scaled, cots)


def expert_grads(rows, cots, scaled, d_gate, d_up, cots_at, first, last, earlier=None, tile=512):
    count, experts, width = len(rows), rows[0].shape[0], rows[0].shape[2]
    hidden = scaled[0].shape[2]
    slots = sum(part.shape[1] for part in rows)
    wide = [pl.BlockSpec((1, part.shape[1], tile), lambda e, n: (first + e, 0, n)) for part in rows]
    wide_cots = [
        pl.BlockSpec((1, part.shape[1], tile), lambda e, n, at=at: (first + e, at, n))
        for part, at in zip(rows, cots_at)
    ]
    narrow = [pl.BlockSpec((1, part.shape[1], hidden), lambda e, n: (first + e, 0, 0)) for part in rows]
    tall = pl.BlockSpec((1, tile, hidden), lambda e, n: (first + e, n, 0))
    given = [] if earlier is None else list(earlier)
    return pl.pallas_call(
        functools.partial(grad_kernel, count),
        grid=(last - first, width // tile),
        in_specs=wide + wide_cots + narrow * 3 + [pl.BlockSpec(memory_space=pl.ANY)] * len(given),
        out_specs=[tall, tall, pl.BlockSpec((1, hidden, tile), lambda e, n: (first + e, 0, n))],
        out_shape=[
            jax.ShapeDtypeStruct((experts, width, hidden), F32),
            jax.ShapeDtypeStruct((experts, width, hidden), F32),
            jax.ShapeDtypeStruct((experts, hidden, width), F32),
        ],
        input_output_aliases={5 * count + i: i for i in range(len(given))},
        compiler_params=pltpu.CompilerParams(vmem_limit_bytes=VMEM_GRANT),
        cost_estimate=pl.CostEstimate(
            flops=6 * (last - first) * slots * width * hidden,
            bytes_accessed=(last - first) * (4 * slots * width + 12 * width * hidden),
            transcendentals=0,
        ),
    )(*rows, *cots, *scaled, *d_gate, *d_up, *given)


def sums_kernel(counts, *refs):
    terms, outs = refs[: sum(counts)], refs[sum(counts) :]
    for count, out in zip(counts, outs):
        value = terms[0][...].astype(F32)
        for term in terms[1:count]:
            value = value + term[...].astype(F32)
        out[...] = value.astype(BF16)
        terms = terms[count:]


def block_sums(groups, tile=64):
    rows, width = groups[0][0].shape
    counts = [len(group) for group in groups]
    block = pl.BlockSpec((tile, width), lambda i: (i, 0))
    return pl.pallas_call(
        functools.partial(sums_kernel, counts),
        grid=(rows // tile,),
        in_specs=[block] * sum(counts),
        out_specs=[block] * len(groups),
        out_shape=[jax.ShapeDtypeStruct((rows, width), BF16)] * len(groups),
        compiler_params=pltpu.CompilerParams(vmem_limit_bytes=VMEM_GRANT),
        cost_estimate=pl.CostEstimate(
            flops=sum(counts) * rows * width,
            bytes_accessed=2 * (sum(counts) + len(groups)) * rows * width,
            transcendentals=0,
        ),
    )(*[term for group in groups for term in group])


def qkv_kernel(*refs):
    blocks, (q_w, k_w, v_w, q_out, k_out, v_out, q_sq, k_sq) = refs[:-8], refs[-8:]
    lanes = q_sq.shape[1]
    rows = blocks[0].shape[0]
    for b, block in enumerate(blocks):
        here = pl.ds(b * rows, rows)
        for weight, out, squares in ((q_w, q_out, q_sq), (k_w, k_out, k_sq)):
            value = nn(block[...], weight[...])
            out[here, :] = value
            value = value * value
            total = value[:, :lanes]
            for low in range(lanes, value.shape[1], lanes):
                total = total + value[:, low : low + lanes]

            @pl.when(pl.program_id(0) == 0)
            def _(squares=squares, total=total):
                squares[here, :] = total

            @pl.when(pl.program_id(0) > 0)
            def _(squares=squares, total=total):
                squares[here, :] += total

        v_out[here, :] = nn(block[...], v_w[...]).astype(BF16)


def qkv(blocks, w_query, w_key, w_value, tile=256):
    rows, depth = blocks[0].shape
    width = w_query.shape[1]
    count = len(blocks) * rows
    weight = pl.BlockSpec((depth, tile), lambda n: (0, n))
    out = pl.BlockSpec((count, tile), lambda n: (0, n))
    return pl.pallas_call(
        qkv_kernel,
        grid=(width // tile,),
        in_specs=[resident(rows, depth)] * len(blocks) + [weight] * 3,
        out_specs=[out] * 3 + [resident(count, HDIM)] * 2,
        out_shape=[
            jax.ShapeDtypeStruct((count, width), F32),
            jax.ShapeDtypeStruct((count, width), F32),
            jax.ShapeDtypeStruct((count, width), BF16),
            jax.ShapeDtypeStruct((count, HDIM), F32),
            jax.ShapeDtypeStruct((count, HDIM), F32),
        ],
        compiler_params=pltpu.CompilerParams(vmem_limit_bytes=VMEM_GRANT),
        cost_estimate=pl.CostEstimate(
            flops=6 * count * depth * width,
            bytes_accessed=2 * count * depth + 6 * depth * width + 10 * count * width,
            transcendentals=0,
        ),
    )(*blocks, w_query, w_key, w_value)


def pair_kernel(near_ref, far_ref, *outs):
    for b, out in enumerate(outs):
        out[...] = (near_ref[b].astype(F32) + far_ref[b].astype(F32)).astype(BF16)


def pair_sum(near, far, tile=64):
    count, rows, width = near.shape
    stack = pl.BlockSpec((count, tile, width), lambda i: (0, i, 0))
    return pl.pallas_call(
        pair_kernel,
        grid=(rows // tile,),
        in_specs=[stack, stack],
        out_specs=[pl.BlockSpec((tile, width), lambda i: (i, 0))] * count,
        out_shape=[jax.ShapeDtypeStruct((rows, width), BF16)] * count,
        compiler_params=pltpu.CompilerParams(vmem_limit_bytes=VMEM_GRANT),
        cost_estimate=pl.CostEstimate(
            flops=count * rows * width, bytes_accessed=6 * count * rows * width, transcendentals=0
        ),
    )(near, far)


def turn(values, cosine, sine):
    return values * cosine + pltpu.roll(values, values.shape[1] // 2, 1) * sine


def attend_kernel(
    row_block, scale, q_ref, k_ref, v_ref, cols_ref, qg_ref, kg_ref, cos_ref, sin_ref, kpos_ref,
    out_ref, lse_ref, qrot_ref, krot_ref,
):
    cosine, sine = cos_ref[...], sin_ref[...]
    qrot_ref[...] = turn(q_ref[...] * cols_ref[:, 0:1] * qg_ref[...], cosine, sine).astype(BF16)
    krot_ref[...] = turn(k_ref[...] * cols_ref[:, 1:2] * kg_ref[...], cosine, sine).astype(BF16)
    for low in range(0, q_ref.shape[0], row_block):
        rows = pl.ds(low, row_block)
        scores = nt(qrot_ref[rows, :], krot_ref[...]) * scale
        scores = jnp.where(kpos_ref[...] <= cols_ref[rows, 2:3], scores, -1e30)
        top = jnp.max(scores, axis=1, keepdims=True)
        powers = jnp.exp(scores - top)
        total = jnp.sum(powers, axis=1, keepdims=True)
        soft = (powers * (1.0 / total)).astype(BF16)
        out_ref[rows, :] = nn(soft, v_ref[...]).astype(BF16)
        lse_ref[rows, :] = jnp.broadcast_to(top + jnp.log(total), (row_block, HDIM))


def attend_back_kernel(
    row_block, scale, q_ref, k_ref, v_ref, qrot_ref, krot_ref, do_ref, lse_ref, cols_ref, qg_ref, kg_ref,
    cos_ref, sin_ref, kpos_ref,
    dq_ref, dk_ref, dv_ref, qgain_ref, kgain_ref, qin_ref, kin_ref, dq_acc, dk_acc, dv_acc,
):
    for low in range(0, q_ref.shape[0], row_block):
        rows = pl.ds(low, row_block)
        query, d_out = qrot_ref[rows, :], do_ref[rows, :]
        scores = nt(query, krot_ref[...]) * scale
        soft = jnp.where(kpos_ref[...] <= cols_ref[rows, 2:3], jnp.exp(scores - lse_ref[rows, 0:1]), 0.0)
        d_weights = nt(d_out, v_ref[...])
        spread = soft * d_weights
        mean = jnp.sum(spread, axis=1, keepdims=True)
        d_scores = (spread - soft * mean).astype(BF16)
        dq_acc[rows, :] = nn(d_scores, krot_ref[...]) * scale
        d_keys = contract_rows(d_scores, query)
        d_values = contract_rows(soft.astype(BF16), d_out)
        if low:
            dk_acc[...] += d_keys
            dv_acc[...] += d_values
        else:
            dk_acc[...] = d_keys
            dv_acc[...] = d_values
    dv_ref[...] = dv_acc[...].astype(BF16)
    cosine, sine = cos_ref[...], -sin_ref[...]
    for lane, raw_ref, gain_ref, grad, hat_ref, gain_out, inner_out in (
        (0, q_ref, qg_ref, dq_acc[...], dq_ref, qgain_ref, qin_ref),
        (1, k_ref, kg_ref, dk_acc[...] * scale, dk_ref, kgain_ref, kin_ref),
    ):
        hat = raw_ref[...] * cols_ref[:, lane : lane + 1]
        turned = turn(grad, cosine, sine)
        gain_out[...] = jnp.sum(turned * hat, axis=0, keepdims=True)
        d_hat = turned * gain_ref[...]
        hat_ref[...] = d_hat
        inner = d_hat * hat

        @pl.when(pl.program_id(0) == 0)
        def _(inner=inner, inner_out=inner_out):
            inner_out[...] = inner

        @pl.when(pl.program_id(0) > 0)
        def _(inner=inner, inner_out=inner_out):
            inner_out[...] += inner


def head_columns(rows):
    return pl.BlockSpec((rows, HDIM), lambda h: (0, h))


def whole(*shape):
    return pl.BlockSpec(shape, lambda h: (0,) * len(shape))


def attend_forward(q_raw, k_raw, v_low, cols, q_gain, k_gain, cosine, sine, kpos):
    seq_len, width = q_raw.shape
    heads = width // HDIM
    part, one = head_columns(seq_len), head_columns(1)
    return pl.pallas_call(
        functools.partial(attend_kernel, min(256, seq_len), HDIM ** (-0.5)),
        grid=(heads,),
        in_specs=[part, part, part, whole(seq_len, HDIM), one, one]
        + [whole(seq_len, HDIM), whole(seq_len, HDIM), whole(1, seq_len)],
        out_specs=[part, part, part, part],
        out_shape=[
            jax.ShapeDtypeStruct((seq_len, width), BF16),
            jax.ShapeDtypeStruct((seq_len, width), F32),
            jax.ShapeDtypeStruct((seq_len, width), BF16),
            jax.ShapeDtypeStruct((seq_len, width), BF16),
        ],
        compiler_params=pltpu.CompilerParams(vmem_limit_bytes=VMEM_GRANT),
        cost_estimate=pl.CostEstimate(
            flops=4 * seq_len * seq_len * width,
            bytes_accessed=20 * seq_len * width,
            transcendentals=heads * seq_len * seq_len,
        ),
    )(q_raw, k_raw, v_low, cols, q_gain, k_gain, cosine, sine, kpos)


def attend_backward(
    q_raw, k_raw, v_low, q_rot, k_rot, d_out, lse, cols, q_gain, k_gain, cosine, sine, kpos
):
    seq_len, width = q_raw.shape
    heads = width // HDIM
    part, one = head_columns(seq_len), head_columns(1)
    return pl.pallas_call(
        functools.partial(attend_back_kernel, min(256, seq_len), HDIM ** (-0.5)),
        grid=(heads,),
        in_specs=[part, part, part, part, part, part, part, whole(seq_len, HDIM), one, one]
        + [whole(seq_len, HDIM), whole(seq_len, HDIM), whole(1, seq_len)],
        out_specs=[part, part, part, one, one, whole(seq_len, HDIM), whole(seq_len, HDIM)],
        out_shape=[
            jax.ShapeDtypeStruct((seq_len, width), F32),
            jax.ShapeDtypeStruct((seq_len, width), F32),
            jax.ShapeDtypeStruct((seq_len, width), BF16),
            jax.ShapeDtypeStruct((1, width), F32),
            jax.ShapeDtypeStruct((1, width), F32),
            jax.ShapeDtypeStruct((seq_len, HDIM), F32),
            jax.ShapeDtypeStruct((seq_len, HDIM), F32),
        ],
        scratch_shapes=[pltpu.VMEM((seq_len, HDIM), F32)] * 3,
        compiler_params=pltpu.CompilerParams(vmem_limit_bytes=VMEM_GRANT),
        cost_estimate=pl.CostEstimate(
            flops=10 * seq_len * seq_len * width,
            bytes_accessed=32 * seq_len * width,
            transcendentals=heads * seq_len * seq_len,
        ),
    )(q_raw, k_raw, v_low, q_rot, k_rot, d_out, lse, cols, q_gain, k_gain, cosine, sine, kpos)


def local_gathered(
    hidden_in,
    cotangent,
    seq_lengths,
    expert_ids,
    attn_gain,
    w_query,
    w_key,
    w_value,
    query_gain,
    key_gain,
    w_out,
    ffn_gain,
    w_router,
    w_gate,
    w_up,
    w_down,
):
    tensor_count = lax.axis_size("tensor")
    group_count = lax.axis_size("dp")
    tok_rows, model_width = hidden_in.shape
    topk = expert_ids.shape[1]
    expert_total = w_router.shape[1]
    experts = w_gate.shape[0]
    slot_count = tok_rows * topk // expert_total
    devices = len(PLACES)
    seq_len = tok_rows * tensor_count
    local_width = w_query.shape[1]
    half_width = HDIM // 2
    live_length = seq_lengths[0]
    absolute, position = place_indices()

    member = lax.axis_index("tensor")
    blocks_at = member ^ jnp.arange(tensor_count)

    def turn_tables(blocks_at):
        cosine, sine = (
            table.reshape(tensor_count, tok_rows, half_width)[blocks_at].reshape(seq_len, half_width)
            for table in rope_tables(seq_len, HDIM)
        )
        return jnp.concatenate([cosine, cosine], axis=1), jnp.concatenate([-sine, sine], axis=1)

    positions = (blocks_at[:, None] * tok_rows + jnp.arange(tok_rows)[None, :]).reshape(-1)
    never = 2 * seq_len
    key_pos = jnp.where(positions < live_length, positions, never).astype(F32)[None, :]

    def token_sums(*values):
        stacked = jnp.stack([value.reshape(tensor_count, tok_rows) for value in values])
        summed = lax.psum(stacked[:, blocks_at], "tensor")
        return summed[:, blocks_at].reshape(len(values), seq_len)

    def to_groups(by_expert):
        copies = jnp.broadcast_to(
            by_expert.reshape(group_count, 1, experts, tok_rows),
            (group_count, tensor_count, experts, tok_rows),
        ).reshape(devices, experts, tok_rows)
        return lax.all_to_all(copies, BOTH, split_axis=0, concat_axis=0, tiled=True)[absolute]

    resid = hidden_in.astype(F32)
    scale_one = rms_scale(resid)
    normed = resid * scale_one
    attn_in = (normed * attn_gain.astype(F32)).astype(BF16)
    q_gain = query_gain.astype(F32)[None, :]
    k_gain = key_gain.astype(F32)[None, :]

    hot = jnp.any(expert_ids.T[None, :, :] == jnp.arange(expert_total)[:, None, None], axis=1)
    earlier = jnp.triu(jnp.ones((tok_rows, tok_rows), F32), 1).astype(BF16)
    rank = jnp.dot(hot.astype(BF16), earlier, preferred_element_type=F32)
    slot_of = jnp.where(hot, rank, -1.0)

    def all_picks(slot_of):
        slots = jnp.arange(slot_count, dtype=F32)
        wide = (slot_of[:, :, None, :] == slots[None, None, :, None]).astype(BF16)
        return [
            wide[low : low + len(chunk)].reshape(len(chunk), experts * slot_count, tok_rows)
            for chunk, low in zip(CHUNKS, STARTS)
        ]


    stages = Stages(attn_in)
    cot, ffn = Gather(cotangent), Gather(None)
    d_sum, out_sum = Scatter(), Scatter()
    order = range(len(CHUNKS))
    cot_rows, cot_acts, kept = {}, {}, {}

    def advance(works=(), extra=(), **hops):
        tables = {"cot": cot, "ffn": ffn, "d": d_sum, "out": out_sum}
        sends = list(extra)
        spans = []
        for name, moves in hops.items():
            spans.append((tables[name], moves, len(sends)))
            sends += tables[name].sends(moves)
        got, made = stages.run(sends, works)
        for table, moves, low in spans:
            table.take(moves, got[low : low + len(moves)])
        return got[: len(extra)], made

    def cot_work(*chunks):
        made = [cot.chunk(i) for i in chunks]

        def work(picks_i, w_down_i, *args):
            blocks = []
            for i, (_, _, late), (values, crossing) in zip(chunks, made, args):
                blocks += Gather.complete(i, values, crossing, late)
            return cot_chunk(picks_i, w_down_i, blocks, slot_count)

        picks_i = picks[chunks[0]] if len(chunks) == 1 else jnp.concatenate([picks[i] for i in chunks], axis=0)
        return work, (picks_i, w_down) + tuple((values, crossing) for values, crossing, _ in made)

    def cot_done(chunks, made):
        for n, i in enumerate(chunks):
            cot_rows[i], cot_acts[i] = (made[0], n), (made[1], n)

    def main_work(i):
        values, crossing, late = ffn.chunk(i)

        def work(picks_i, gates_i, acts_i, gate_w, up_w, values, crossing):
            blocks = Gather.complete(i, values, crossing, late)
            return main_chunk(picks_i, gates_i, acts_i, cot_acts[i][1], gate_w, up_w, blocks, slot_count)

        gates_i = token_gates[STARTS[i] : STARTS[i] + len(CHUNKS[i])]
        return work, (picks[i], gates_i, cot_acts[i][0], w_gate, w_up, values, crossing)

    def out_work(*chunks):
        def work(picks_i, scaled_i, w_down_i):
            return out_chunk(picks_i, scaled_i, w_down_i, slot_count)

        return work, ([picks[i] for i in chunks], [kept[i][1] for i in chunks], w_down)

    (across, mate), ((cosine, sine), slot_of) = advance(
        [(turn_tables, (blocks_at,)), (to_groups, (slot_of,))],
        extra=[(attn_in, "y"), (attn_in, "c")],
        cot=[("z", (0, 0, 0)), ("x", (0, 0, 0))],
    )

    def project(block, mate, across, w_query, w_key, w_value):
        blocks = [block, mate, across, send(across, "c")]
        q_raw, k_raw, v_low, q_square, k_square = qkv(blocks, w_query, w_key, w_value)
        squares = token_sums(jnp.sum(q_square, axis=1), jnp.sum(k_square, axis=1))
        return blocks, q_raw, k_raw, v_low, squares

    _, (made,) = advance(
        [(project, (attn_in, mate, across, w_query, w_key, w_value))],
        cot=[("z", (1, 0, 0)), ("x", (1, 0, 0)), ("y", (0, 0, 0)), ("c", (0, 0, 0)), ("c", (1, 0, 0))],
    )
    seq_blocks, q_raw, k_raw, v_low, squares = made

    def columns_of(squares):
        scales = lax.rsqrt(squares / model_width + EPS)
        columns = jnp.stack([scales[0], scales[1], positions.astype(F32)], axis=1)
        return jnp.pad(columns, ((0, 0), (0, HDIM - columns.shape[1])))

    cols = columns_of(squares)
    _, (made,) = advance(
        [(attend_forward, (q_raw, k_raw, v_low, cols, q_gain, k_gain, cosine, sine, key_pos))],
        cot=[("z", (2, 0, 0)), ("x", (2, 0, 0)), ("y", (1, 0, 0)), ("c", (0, 1, 0)), ("c", (0, 0, 1))],
    )
    o_low, lse, q_rot, k_rot = made

    def project_back(o_low, w_out):
        parts = [
            jnp.dot(o_low[r * tok_rows : (r + 1) * tok_rows], w_out, preferred_element_type=F32).astype(BF16)
            for r in range(tensor_count)
        ]
        across = add_low(parts[2], send(parts[3], "c"))
        return add_wide(parts[0], send(parts[1], "c")) + send(across, "y").astype(F32)

    _, (attn_rows, picks) = advance(
        [(project_back, (o_low, w_out)), (all_picks, (slot_of,))],
        cot=[("x", (3, 0, 0)), ("c", (2, 0, 0)), ("c", (1, 1, 0))],
    )
    mixed = resid + attn_rows
    scale_two = rms_scale(mixed)
    mixed_norm = mixed * scale_two
    ffn_in = (mixed_norm * ffn_gain.astype(F32)).astype(BF16)
    ffn.held[0, 0, 0, 0] = ffn_in

    def route(ffn_in, w_router):
        logits = jnp.dot(ffn_in, w_router, preferred_element_type=F32)
        return jax.nn.softmax(logits, axis=-1)

    def join(*blocks):
        return jnp.concatenate(blocks, axis=0)

    _, (router_probs, made, gathered) = advance(
        [(route, (ffn_in, w_router)), cot_work(0), (join, tuple(seq_blocks))],
        ffn=[("z", (0, 0, 0)), ("x", (0, 0, 0)), ("y", (0, 0, 0))],
        cot=[("c", (1, 0, 1)), ("c", (2, 1, 0))],
    )
    cot_done((0,), made)
    _, (made, token_gates) = advance(
        [cot_work(1), (to_groups, (router_probs.T,))],
        ffn=[("z", (1, 0, 0)), ("x", (1, 0, 0)), ("y", (1, 0, 0))]
        + [("c", (0, 0, 0)), ("c", (0, 1, 0)), ("c", (1, 0, 0)), ("c", (0, 0, 1))],
    )
    cot_done((1,), made)
    _, (made,) = advance(
        [main_work(0)],
        ffn=[("z", (2, 0, 0)), ("x", (2, 0, 0)), ("c", (2, 0, 0))],
        cot=[("y", (2, 0, 0)), ("c", (3, 0, 0))],
    )
    kept[0], near, far = made[0], *made[1]
    _, (made,) = advance(
        [(core_sum, (near, far))],
        ffn=[("x", (3, 0, 0)), ("c", (1, 1, 0)), ("c", (1, 0, 1)), ("c", (2, 1, 0))],
        cot=[("y", (3, 0, 0))],
    )
    d_sum.put(0, made)
    _, (made,) = advance(
        [main_work(1)],
        ffn=[("y", (2, 0, 0))],
        cot=[("x", (0, 0, 1)), ("c", (3, 1, 0)), ("c", (2, 0, 1))],
    )
    kept[1], near, far = made[0], *made[1]
    _, (made, other) = advance(
        [(core_sum, (near, far)), cot_work(2)],
        ffn=[("y", (3, 0, 0)), ("c", (3, 0, 0)), ("c", (3, 1, 0))],
        cot=[("x", (1, 0, 1))],
    )
    d_sum.put(1, made)
    cot_done((2,), other)
    _, (made,) = advance(
        [main_work(2)],
        cot=[("x", (2, 0, 1)), ("y", (3, 1, 0)), ("c", (0, 1, 1)), ("c", (1, 1, 1))],
    )
    kept[2], near, far = made[0], *made[1]
    _, (made, other) = advance(
        [(core_sum, (near, far)), cot_work(3, 4)],
        ffn=[("x", (2, 0, 1)), ("y", (1, 1, 0))],
    )
    d_sum.put(2, made)
    cot_done((3, 4), other)
    _, (made,) = advance([main_work(3)], ffn=[("x", (3, 0, 1)), ("y", (0, 1, 0))])
    kept[3], near, far = made[0], *made[1]
    _, (made,) = advance([(core_sum, (near, far))], ffn=[("c", (0, 1, 1)), ("c", (3, 1, 1))])
    d_sum.put(3, made)

    _, (made,) = advance([main_work(4)], d=[("x", (1, 1, 1)), ("y", (2, 1, 1))])
    kept[4], near, far = made[0], *made[1]

    def return_probs(*d_probs):
        d_probs = jnp.concatenate(d_probs, axis=0)[position]
        arrived = lax.all_to_all(d_probs, BOTH, split_axis=0, concat_axis=0, tiled=True)
        arrived = arrived.reshape(group_count, tensor_count, experts, tok_rows)
        return jnp.sum(arrived, axis=1).reshape(expert_total, tok_rows).T

    outs = {}
    _, (made, outs[0], d_probs) = advance(
        [(core_sum, (near, far)), out_work(0), (return_probs, tuple(kept[i][4] for i in order))],
        d=[("x", (1, 1, 0)), ("y", (1, 0, 1))],
    )
    d_sum.put(4, made)
    _, (outs[1], made) = advance(
        [out_work(1), (core_sum, tuple(outs[0]))], d=[("x", (3, 1, 1)), ("y", (0, 1, 1))]
    )
    out_sum.put(0, made)
    _, (outs[2], made) = advance(
        [out_work(2), (core_sum, tuple(outs[1]))],
        d=[("x", (2, 1, 0)), ("y", (2, 0, 1)), ("z", (1, 0, 0))],
    )
    out_sum.put(1, made)
    _, (last_outs, made) = advance(
        [out_work(3, 4), (core_sum, tuple(outs[2]))],
        d=[("x", (3, 1, 0)), ("y", (3, 0, 1)), ("z", (2, 0, 0))],
    )
    out_sum.put(2, made)
    def saved(n):
        return [kept[i][n] for i in order]

    def grads_of(first, last, earlier=None):
        all_cots = [cot_rows[i][0] for i in order]

        places = [cot_rows[i][1] for i in order]

        def work(*args):
            return expert_grads(*args[:5], places, first, last, args[5] if len(args) > 5 else None)

        args = (saved(0), all_cots, saved(1), saved(2), saved(3))
        return work, args if earlier is None else args + (earlier,)

    thirds = [experts * n // 3 for n in range(4)]
    _, (made, weight_grads) = advance(
        [(core_sum, tuple(last_outs)), grads_of(thirds[0], thirds[1])],
        d=[("x", (0, 1, 0)), ("y", (0, 0, 1)), ("z", (3, 0, 0))],
    )
    out_sum.put(3, made[:2])
    out_sum.put(4, made[2:])
    d_ffn = d_sum.total()

    d_result = cotangent.astype(F32)
    d_logits = (
        router_probs * (d_probs - jnp.sum(router_probs * d_probs, axis=-1, keepdims=True))
    ).astype(BF16)
    router_part = contract_rows(d_logits, ffn_in)
    d_ffn = d_ffn + times_transpose(d_logits, w_router)
    ffn_gain_part = jnp.sum(d_ffn * mixed_norm, axis=0)
    d_norm_two = d_ffn * ffn_gain.astype(F32)
    d_mixed = d_result + scale_two * (
        d_norm_two - mixed_norm * jnp.mean(d_norm_two * mixed_norm, axis=-1, keepdims=True)
    )
    d_attn = d_mixed.astype(BF16)
    router_sums = jnp.concatenate(
        [router_part, jnp.broadcast_to(ffn_gain_part[None, :], (16, model_width))], axis=0
    ).astype(BF16)

    (across, mate, other), (weight_grads,) = advance(
        [grads_of(thirds[1], thirds[2], weight_grads)],
        extra=[(d_attn, "y"), (d_attn, "c"), (router_sums, "z1")],
        out=[("x", (1, 1, 1))],
    )
    router_sums = add_low(router_sums, other)

    def attend_back(d_attn, mate, across, w_out, o_low, *rest):
        d_blocks = [d_attn, mate, across, send(across, "c")]
        d_attended = join(*[times_transpose(block, w_out).astype(BF16) for block in d_blocks])
        q_raw, k_raw, v_low, q_rot, k_rot, lse, cols = rest
        *made, q_inner, k_inner = attend_backward(
            q_raw, k_raw, v_low, q_rot, k_rot, d_attended, lse, cols, q_gain, k_gain, cosine, sine, key_pos
        )
        inner = token_sums(jnp.sum(q_inner, axis=1), jnp.sum(k_inner, axis=1)) / model_width
        return made, inner, contract_rows(o_low, join(*d_blocks)).astype(BF16)

    _, (made,) = advance(
        [
            (
                attend_back,
                (d_attn, mate, across, w_out, o_low, q_raw, k_raw, v_low, q_rot, k_rot, lse, cols),
            )
        ],
        out=[("x", (3, 1, 1)), ("x", (1, 1, 0)), ("y", (2, 1, 1)), ("y", (1, 0, 1))],
    )
    (dq_hat, dk_hat, dv_raw, query_gain_part, key_gain_part), inner, grad_w_out = made

    def value_grad(gathered, dv_raw):
        return contract_rows(gathered, dv_raw).astype(BF16)

    def norm_back(q_raw, k_raw, cols, dq_hat, dk_hat, inner):
        raws = []
        for n, (raw, d_hat) in enumerate(((q_raw, dq_hat), (k_raw, dk_hat))):
            scale = cols[:, n : n + 1]
            raws.append((scale * (d_hat - raw * scale * inner[n][:, None])).astype(BF16))
        return raws

    out_weight = DpSum(grad_w_out)
    (other, *got), ((dq_raw, dk_raw), grad_value, (grad_w_gate, grad_w_up, grad_w_down)) = advance(
        [
            (norm_back, (q_raw, k_raw, cols, dq_hat, dk_hat, inner)),
            (value_grad, (gathered, dv_raw)),
            grads_of(thirds[2], thirds[3], weight_grads),
        ],
        extra=[(router_sums, "z2")] + out_weight.split_x(),
        out=[("x", (2, 1, 0)), ("y", (2, 0, 1)), ("z", (1, 0, 0))],
    )
    router_sums = add_low(router_sums, other)
    out_weight.add_x(got)
    value_weight = DpSum(grad_value)

    def projections_back(gathered, dq_raw, dk_raw, dv_raw, w_query, w_key, w_value):
        grads = [contract_rows(gathered, part).astype(BF16) for part in (dk_raw, dq_raw)]
        total_term = times_transpose(dq_raw, w_query)
        total_term = total_term + times_transpose(dk_raw, w_key)
        total_term = (total_term + times_transpose(dv_raw, w_value)).astype(BF16)
        return grads, total_term

    got, (((grad_key, grad_query), total_term), out_piece) = advance(
        [
            (projections_back, (gathered, dq_raw, dk_raw, dv_raw, w_query, w_key, w_value)),
            (out_weight.reduce_z, (out_weight.sum,)),
        ],
        extra=value_weight.split_x(),
        out=[("x", (3, 1, 0)), ("y", (3, 0, 1)), ("z", (2, 0, 0))],
    )
    value_weight.add_x(got)
    key_weight, query_weight = DpSum(grad_key), DpSum(grad_query)
    parts = jnp.split(total_term, tensor_count, axis=0)
    (d_other, other, *got), (value_piece,) = advance(
        [(value_weight.reduce_z, (value_weight.sum,))],
        extra=[(jnp.concatenate([parts[1], parts[3]], axis=0), "c"), (router_sums, "c")] + key_weight.split_x(),
        out=[("y", (0, 1, 1))],
    )
    router_sums = add_low(router_sums, other)
    key_weight.add_x(got)
    out_weight.part = out_piece
    (d_across, *got), _ = advance(
        extra=[(add_low(parts[2], d_other[tok_rows:]), "y")] + query_weight.split_x() + out_weight.join_z(),
    )
    query_weight.add_x(got[:1])
    out_weight.took_z(got[1:])
    d_attn_in = add_wide(parts[0], d_other[:tok_rows], d_across)
    attn_gain_part = jnp.sum(d_attn_in * normed, axis=0)
    d_norm_one = d_attn_in * attn_gain.astype(F32)
    d_input = d_mixed + scale_one * (
        d_norm_one - normed * jnp.mean(d_norm_one * normed, axis=-1, keepdims=True)
    )
    (other, third, *got), (value_weight.whole_half, d_input) = advance(
        [
            (value_weight.collect_z, (value_piece,)),
            (lambda value: value, (d_input.astype(BF16),)),
        ],
        extra=[(attn_gain_part, "c"), (router_sums, "y")] + out_weight.join_x(),
        out=[("y", (0, 0, 1))],
    )
    router_sums = add_low(router_sums, third)
    attn_gain_part = attn_gain_part + other
    out_weight.took_x(got)
    (other, *got), (key_piece, grad_w_out) = advance(
        [
            (key_weight.reduce_z, (key_weight.sum,)),
            (lambda value: value, (out_weight.result,)),
        ],
        extra=[(attn_gain_part, "y")] + value_weight.join_x(),
    )
    value_weight.took_x(got)
    gain_parts = jnp.concatenate([attn_gain_part + other, query_gain_part[0], key_gain_part[0]])
    (other, third), (query_piece, grad_value) = advance(
        [
            (query_weight.reduce_z, (query_weight.sum,)),
            (lambda value: value, (value_weight.result,)),
        ],
        extra=[(gain_parts, "x"), (router_sums, "x")],
        out=[("x", (0, 1, 0))],
    )
    gain_parts = gain_parts + other
    router_sums = add_wide(router_sums, third)
    (next_z, far_z, last_z), (key_weight.whole_half,) = advance(
        [(key_weight.collect_z, (key_piece,))],
        extra=[(gain_parts, "u1"), (gain_parts, "u2"), (gain_parts, "u3")],
    )
    gain_sums = (gain_parts + far_z) + (next_z + last_z)
    got, (query_weight.whole_half, gain_sums, router_sums) = advance(
        [
            (query_weight.collect_z, (query_piece,)),
            (lambda value: value, (gain_sums,)),
            (lambda value: value, (router_sums,)),
        ],
        extra=key_weight.join_x(),
    )
    key_weight.took_x(got)
    got, (grad_key,) = advance(
        [(lambda value: value, (key_weight.result,))],
        extra=query_weight.join_x(),
        out=[("z", (3, 0, 0))],
    )
    query_weight.took_x(got)
    grad_query = query_weight.result
    result = (mixed + out_sum.total()).astype(BF16)
    return (
        result,
        d_input,
        grad_query,
        grad_key,
        grad_value,
        gain_sums[model_width : model_width + local_width],
        gain_sums[model_width + local_width :],
        grad_w_out,
        gain_sums[:model_width],
        router_sums[expert_total],
        router_sums[:expert_total].T,
        grad_w_gate,
        grad_w_up,
        grad_w_down,
    )


def local_sent(
    hidden_in,
    cotangent,
    seq_lengths,
    expert_ids,
    attn_gain,
    w_query,
    w_key,
    w_value,
    query_gain,
    key_gain,
    w_out,
    ffn_gain,
    w_router,
    w_gate,
    w_up,
    w_down,
):
    tensor_count = lax.axis_size("tensor")
    group_count = lax.axis_size("dp")
    device_total = tensor_count * group_count
    tok_rows, model_width = hidden_in.shape
    topk_count = expert_ids.shape[1]
    local_experts = w_gate.shape[0]
    expert_total = w_router.shape[1]
    slot_count = tok_rows * topk_count // expert_total
    per_group = local_experts * slot_count
    seq_len = tok_rows * tensor_count
    local_width = w_query.shape[1]
    head_width = HDIM
    local_heads = local_width // head_width
    block_rows = min(512, seq_len)
    block_count = seq_len // block_rows
    score_scale = head_width ** (-0.5)
    live_length = seq_lengths[0]
    cosine, sine_table = (table[:, None, :] for table in rope_tables(seq_len, head_width))
    key_pos = jnp.arange(seq_len)
    key_live = key_pos < live_length

    def send_out(rows_low):
        grouped_rows = rows_low.reshape(group_count, 1, per_group, model_width)
        copies = jnp.broadcast_to(
            grouped_rows, (group_count, tensor_count, per_group, model_width)
        ).reshape(device_total, per_group, model_width)
        arrived = lax.all_to_all(copies, ("dp", "tensor"), split_axis=0, concat_axis=0, tiled=True)
        return arrived.reshape(device_total, local_experts, slot_count, model_width)

    def send_back(parts_low):
        returned = lax.all_to_all(
            parts_low.reshape(device_total, per_group, model_width),
            ("dp", "tensor"),
            split_axis=0,
            concat_axis=0,
            tiled=True,
        )
        return jnp.sum(
            returned.reshape(group_count, tensor_count, per_group, model_width).astype(F32),
            axis=1,
        ).reshape(-1, model_width)

    resid = hidden_in.astype(F32)
    scale_one = rms_scale(resid)
    normed = resid * scale_one
    attn_in = (normed * attn_gain.astype(F32)).astype(BF16)
    gathered = lax.all_gather(attn_in, "tensor", axis=0, tiled=True)
    q_raw = jnp.dot(gathered, w_query, preferred_element_type=F32)
    k_raw = jnp.dot(gathered, w_key, preferred_element_type=F32)
    v_raw = jnp.dot(gathered, w_value, preferred_element_type=F32)
    q_square, k_square = lax.psum(
        (jnp.sum(q_raw * q_raw, axis=1), jnp.sum(k_raw * k_raw, axis=1)), "tensor"
    )
    q_rscale = lax.rsqrt(q_square / model_width + EPS)[:, None]
    k_rscale = lax.rsqrt(k_square / model_width + EPS)[:, None]
    query_hat = q_raw * q_rscale
    key_hat = k_raw * k_rscale
    q_gain = query_gain.astype(F32)
    k_gain = key_gain.astype(F32)
    q_rot = rotate(
        (query_hat * q_gain).reshape(seq_len, local_heads, head_width), cosine, sine_table
    ).astype(BF16)
    k_rot = rotate(
        (key_hat * k_gain).reshape(seq_len, local_heads, head_width), cosine, sine_table
    ).astype(BF16)
    v_low = v_raw.astype(BF16).reshape(seq_len, local_heads, head_width)
    starts = jnp.arange(block_count) * block_rows
    q_blocks = q_rot.reshape(block_count, block_rows, local_heads, head_width)

    def allowed_mask(row_start):
        q_pos = row_start + jnp.arange(block_rows)
        return ((key_pos[None, :] <= q_pos[:, None]) & key_live[None, :])[None]

    def attend(inputs):
        q_block, row_start = inputs
        scores = (
            jnp.einsum("qhd,khd->hqk", q_block, k_rot, preferred_element_type=F32)
            * score_scale
        )
        scores = jnp.where(allowed_mask(row_start), scores, -1e30)
        row_max = jnp.max(scores, axis=-1, keepdims=True)
        exp_scores = jnp.exp(scores - row_max)
        row_total = jnp.sum(exp_scores, axis=-1, keepdims=True)
        soft_low = (exp_scores / row_total).astype(BF16)
        attended = jnp.einsum("hqk,khd->qhd", soft_low, v_low, preferred_element_type=F32)
        return (attended, (row_max + jnp.log(row_total))[..., 0])

    o_blocks, lse_blocks = lax.map(attend, (q_blocks, starts))
    o_low = o_blocks.reshape(seq_len, local_width).astype(BF16)
    attn_rows = lax.psum_scatter(
        jnp.dot(o_low, w_out, preferred_element_type=F32),
        "tensor",
        scatter_dimension=0,
        tiled=True,
    )
    mixed = resid + attn_rows
    scale_two = rms_scale(mixed)
    mixed_norm = mixed * scale_two
    ffn_in = (mixed_norm * ffn_gain.astype(F32)).astype(BF16)
    logits = jnp.dot(ffn_in, w_router, preferred_element_type=F32)
    router_probs = jax.nn.softmax(logits, axis=-1)
    expert_hot = (expert_ids[:, :, None] == jnp.arange(expert_total)[None, None, :]).astype(
        F32
    )
    gate_values = jnp.einsum("tke,te->tk", expert_hot, router_probs)
    flat_ids = expert_ids.reshape(-1)
    sort_order = jnp.argsort(flat_ids, stable=True)
    inverse = jnp.argsort(sort_order)
    expert_in = send_out(ffn_in[sort_order // topk_count])
    gate_pre = jnp.einsum("secd,edf->secf", expert_in, w_gate, preferred_element_type=F32)
    up_pre = jnp.einsum("secd,edf->secf", expert_in, w_up, preferred_element_type=F32)
    silu_gate = jax.nn.silu(gate_pre)
    acts = (silu_gate * up_pre).astype(BF16)
    partial_value = jnp.einsum(
        "secf,efd->secd", acts, w_down, preferred_element_type=F32
    ).astype(BF16)
    out_sorted = send_back(partial_value)
    out_assign = out_sorted[inverse].reshape(tok_rows, topk_count, model_width)
    expert_mix = jnp.einsum("tk,tkd->td", gate_values, out_assign)
    result = mixed + expert_mix
    d_result = cotangent.astype(F32)
    d_gates = jnp.einsum("tkd,td->tk", out_assign, d_result)
    d_out = (
        (gate_values[:, :, None] * d_result[:, None, :])
        .astype(BF16)
        .reshape(-1, model_width)[sort_order]
    )
    d_arrived = send_out(d_out)
    d_acts = jnp.einsum("secd,efd->secf", d_arrived, w_down, preferred_element_type=F32)
    sigmoid_gate = jax.nn.sigmoid(gate_pre)
    d_gate_pre = (d_acts * up_pre * sigmoid_gate * (1.0 + gate_pre * (1.0 - sigmoid_gate))).astype(
        BF16
    )
    d_up_pre = (d_acts * silu_gate).astype(BF16)
    grad_w_down = jnp.einsum("secf,secd->efd", acts, d_arrived, preferred_element_type=F32)
    grad_w_gate = jnp.einsum(
        "secd,secf->edf", expert_in, d_gate_pre, preferred_element_type=F32
    )
    grad_w_up = jnp.einsum(
        "secd,secf->edf", expert_in, d_up_pre, preferred_element_type=F32
    )
    d_rows = (
        jnp.einsum("secf,edf->secd", d_gate_pre, w_gate, preferred_element_type=F32)
        + jnp.einsum("secf,edf->secd", d_up_pre, w_up, preferred_element_type=F32)
    ).astype(BF16)
    d_sorted = send_back(d_rows)
    d_ffn = jnp.sum(d_sorted[inverse].reshape(tok_rows, topk_count, model_width), axis=1)
    d_probs = jnp.einsum("tk,tke->te", d_gates, expert_hot)
    d_logits = (
        router_probs * (d_probs - jnp.sum(router_probs * d_probs, axis=-1, keepdims=True))
    ).astype(BF16)
    router_part = contract_rows(ffn_in, d_logits)
    d_ffn = d_ffn + times_transpose(d_logits, w_router)
    ffn_gain_part = jnp.sum(d_ffn * mixed_norm, axis=0)
    d_norm_two = d_ffn * ffn_gain.astype(F32)
    d_mixed = d_result + scale_two * (
        d_norm_two - mixed_norm * jnp.mean(d_norm_two * mixed_norm, axis=-1, keepdims=True)
    )
    d_attn = d_mixed.astype(BF16)
    d_attn_all = lax.all_gather(d_attn, "tensor", axis=0, tiled=True)
    grad_w_out = contract_rows(o_low, d_attn_all)
    d_attended = (
        times_transpose(d_attn_all, w_out)
        .astype(BF16)
        .reshape(block_count, block_rows, local_heads, head_width)
    )

    def attend_back(carry, inputs):
        dk_total, dv_total = carry
        q_block, do_block, lse_block, row_start = inputs
        scores = (
            jnp.einsum("qhd,khd->hqk", q_block, k_rot, preferred_element_type=F32)
            * score_scale
        )
        allowed = allowed_mask(row_start)
        scores = jnp.where(allowed, scores, -1e30)
        soft = jnp.where(allowed, jnp.exp(scores - lse_block[..., None]), 0.0)
        d_weights = jnp.einsum("qhd,khd->hqk", do_block, v_low, preferred_element_type=F32)
        d_scores = (soft * (d_weights - jnp.sum(soft * d_weights, axis=-1, keepdims=True))).astype(
            BF16
        )
        dq_block = (
            jnp.einsum("hqk,khd->qhd", d_scores, k_rot, preferred_element_type=F32)
            * score_scale
        )
        dk_total = (
            dk_total
            + jnp.einsum("hqk,qhd->khd", d_scores, q_block, preferred_element_type=F32)
            * score_scale
        )
        dv_total = dv_total + jnp.einsum(
            "hqk,qhd->khd", soft.astype(BF16), do_block, preferred_element_type=F32
        )
        return ((dk_total, dv_total), dq_block)

    zero_field = jnp.zeros((seq_len, local_heads, head_width), F32)
    (dk_rot, dv_full), dq_blocks = lax.scan(
        attend_back, (zero_field, zero_field), (q_blocks, d_attended, lse_blocks, starts)
    )
    dq_gain = unrotate(
        dq_blocks.reshape(seq_len, local_heads, head_width), cosine, sine_table
    ).reshape(seq_len, local_width)
    dk_gain = unrotate(dk_rot, cosine, sine_table).reshape(seq_len, local_width)
    query_gain_part = jnp.sum(dq_gain * query_hat, axis=0)
    key_gain_part = jnp.sum(dk_gain * key_hat, axis=0)
    dq_hat = dq_gain * q_gain
    dk_hat = dk_gain * k_gain
    q_inner, k_inner = lax.psum(
        (jnp.sum(dq_hat * query_hat, axis=1), jnp.sum(dk_hat * key_hat, axis=1)), "tensor"
    )
    dq_raw = (q_rscale * (dq_hat - query_hat * (q_inner / model_width)[:, None])).astype(
        BF16
    )
    dk_raw = (k_rscale * (dk_hat - key_hat * (k_inner / model_width)[:, None])).astype(BF16)
    dv_raw = dv_full.reshape(seq_len, local_width).astype(BF16)
    grad_query = contract_rows(gathered, dq_raw)
    grad_key = contract_rows(gathered, dk_raw)
    grad_value = contract_rows(gathered, dv_raw)
    total_term = times_transpose(dq_raw, w_query)
    total_term = total_term + times_transpose(dk_raw, w_key)
    d_attn_in = lax.psum_scatter(
        (total_term + times_transpose(dv_raw, w_value)).astype(BF16),
        "tensor",
        scatter_dimension=0,
        tiled=True,
    ).astype(F32)
    attn_gain_part = jnp.sum(d_attn_in * normed, axis=0)
    d_norm_one = d_attn_in * attn_gain.astype(F32)
    d_input = d_mixed + scale_one * (
        d_norm_one - normed * jnp.mean(d_norm_one * normed, axis=-1, keepdims=True)
    )
    dp_sums = (
        lax.psum(grad_query.astype(BF16), "dp").astype(F32),
        lax.psum(grad_key.astype(BF16), "dp").astype(F32),
        lax.psum(grad_value.astype(BF16), "dp").astype(F32),
        lax.psum(query_gain_part.astype(BF16), "dp").astype(F32),
        lax.psum(key_gain_part.astype(BF16), "dp").astype(F32),
        lax.psum(grad_w_out.astype(BF16), "dp").astype(F32),
    )
    shared = lax.psum((attn_gain_part, ffn_gain_part, router_part), ("dp", "tensor"))
    return (
        result.astype(BF16),
        d_input.astype(BF16),
        dp_sums[0],
        dp_sums[1],
        dp_sums[2],
        dp_sums[3],
        dp_sums[4],
        dp_sums[5],
        shared[0],
        shared[1],
        shared[2],
        grad_w_gate,
        grad_w_up,
        grad_w_down,
    )


def solution(mesh):
    rows, columns = P(BOTH, None), P(None, "tensor")
    gathered_plan = (mesh.shape["dp"], mesh.shape["tensor"]) == (2 * RING, 4)
    return jax.shard_map(
        local_gathered if gathered_plan else local_sent,
        mesh=mesh,
        in_specs=(
            rows,
            rows,
            P("dp"),
            rows,
            P(),
            columns,
            columns,
            columns,
            P("tensor"),
            P("tensor"),
            P("tensor", None),
            P(),
            P(),
            P("dp", None, "tensor"),
            P("dp", None, "tensor"),
            P("dp", "tensor", None),
        ),
        out_specs=(
            rows,
            rows,
            columns,
            columns,
            columns,
            P("tensor"),
            P("tensor"),
            P("tensor", None),
            P(),
            P(),
            P(),
            P("dp", None, "tensor"),
            P("dp", None, "tensor"),
            P("dp", "tensor", None),
        ),
        check_vma=False,
    )
```
